32 devices in a mesh: chan: 8 (over y, x, core), tile: 4 (over z).
Axes of the slice: x: 2, y: 2, z: 4, core: 2. Of those that a mesh axis runs over, the one named last changes fastest.
Arguments:
- generator: bfloat16 [32, 1024, 1024], P('chan', 'tile'), as said below
- hamiltonian: bfloat16 [32, 1024, 1024], P('chan', 'tile')
- chan_sizes: int32 [32], P('chan'), may hold values from 512 to 1024
- pair_occupation: int32 [2, 32, 1024], P(None, 'chan'), may hold values 0 or 1
- recoupled_occupation: int32 [2, 32, 1024], P(None, ('chan', 'tile')), may hold values 0 or 1
- recouple_map: int32 [32, 1024], P(('chan', 'tile')), may hold values from 0 to 1023, each once within a row
- recouple_weights: float32 [32, 1024, 1024], P(('chan', 'tile')), may hold values from -2 to 2
Outputs:
- commutator: bfloat16 [32, 1024, 1024], P('chan', 'tile')
The draws below stay inside these ranges and needn't reach their ends.
Inputs may be any that keep to these rules, and one draw needn't show every extreme that they name: generator[c] is antisymmetric and hamiltonian[c] is symmetric in every channel.
All inputs are finite; a program needn't handle non-finite values. No bound on the sum of `pair_occupation` or of `recoupled_occupation` on one device may be relied on, other than what follows from the above.
Results may differ from the reference program's by a relative error of at most 0.0045.
Values may be sent and summed in bfloat16 or wider, within the bound.
No kernel may reach another device: no remote copies, remote signals or barrier semaphores. Data moves between devices by JAX's collectives and lax.ppermute only.
A program may use at most 128 MiB of HBM per device.

```python
import math
import jax
import jax.numpy as jnp
from jax import lax

M = 1024
CH_DEV = 4
NCH = 32
MP = 1024
PH_DEV = 1
NPH = 32
N_CHAN = 8
N_TILE = 4


def pair_block(key, symmetric):
    base = jax.random.normal(key, (NCH, M, M), jnp.float32) * M ** (-0.25) / math.sqrt(2.0)
    flipped = jnp.swapaxes(base, 1, 2)
    if symmetric:
        return (base + flipped).astype(jnp.bfloat16)
    return (base - flipped).astype(jnp.bfloat16)


def draw_generator(key, part):
    return pair_block(jax.random.fold_in(key, 11), False)


def draw_hamiltonian(key, part):
    return pair_block(jax.random.fold_in(key, 12), True)


def place_ends(array, own_key, least, high):
    extent = array.shape
    spot = [jax.random.randint(jax.random.fold_in(own_key, axis), (), 0, extent[axis]) for axis in range(len(extent))]
    array = array.at[tuple(spot)].set(least)
    longest = extent.index(max(extent))
    spot[longest] = (spot[longest] + 1) % extent[longest]
    return array.at[tuple(spot)].set(high)


def block_scale(own_key, shape, pieces, low, high):
    def one(position, shards_of):
        draws = jax.random.uniform(jax.random.fold_in(jax.random.fold_in(own_key, 6), position), (shards_of,), jnp.float32, low / len(pieces), high / len(pieces))
        return jnp.repeat(jnp.exp(draws), shape[position] // shards_of).reshape((-1,) + (1,) * (len(shape) - position - 1))

    level = one(*pieces[0])
    for cut in pieces[1:]:
        level = level * one(*cut)
    return level


def setup_inputs(seed: int = 0) -> dict:
    splits = jax.random.split(jax.random.key(seed), 8)
    return {
        "generator": draw_generator(jax.random.fold_in(splits[7], 71), 0),
        "hamiltonian": draw_hamiltonian(jax.random.fold_in(splits[7], 71), 0),
        "chan_sizes": place_ends(jax.random.randint(splits[2], (NCH,), M // 2, M + 1), jax.random.fold_in(splits[2], 1), M // 2, M).astype(jnp.int32),
        "pair_occupation": place_ends((jax.random.randint(splits[3], (2, NCH, M), 0, 4) < 1).astype(jnp.int32), jax.random.fold_in(splits[3], 1), 0, 1),
        "recoupled_occupation": place_ends((jax.random.randint(splits[4], (2, NPH, MP), 0, 2) < 1).astype(jnp.int32), jax.random.fold_in(splits[4], 1), 0, 1),
        "recouple_map": jax.vmap(lambda own: jax.random.permutation(own, MP))(jax.random.split(splits[5], NPH)).reshape((NPH, MP)).astype(jnp.int32),
        "recouple_weights": jnp.clip(jax.random.uniform(splits[6], (NPH, MP, MP), jnp.float32, -2.0, 2.0) * block_scale(splits[6], (NPH, MP, MP), ((0, 32),), -0.4, 0.0), -2.0, 2.0),
    }


def to_recoupled(values):
    tile_rows = M // N_TILE
    group_rows = CH_DEV * tile_rows // N_CHAN
    shaped = values.reshape(N_CHAN, CH_DEV, N_TILE, tile_rows, M)
    shaped = jnp.transpose(shaped, (0, 2, 1, 3, 4))
    shaped = shaped.reshape(N_CHAN, N_TILE, N_CHAN, group_rows, PH_DEV, MP)
    shaped = jnp.transpose(shaped, (2, 1, 4, 0, 3, 5))
    return shaped.reshape(NPH, MP, MP)


def from_recoupled(values):
    tile_rows = M // N_TILE
    group_rows = CH_DEV * tile_rows // N_CHAN
    shaped = values.reshape(N_CHAN, N_TILE, PH_DEV, N_CHAN, group_rows, MP)
    shaped = jnp.transpose(shaped, (3, 1, 0, 4, 2, 5))
    shaped = shaped.reshape(N_CHAN, N_TILE, CH_DEV, tile_rows, M)
    shaped = jnp.transpose(shaped, (0, 2, 1, 3, 4))
    return shaped.reshape(NCH, M, M)


def ladder_one(items):
    left, right, weight = items
    first = jnp.dot(left * weight[None, :], right, preferred_element_type=jnp.float32)
    second = jnp.dot(right * weight[None, :], left, preferred_element_type=jnp.float32)
    return first - second


def crossed_one(items):
    left, right, column_map, weights, occ_first, occ_second = items
    left_bar = (jnp.take(left, column_map, axis=1).astype(jnp.float32) * weights).astype(jnp.bfloat16)
    right_bar = (jnp.take(right, column_map, axis=1).astype(jnp.float32) * weights).astype(jnp.bfloat16)
    signs = (occ_first - occ_second).astype(jnp.bfloat16)
    crossed = jnp.dot(left_bar * signs[None, :], right_bar, preferred_element_type=jnp.float32)
    crossed = crossed - jnp.dot(right_bar * signs[None, :], left_bar, preferred_element_type=jnp.float32)
    inverse = jnp.argsort(column_map).astype(jnp.int32)
    return jnp.take(crossed * weights, inverse, axis=1).astype(jnp.bfloat16)


def reference(generator, hamiltonian, chan_sizes, pair_occupation, recoupled_occupation, recouple_map, recouple_weights):
    states = jnp.arange(M, dtype=jnp.int32)
    live_vec = states[None, :] < chan_sizes[:, None]
    live_mask = live_vec[:, :, None] & live_vec[:, None, :]
    zero = jnp.zeros((), jnp.bfloat16)
    eta_live = jnp.where(live_mask, generator, zero)
    gamma_live = jnp.where(live_mask, hamiltonian, zero)
    weight = ((1 - pair_occupation[0] - pair_occupation[1]) * live_vec.astype(jnp.int32)).astype(jnp.bfloat16)
    ladder = lax.map(ladder_one, (eta_live, gamma_live, weight))
    back_bar = lax.map(crossed_one, (to_recoupled(eta_live), to_recoupled(gamma_live), recouple_map, recouple_weights, recoupled_occupation[0], recoupled_occupation[1]))
    back = from_recoupled(back_bar)
    total = ladder + back.astype(jnp.float32)
    return jnp.where(live_mask, total, jnp.zeros((), jnp.float32)).astype(jnp.bfloat16)
```

```python
import functools

import jax
import jax.numpy as jnp
from jax import lax
from jax.experimental import pallas as pl
from jax.experimental.pallas import tpu as pltpu
from jax.sharding import PartitionSpec as P

BF16 = jnp.bfloat16
F32 = jnp.float32
ANY = pl.BlockSpec(memory_space=pl.ANY)
VMEM = pl.BlockSpec(memory_space=pltpu.VMEM)
SMEM = pl.BlockSpec(memory_space=pltpu.SMEM)


def params(mib):
    return pltpu.CompilerParams(vmem_limit_bytes=mib << 20)


def xor_permute(block, axis, size, step):
    return lax.ppermute(block, axis, [(i, i ^ step) for i in range(size)])


def aligned(start, size):
    return pl.ds(pl.multiple_of(start, size), size)


def row_tiles(states):
    rows = min(256, states)
    return [(start, rows) for start in range(0, states, rows)]


def prepare_kernel(ph_count, states, map_ref, occ_ref, weights_ref, turned_ref, select_ref):
    for q in range(ph_count):
        map_row = map_ref[q : q + 1, :]
        signs = (occ_ref[0, q : q + 1, :] - occ_ref[1, q : q + 1, :]).astype(F32)
        for start, rows in row_tiles(states):
            here = lax.broadcasted_iota(jnp.int32, (rows, states), 0) + start == map_row
            hot = jnp.where(here, 1.0, 0.0).astype(F32)
            select_ref[q, start : start + rows, :] = (hot * signs).astype(BF16)
            hot = hot.astype(BF16)
            for top, height in row_tiles(states):
                rest = weights_ref[q, top : top + height, :]
                total = jnp.zeros((height, rows), F32)
                for _ in range(3):
                    part = rest.astype(BF16)
                    rest = rest - part.astype(F32)
                    total = total + lax.dot_general(
                        part, hot, (((1,), (1,)), ((), ())), preferred_element_type=F32
                    )
                turned_ref[q, top : top + height, start : start + rows] = total


def prepare(recouple_map, recoupled_occupation, recouple_weights):
    ph_count, states = recouple_map.shape
    return pl.pallas_call(
        functools.partial(prepare_kernel, ph_count, states),
        out_shape=(
            jax.ShapeDtypeStruct(recouple_weights.shape, F32),
            jax.ShapeDtypeStruct(recouple_weights.shape, BF16),
        ),
        in_specs=[VMEM] * 3,
        out_specs=(VMEM, VMEM),
        compiler_params=params(40),
        name="prepare",
    )(recouple_map, recoupled_occupation, recouple_weights)


def block_starts(me, blocks, rows):
    return [(me ^ d) * rows for d in range(blocks)]


def left_kernel(ph_count, states, blocks, me_ref, turned_ref, select_ref, *rest):
    recv_refs, (bar_ref, left_ref, recv, sems) = rest[:blocks], rest[blocks:]
    rows = recv_refs[0].shape[0]
    copies = []
    for d, start in enumerate(block_starts(me_ref[0], blocks, rows)):
        copy = pltpu.make_async_copy(recv_refs[d], recv.at[aligned(start, rows), :], sems.at[d])
        copy.start()
        copies.append(copy)
    for copy in copies:
        copy.wait()
    for q in range(ph_count):
        for top, height in row_tiles(states):
            span = slice(top, top + height)
            values = recv[span, q * states : (q + 1) * states].astype(F32) * turned_ref[q, span, :]
            values = values.astype(BF16)
            bar_ref[q, span, :] = values
            left_ref[q, span, :] = jnp.dot(
                values, select_ref[q], preferred_element_type=F32
            ).astype(BF16)


def left_operand(me, turned, select, received):
    ph_count, states, _ = turned.shape
    blocks = len(received)
    return pl.pallas_call(
        functools.partial(left_kernel, ph_count, states, blocks),
        out_shape=(
            jax.ShapeDtypeStruct(turned.shape, BF16),
            jax.ShapeDtypeStruct(turned.shape, BF16),
        ),
        in_specs=[SMEM, VMEM, VMEM] + [ANY] * blocks,
        out_specs=(VMEM, VMEM),
        scratch_shapes=[
            pltpu.VMEM((states, ph_count * states), BF16),
            pltpu.SemaphoreType.DMA((blocks,)),
        ],
        compiler_params=params(40),
        name="left_operand",
    )(me, turned, select, *received)


def crossed_kernel(
    ph_count, states, blocks, me_ref, turned_ref, select_ref, eta_bar_ref, eta_left_ref, *rest
):
    recv_refs, out_refs = rest[:blocks], rest[blocks : 2 * blocks]
    recv, bar, left, back, sems = rest[2 * blocks :]
    rows = recv_refs[0].shape[0]
    starts = block_starts(me_ref[0], blocks, rows)
    copies = []
    for d, start in enumerate(starts):
        copy = pltpu.make_async_copy(recv_refs[d], recv.at[aligned(start, rows), :], sems.at[d])
        copy.start()
        copies.append(copy)
    for copy in copies:
        copy.wait()
    for q in range(ph_count):
        columns = slice(q * states, (q + 1) * states)
        for top, height in row_tiles(states):
            span = slice(top, top + height)
            values = recv[span, columns].astype(F32) * turned_ref[q, span, :]
            values = values.astype(BF16)
            bar[span, :] = values
            left[span, :] = jnp.dot(values, select_ref[q], preferred_element_type=F32).astype(BF16)
        for top, height in row_tiles(states):
            span = slice(top, top + height)
            crossed = jnp.dot(eta_left_ref[q, span, :], bar[...], preferred_element_type=F32)
            crossed = crossed - jnp.dot(
                left[span, :], eta_bar_ref[q], preferred_element_type=F32
            )
            back[span, columns] = (crossed * turned_ref[q, span, :]).astype(BF16)
    copies = []
    for d, start in enumerate(starts):
        copy = pltpu.make_async_copy(back.at[aligned(start, rows), :], out_refs[d], sems.at[d])
        copy.start()
        copies.append(copy)
    for copy in copies:
        copy.wait()


def crossed_blocks(me, turned, select, eta_bar, eta_left, received):
    ph_count, states, _ = turned.shape
    blocks = len(received)
    return pl.pallas_call(
        functools.partial(crossed_kernel, ph_count, states, blocks),
        out_shape=[jax.ShapeDtypeStruct(block.shape, BF16) for block in received],
        in_specs=[SMEM, VMEM, VMEM, VMEM, VMEM] + [ANY] * blocks,
        out_specs=[ANY] * blocks,
        scratch_shapes=[
            pltpu.VMEM((states, ph_count * states), BF16),
            pltpu.VMEM((states, states), BF16),
            pltpu.VMEM((states, states), BF16),
            pltpu.VMEM((states, ph_count * states), BF16),
            pltpu.SemaphoreType.DMA((blocks,)),
        ],
        compiler_params=params(48),
        name="crossed",
    )(me, turned, select, eta_bar, eta_left, *received)


def pack_kernel(tiles, rows, place_ref, eta_ref, gamma_ref, *rest):
    out_refs, sems = rest[:-1], rest[-1]
    place = place_ref[0]
    copies = []
    for step in range(1, tiles):
        owner = place ^ step
        for n, source in enumerate((eta_ref, gamma_ref)):
            for m, other in enumerate(range(step, tiles)):
                column = owner ^ other
                copies.append(
                    pltpu.make_async_copy(
                        source.at[owner, :, aligned(column * rows, rows)],
                        out_refs[step - 1].at[n, m],
                        sems.at[len(copies)],
                    )
                )
    for copy in copies:
        copy.start()
    for copy in copies:
        copy.wait()


def pack(place, eta, gamma):
    tiles, rows, _ = eta.shape
    return pl.pallas_call(
        functools.partial(pack_kernel, tiles, rows),
        out_shape=[
            jax.ShapeDtypeStruct((2, tiles - step, rows, rows), BF16) for step in range(1, tiles)
        ],
        in_specs=[SMEM, ANY, ANY],
        out_specs=[ANY] * (tiles - 1),
        scratch_shapes=[pltpu.SemaphoreType.DMA((tiles * (tiles - 1),))],
        name="pack",
    )(place, eta, gamma)


def ladder_kernel(tiles, rows, place_ref, sizes_ref, occ_ref, eta_ref, gamma_ref, *rest):
    packed_refs = rest[: tiles - 1]
    out_refs = rest[tiles - 1 : 2 * tiles - 1]
    eta, gamma, weight, sems = rest[2 * tiles - 1 :]
    place = place_ref[0]
    size = sizes_ref[place]
    states = tiles * rows
    copies = []
    for source, full in ((eta_ref, eta), (gamma_ref, gamma)):
        for k in range(tiles):
            copies.append(
                pltpu.make_async_copy(
                    source.at[place, :, aligned((place ^ k) * rows, rows)],
                    full.at[0:rows, k * rows : (k + 1) * rows],
                    sems.at[len(copies)],
                )
            )
    for copy in copies:
        copy.start()
    occupied = occ_ref[0] + occ_ref[1]
    own = lax.broadcasted_iota(jnp.int32, occupied.shape, 0) == place
    free = jnp.sum(jnp.where(own, 1 - occupied, 0), axis=0, keepdims=True)
    free = jnp.where(lax.broadcasted_iota(jnp.int32, free.shape, 1) < size, free, 0)
    weight[...] = free.astype(F32)
    for k in range(1, tiles):
        for n, full in enumerate((eta, gamma)):
            for m, other in enumerate(range(k, tiles)):
                full[k * rows : (k + 1) * rows, other * rows : (other + 1) * rows] = packed_refs[
                    k - 1
                ][n, m]
    for copy in copies:
        copy.wait()
    for k in range(tiles):
        for other in range(k + 1, tiles):
            here, there = slice(k * rows, (k + 1) * rows), slice(other * rows, (other + 1) * rows)
            eta[there, here] = -eta[here, there].T
            gamma[there, here] = gamma[here, there].T
    scale = jnp.concatenate(
        [weight[:, aligned((place ^ k) * rows, rows)] for k in range(tiles)], axis=1
    ).astype(BF16)
    for k in range(tiles):
        here = slice(k * rows, (k + 1) * rows)
        total = jnp.dot(eta[here, :] * scale, gamma[...], preferred_element_type=F32)
        total = total - jnp.dot(gamma[here, :] * scale, eta[...], preferred_element_type=F32)
        total = total.astype(BF16)
        for other in range(tiles):
            out_refs[k][:, aligned((place ^ other) * rows, rows)] = total[
                :, other * rows : (other + 1) * rows
            ]


def ladder_blocks(place, sizes, pair_occupation, eta, gamma, packed):
    tiles, rows, states = eta.shape
    return pl.pallas_call(
        functools.partial(ladder_kernel, tiles, rows),
        out_shape=[jax.ShapeDtypeStruct((rows, states), BF16) for _ in range(tiles)],
        in_specs=[SMEM, SMEM, VMEM, ANY, ANY] + [VMEM] * (tiles - 1),
        out_specs=[VMEM] * tiles,
        scratch_shapes=[
            pltpu.VMEM((states, states), BF16),
            pltpu.VMEM((states, states), BF16),
            pltpu.VMEM((1, states), F32),
            pltpu.SemaphoreType.DMA((2 * tiles,)),
        ],
        compiler_params=params(32),
        name="ladder",
    )(place, sizes, pair_occupation, eta, gamma, *packed)


def finish_kernel(
    chan_count, tile_rows, blocks, ladders, me_ref, place_ref, sizes_ref, *rest
):
    back_refs, ladder_refs = rest[:blocks], rest[blocks : blocks + ladders]
    out_ref, back, ladder, sems = rest[blocks + ladders :]
    place = place_ref[0]
    rows = back_refs[0].shape[0]
    height = ladder_refs[0].shape[0]
    copies = []
    for k in range(ladders):
        copies.append(
            pltpu.make_async_copy(
                ladder_refs[k],
                ladder.at[aligned((place ^ k if ladders > 1 else 0) * height, height), :],
                sems.at[len(copies)],
            )
        )
    for d, start in enumerate(block_starts(me_ref[0], blocks, rows)):
        copies.append(
            pltpu.make_async_copy(
                back_refs[d], back.at[aligned(start, rows), :], sems.at[len(copies)]
            )
        )
    for copy in copies:
        copy.start()
    for copy in copies:
        copy.wait()
    states = out_ref.shape[2]
    for c in range(chan_count):
        size = sizes_ref[c]
        span = slice(c * tile_rows, (c + 1) * tile_rows)
        total = ladder[span, :].astype(F32) + back[span, :].astype(F32)
        row = place * tile_rows + lax.broadcasted_iota(jnp.int32, (tile_rows, states), 0)
        column = lax.broadcasted_iota(jnp.int32, (tile_rows, states), 1)
        live = jnp.maximum(row, column) < size
        out_ref[c] = jnp.where(live, total, 0.0).astype(BF16)


def finish(me, place, sizes, shape, back, ladder):
    chan_count, tile_rows, states = shape
    flat = (chan_count * tile_rows, states)
    return pl.pallas_call(
        functools.partial(finish_kernel, chan_count, tile_rows, len(back), len(ladder)),
        out_shape=jax.ShapeDtypeStruct(shape, BF16),
        in_specs=[SMEM] * 3 + [ANY] * (len(back) + len(ladder)),
        out_specs=VMEM,
        scratch_shapes=[
            pltpu.VMEM(flat, BF16),
            pltpu.VMEM(flat, ladder[0].dtype),
            pltpu.SemaphoreType.DMA((len(back) + len(ladder),)),
        ],
        compiler_params=params(32),
        name="finish",
    )(me, place, sizes, *back, *ladder)


def ladder_gathered(live_columns, pair_occupation, eta_live, gamma_live):
    weight = (1 - pair_occupation[0] - pair_occupation[1]) * live_columns.astype(jnp.int32)
    first = jnp.einsum(
        "crk,ckj->crj",
        eta_live * weight.astype(BF16)[:, None, :],
        lax.all_gather(gamma_live, "tile", axis=1, tiled=True),
        preferred_element_type=F32,
    )
    mirrored = lax.all_to_all(first, "tile", split_axis=2, concat_axis=1, tiled=True)
    total = first + jnp.swapaxes(mirrored, 1, 2)
    return [total.reshape(-1, total.shape[2])]


def per_device(
    chans,
    tiles,
    generator,
    hamiltonian,
    chan_sizes,
    pair_occupation,
    recoupled_occupation,
    recouple_map,
    recouple_weights,
):
    chan_count, tile_rows, states = generator.shape
    block_rows = chan_count * tile_rows
    chan_place = lax.axis_index("chan")
    tile_place = lax.axis_index("tile")
    me = jnp.reshape(chan_place, (1,))
    place = jnp.reshape(tile_place, (1,))
    owned = tiles == chan_count
    stepped = chans <= 8 and chans & (chans - 1) == 0

    columns = lax.broadcasted_iota(jnp.int32, (chan_count, states), 1)
    live_columns = columns < chan_sizes[:, None]
    row_index = tile_place * tile_rows + lax.broadcasted_iota(jnp.int32, (chan_count, tile_rows), 1)
    live_rows = row_index < chan_sizes[:, None]
    live_mask = live_rows[:, :, None] & live_columns[:, None, :]
    zero = jnp.zeros((), BF16)
    eta_live = jnp.where(live_mask, generator, zero)
    gamma_live = jnp.where(live_mask, hamiltonian, zero)

    def cut(values):
        flat = values.reshape(block_rows, states)
        if not stepped:
            return [flat]
        rows = block_rows // chans
        return [
            lax.dynamic_slice_in_dim(flat, (chan_place ^ d) * rows, rows, 0) for d in range(chans)
        ]

    def exchange(blocks):
        if not stepped:
            return [lax.all_to_all(blocks[0], "chan", split_axis=0, concat_axis=0, tiled=True)]
        return [blocks[0]] + [
            xor_permute(block, "chan", chans, d) for d, block in enumerate(blocks) if d
        ]

    recv_eta = exchange(cut(eta_live))
    if owned:
        packed = pack(place, generator, hamiltonian)
        packed = [xor_permute(p, "tile", tiles, k + 1) for k, p in enumerate(packed)]
    recv_gamma = exchange(cut(gamma_live))
    turned, select = prepare(recouple_map, recoupled_occupation, recouple_weights)
    eta_bar, eta_left = left_operand(me, turned, select, recv_eta)
    if owned:
        ladder = ladder_blocks(place, chan_sizes, pair_occupation, generator, hamiltonian, packed)
        ladder = [ladder[0]] + [
            xor_permute(block, "tile", tiles, k) for k, block in enumerate(ladder) if k
        ]
    else:
        ladder = ladder_gathered(live_columns, pair_occupation, eta_live, gamma_live)
    back = exchange(crossed_blocks(me, turned, select, eta_bar, eta_left, recv_gamma))
    return finish(me, place, chan_sizes, generator.shape, back, ladder)


def solution(mesh):
    return jax.shard_map(
        functools.partial(per_device, mesh.shape["chan"], mesh.shape["tile"]),
        mesh=mesh,
        in_specs=(
            P("chan", "tile", None),
            P("chan", "tile", None),
            P("chan"),
            P(None, "chan", None),
            P(None, ("chan", "tile"), None),
            P(("chan", "tile"), None),
            P(("chan", "tile"), None, None),
        ),
        out_specs=P("chan", "tile", None),
        check_vma=False,
    )
```

```python
import functools

import jax
import jax.numpy as jnp
from jax import lax
from jax.experimental import pallas as pl
from jax.experimental.pallas import tpu as pltpu
from jax.sharding import PartitionSpec as P

BF16 = jnp.bfloat16
F32 = jnp.float32
ANY = pl.BlockSpec(memory_space=pl.ANY)
VMEM = pl.BlockSpec(memory_space=pltpu.VMEM)
SMEM = pl.BlockSpec(memory_space=pltpu.SMEM)


def params(mib):
    return pltpu.CompilerParams(vmem_limit_bytes=mib << 20)


def xor_permute(block, axis, size, step):
    return lax.ppermute(block, axis, [(i, i ^ step) for i in range(size)])


def aligned(start, size):
    return pl.ds(pl.multiple_of(start, size), size)


def row_tiles(states):
    rows = min(256, states)
    return [(start, rows) for start in range(0, states, rows)]


def block_order(blocks):
    half = list(range(0, blocks, 2))
    return half, [d for d in range(blocks) if d not in half]


def prepare_kernel(
    ph_count, states, order, me_ref, map_ref, occ_ref, weights_ref, turned_ref, select_ref
):
    rows = states // len(order)
    for q in range(ph_count):
        map_row = map_ref[q : q + 1, :]
        spans = [aligned((me_ref[0] ^ d) * rows, rows) for d in order]
        kept_map = jnp.concatenate([map_ref[q : q + 1, s] for s in spans], axis=1)
        signs = jnp.concatenate(
            [occ_ref[0, q : q + 1, s] - occ_ref[1, q : q + 1, s] for s in spans], axis=1
        ).astype(F32)
        for start, height in row_tiles(states):
            index = lax.broadcasted_iota(jnp.int32, (height, states), 0) + start
            select_ref[q, start : start + height, :] = jnp.where(
                index == kept_map, signs, 0.0
            ).astype(BF16)
            hot = jnp.where(index == map_row, 1.0, 0.0).astype(BF16)
            for top, tall in row_tiles(states):
                rest = weights_ref[q, top : top + tall, :]
                total = jnp.zeros((tall, height), F32)
                for _ in range(3):
                    part = rest.astype(BF16)
                    rest = rest - part.astype(F32)
                    total = total + lax.dot_general(
                        part, hot, (((1,), (1,)), ((), ())), preferred_element_type=F32
                    )
                turned_ref[q, top : top + tall, start : start + height] = total


def prepare(me, order, recouple_map, recoupled_occupation, recouple_weights):
    ph_count, states = recouple_map.shape
    return pl.pallas_call(
        functools.partial(prepare_kernel, ph_count, states, order),
        out_shape=(
            jax.ShapeDtypeStruct(recouple_weights.shape, F32),
            jax.ShapeDtypeStruct(recouple_weights.shape, BF16),
        ),
        in_specs=[SMEM] + [VMEM] * 3,
        out_specs=(VMEM, VMEM),
        compiler_params=params(12),
        name="prepare",
    )(me, recouple_map, recoupled_occupation, recouple_weights)


def weigh_blocks(states, order, me, turned_ref, select_ref, recv_refs, bar_ref, left_ref):
    for recv_ref, (slot, d) in zip(recv_refs, enumerate(order)):
        rows = recv_ref.shape[1]
        span = aligned((me ^ d) * rows, rows)
        for q in range(turned_ref.shape[0]):
            weights = turned_ref[q, span, :]
            for n in range(2):
                values = recv_ref[n, :, q * states : (q + 1) * states].astype(F32) * weights
                bar_ref[n, q, slot * rows : (slot + 1) * rows, :] = values.astype(BF16)
    for q in range(turned_ref.shape[0]):
        for n in range(2):
            for top, height in row_tiles(bar_ref.shape[2]):
                span = slice(top, top + height)
                left_ref[n, q, span, :] = jnp.dot(
                    bar_ref[n, q, span, :], select_ref[q], preferred_element_type=F32
                ).astype(BF16)


def weigh_kernel(states, order, me_ref, turned_ref, select_ref, *rest):
    weigh_blocks(states, order, me_ref[0], turned_ref, select_ref, rest[:-2], *rest[-2:])


def weigh(me, order, turned, select, received):
    ph_count, states, _ = turned.shape
    rows = received[0].shape[1]
    shape = jax.ShapeDtypeStruct((2, ph_count, rows * len(order), states), BF16)
    return pl.pallas_call(
        functools.partial(weigh_kernel, states, order),
        out_shape=(shape, shape),
        in_specs=[SMEM] + [VMEM] * (2 + len(order)),
        out_specs=(VMEM, VMEM),
        compiler_params=params(8),
        name="weigh",
    )(me, turned, select, *received)


def crossed_kernel(
    states, first, second, me_ref, turned_ref, select_ref, bar_ref, left_ref, *rest
):
    blocks = len(first) + len(second)
    recv_refs, out_refs = rest[: len(second)], rest[len(second) : len(second) + blocks]
    scratch = rest[len(second) + blocks :]
    me = me_ref[0]
    halves = [(first, bar_ref, left_ref)]
    if second:
        weigh_blocks(states, second, me, turned_ref, select_ref, recv_refs, *scratch)
        halves.append((second, *scratch))
    for q in range(turned_ref.shape[0]):
        columns = slice(q * states, (q + 1) * states)
        for order, _, left in halves:
            for top, height in row_tiles(left.shape[2]):
                crossed = jnp.zeros((height, states), F32)
                start = 0
                for _, bar, _ in halves:
                    inner = slice(start, start + bar.shape[2])
                    start = inner.stop
                    crossed += jnp.dot(
                        left[0, q, top : top + height, inner],
                        bar[1, q],
                        preferred_element_type=F32,
                    )
                    crossed -= jnp.dot(
                        left[1, q, top : top + height, inner],
                        bar[0, q],
                        preferred_element_type=F32,
                    )
                rows = out_refs[0].shape[0]
                step = min(rows, height)
                for base in range(0, height, step):
                    d = order[(top + base) // rows]
                    inside = (top + base) % rows
                    weights = turned_ref[q, aligned((me ^ d) * rows + inside, step), :]
                    out_refs[d][inside : inside + step, columns] = (
                        crossed[base : base + step] * weights
                    ).astype(BF16)


def crossed_blocks(me, order, turned, select, bar, left, received, flat):
    ph_count, states, _ = turned.shape
    first, second = order
    blocks = len(first) + len(second)
    scratch = []
    if second:
        scratch = [pltpu.VMEM((2, ph_count, states - bar.shape[2], states), BF16)] * 2
    return pl.pallas_call(
        functools.partial(crossed_kernel, states, first, second),
        out_shape=[jax.ShapeDtypeStruct((flat[0] // blocks, flat[1]), BF16)] * blocks,
        in_specs=[SMEM] + [VMEM] * (4 + len(second)),
        out_specs=[VMEM] * blocks,
        scratch_shapes=scratch,
        compiler_params=params(16),
        name="crossed",
    )(me, turned, select, bar, left, *received)


def pack_kernel(
    shape, blocks, tiles, me_ref, place_ref, sizes_ref, eta_ref, gamma_ref, *rest
):
    chan_count, tile_rows, states = shape
    block_refs, owner_refs = rest[:blocks], rest[blocks:-3]
    eta, gamma, sems = rest[-3:]
    me, place = me_ref[0], place_ref[0]
    copies = [
        pltpu.make_async_copy(source, full, sems.at[n])
        for n, (source, full) in enumerate(((eta_ref, eta), (gamma_ref, gamma)))
    ]
    for copy in copies:
        copy.start()
    rows = chan_count * tile_rows // blocks
    row = lax.broadcasted_iota(jnp.int32, (rows, states), 0)
    column = lax.broadcasted_iota(jnp.int32, (rows, states), 1)
    for copy in copies:
        copy.wait()
    for d, out_ref in enumerate(block_refs):
        start = (me ^ d) * rows
        chan = start // tile_rows
        inside = start - chan * tile_rows
        live = jnp.maximum(row + (place * tile_rows + inside), column) < sizes_ref[chan]
        for n, full in enumerate((eta, gamma)):
            values = full[chan, aligned(inside, rows), :]
            out_ref[n] = jnp.where(live, values, jnp.zeros_like(values))
    for step, out_ref in enumerate(owner_refs, 1):
        owner = place ^ step
        for n, full in enumerate((eta, gamma)):
            for m, other in enumerate(range(step, tiles)):
                out_ref[n, m] = full[owner, :, aligned((owner ^ other) * tile_rows, tile_rows)]


def pack(me, place, sizes, eta, gamma, blocks, tiles):
    chan_count, rows, states = eta.shape
    shapes = [(2, chan_count * rows // blocks, states)] * blocks
    shapes += [(2, tiles - step, rows, rows) for step in range(1, tiles)]
    out = pl.pallas_call(
        functools.partial(pack_kernel, eta.shape, blocks, tiles),
        out_shape=[jax.ShapeDtypeStruct(shape, BF16) for shape in shapes],
        in_specs=[SMEM] * 3 + [ANY] * 2,
        out_specs=[VMEM] * len(shapes),
        scratch_shapes=[
            pltpu.VMEM(eta.shape, BF16),
            pltpu.VMEM(eta.shape, BF16),
            pltpu.SemaphoreType.DMA((2,)),
        ],
        compiler_params=params(12),
        name="pack",
    )(me, place, sizes, eta, gamma)
    return out[:blocks], out[blocks:]


def ladder_kernel(tiles, rows, place_ref, sizes_ref, occ_ref, eta_ref, gamma_ref, *rest):
    packed_refs = rest[: tiles - 1]
    out_refs = rest[tiles - 1 : 2 * tiles - 1]
    eta, gamma, weight, sems = rest[2 * tiles - 1 :]
    place = place_ref[0]
    size = sizes_ref[place]
    states = tiles * rows
    copies = []
    for source, full in ((eta_ref, eta), (gamma_ref, gamma)):
        for k in range(tiles):
            copies.append(
                pltpu.make_async_copy(
                    source.at[place, :, aligned((place ^ k) * rows, rows)],
                    full.at[0:rows, k * rows : (k + 1) * rows],
                    sems.at[len(copies)],
                )
            )
    for copy in copies:
        copy.start()
    occupied = occ_ref[0] + occ_ref[1]
    own = lax.broadcasted_iota(jnp.int32, occupied.shape, 0) == place
    free = jnp.sum(jnp.where(own, 1 - occupied, 0), axis=0, keepdims=True)
    free = jnp.where(lax.broadcasted_iota(jnp.int32, free.shape, 1) < size, free, 0)
    weight[...] = free.astype(F32)
    for k in range(1, tiles):
        for n, full in enumerate((eta, gamma)):
            for m, other in enumerate(range(k, tiles)):
                full[k * rows : (k + 1) * rows, other * rows : (other + 1) * rows] = packed_refs[
                    k - 1
                ][n, m]
    for copy in copies:
        copy.wait()
    for k in range(tiles):
        for other in range(k + 1, tiles):
            here, there = slice(k * rows, (k + 1) * rows), slice(other * rows, (other + 1) * rows)
            eta[there, here] = -eta[here, there].T
            gamma[there, here] = gamma[here, there].T
    scale = jnp.concatenate(
        [weight[:, aligned((place ^ k) * rows, rows)] for k in range(tiles)], axis=1
    ).astype(BF16)
    for k in range(tiles):
        here = slice(k * rows, (k + 1) * rows)
        total = jnp.dot(eta[here, :] * scale, gamma[...], preferred_element_type=F32)
        total = total - jnp.dot(gamma[here, :] * scale, eta[...], preferred_element_type=F32)
        total = total.astype(BF16)
        for other in range(tiles):
            out_refs[k][:, aligned((place ^ other) * rows, rows)] = total[
                :, other * rows : (other + 1) * rows
            ]


def ladder_blocks(place, sizes, pair_occupation, eta, gamma, packed):
    tiles, rows, states = eta.shape
    return pl.pallas_call(
        functools.partial(ladder_kernel, tiles, rows),
        out_shape=[jax.ShapeDtypeStruct((rows, states), BF16) for _ in range(tiles)],
        in_specs=[SMEM, SMEM, VMEM, ANY, ANY] + [VMEM] * (tiles - 1),
        out_specs=[VMEM] * tiles,
        scratch_shapes=[
            pltpu.VMEM((states, states), BF16),
            pltpu.VMEM((states, states), BF16),
            pltpu.VMEM((1, states), F32),
            pltpu.SemaphoreType.DMA((2 * tiles,)),
        ],
        compiler_params=params(14),
        name="ladder",
    )(place, sizes, pair_occupation, eta, gamma, *packed)


def finish_kernel(blocks, ladders, me_ref, place_ref, sizes_ref, *rest):
    back_refs, ladder_refs = rest[:blocks], rest[blocks : blocks + ladders]
    out_ref, back = rest[blocks + ladders :]
    chan_count, tile_rows, states = out_ref.shape
    place = place_ref[0]
    rows = back_refs[0].shape[0]
    for d, back_ref in enumerate(back_refs):
        back[aligned((me_ref[0] ^ d) * rows, rows), :] = back_ref[...]
    row = lax.broadcasted_iota(jnp.int32, (tile_rows, states), 0) + place * tile_rows
    highest = jnp.maximum(row, lax.broadcasted_iota(jnp.int32, (tile_rows, states), 1))
    for k in range(chan_count):
        c, ladder = (place ^ k, ladder_refs[k][...]) if ladders > 1 else (k, ladder_refs[0][k])
        total = ladder.astype(F32) + back[aligned(c * tile_rows, tile_rows), :].astype(F32)
        out_ref[c] = jnp.where(highest < sizes_ref[c], total, 0.0).astype(BF16)


def finish(me, place, sizes, shape, back, ladder):
    chan_count, tile_rows, states = shape
    return pl.pallas_call(
        functools.partial(finish_kernel, len(back), len(ladder)),
        out_shape=jax.ShapeDtypeStruct(shape, BF16),
        in_specs=[SMEM] * 3 + [VMEM] * (len(back) + len(ladder)),
        out_specs=VMEM,
        scratch_shapes=[pltpu.VMEM((chan_count * tile_rows, states), BF16)],
        compiler_params=params(12),
        name="finish",
    )(me, place, sizes, *back, *ladder)


def ladder_gathered(sizes, pair_occupation, eta, gamma):
    _, rows, states = eta.shape
    columns = lax.broadcasted_iota(jnp.int32, (eta.shape[0], states), 1)
    weight = (1 - pair_occupation[0] - pair_occupation[1]) * (columns < sizes[:, None])
    first = jnp.einsum(
        "crk,ckj->crj",
        eta * weight.astype(BF16)[:, None, :],
        lax.all_gather(gamma, "tile", axis=1, tiled=True),
        preferred_element_type=F32,
    )
    mirrored = lax.all_to_all(first, "tile", split_axis=2, concat_axis=1, tiled=True)
    return first + jnp.swapaxes(mirrored, 1, 2)


def per_device(
    chans,
    tiles,
    generator,
    hamiltonian,
    chan_sizes,
    pair_occupation,
    recoupled_occupation,
    recouple_map,
    recouple_weights,
):
    chan_count, tile_rows, states = generator.shape
    flat = (chan_count * tile_rows, states)
    me = jnp.reshape(lax.axis_index("chan"), (1,))
    place = jnp.reshape(lax.axis_index("tile"), (1,))
    owned = tiles == chan_count
    stepped = chans <= 8 and chans & (chans - 1) == 0 and tile_rows % (flat[0] // chans) == 0
    blocks = chans if stepped else chan_count
    order = block_order(chans) if stepped else ([0], [])

    def exchange(sent):
        return [sent[0]] + [
            xor_permute(block, "chan", chans, d) for d, block in enumerate(sent) if d
        ]

    def exchange_whole(values):
        return [lax.all_to_all(values, "chan", values.ndim - 2, values.ndim - 2, tiled=True)]

    packed, owned_blocks = pack(
        me if stepped else jnp.zeros_like(me),
        place,
        chan_sizes,
        generator,
        hamiltonian,
        blocks,
        tiles if owned else 1,
    )
    if stepped:
        received = exchange(packed)
    else:
        received = exchange_whole(jnp.concatenate(packed, axis=1))
        me = jnp.zeros_like(me)
    if owned:
        lacking = [xor_permute(p, "tile", tiles, k) for k, p in enumerate(owned_blocks, 1)]
    turned, select = prepare(
        me, order[0] + order[1], recouple_map, recoupled_occupation, recouple_weights
    )
    bar, left = weigh(me, order[0], turned, select, [received[d] for d in order[0]])
    if owned:
        ladder = ladder_blocks(place, chan_sizes, pair_occupation, generator, hamiltonian, lacking)
        ladder = [ladder[0]] + [
            xor_permute(block, "tile", tiles, k) for k, block in enumerate(ladder) if k
        ]
    else:
        ladder = [ladder_gathered(chan_sizes, pair_occupation, generator, hamiltonian)]
    back = crossed_blocks(
        me, order, turned, select, bar, left, [received[d] for d in order[1]], flat
    )
    back = exchange(back) if stepped else exchange_whole(back[0])
    return finish(me, place, chan_sizes, generator.shape, back, ladder)


def solution(mesh):
    return jax.shard_map(
        functools.partial(per_device, mesh.shape["chan"], mesh.shape["tile"]),
        mesh=mesh,
        in_specs=(
            P("chan", "tile", None),
            P("chan", "tile", None),
            P("chan"),
            P(None, "chan", None),
            P(None, ("chan", "tile"), None),
            P(("chan", "tile"), None),
            P(("chan", "tile"), None, None),
        ),
        out_specs=P("chan", "tile", None),
        check_vma=False,
    )
```

```python
import functools

import jax
import jax.numpy as jnp
from jax import lax
from jax.experimental import pallas as pl
from jax.experimental.pallas import tpu as pltpu
from jax.sharding import PartitionSpec as P

BF16 = jnp.bfloat16
F32 = jnp.float32
HBM = pl.BlockSpec(memory_space=pltpu.HBM)
VMEM = pl.BlockSpec(memory_space=pltpu.VMEM)
NT = (((1,), (1,)), ((), ()))
SMEM = pl.BlockSpec(memory_space=pltpu.SMEM)


def params(mib):
    return pltpu.CompilerParams(vmem_limit_bytes=mib << 20)


def cost(flops, moved):
    return pl.CostEstimate(flops=int(flops), bytes_accessed=int(moved), transcendentals=0)


def xor_permute(block, axis, size, step):
    return lax.ppermute(block, axis, [(i, i ^ step) for i in range(size)])


def after(message, *arrived):
    return lax.optimization_barrier((message, *arrived))[0]


def aligned(start, size):
    return pl.ds(pl.multiple_of(start, size), size)


def row_tiles(states):
    rows = min(256, states)
    return [(start, rows) for start in range(0, states, rows)]


def block_order(blocks):
    half = list(range(0, blocks, 2))
    return half, [d for d in range(blocks) if d not in half]


def prepare_kernel(
    ph_count, states, order, me_ref, map_ref, occ_ref, weights_ref, turned_ref, select_ref
):
    rows = states // len(order)
    for q in range(ph_count):
        map_row = map_ref[q : q + 1, :]
        spans = [aligned((me_ref[0] ^ d) * rows, rows) for d in order]
        kept_map = jnp.concatenate([map_ref[q : q + 1, s] for s in spans], axis=1)
        signs = jnp.concatenate(
            [occ_ref[0, q : q + 1, s] - occ_ref[1, q : q + 1, s] for s in spans], axis=1
        ).astype(F32)
        for start, height in row_tiles(states):
            index = lax.broadcasted_iota(jnp.int32, (height, states), 0) + start
            select_ref[q, start : start + height, :] = jnp.where(
                index == kept_map, signs, 0.0
            ).astype(BF16)
            hot = jnp.where(index == map_row, 1.0, 0.0).astype(BF16)
            for top, tall in row_tiles(states):
                rest = weights_ref[q, top : top + tall, :]
                total = jnp.zeros((tall, height), F32)
                for _ in range(3):
                    part = rest.astype(BF16)
                    rest = rest - part.astype(F32)
                    total = total + lax.dot_general(
                        part, hot, NT, preferred_element_type=F32
                    )
                turned_ref[q, top : top + tall, start : start + height] = total


def prepare(me, order, recouple_map, recoupled_occupation, recouple_weights):
    ph_count, states = recouple_map.shape
    return pl.pallas_call(
        functools.partial(prepare_kernel, ph_count, states, order),
        out_shape=(
            jax.ShapeDtypeStruct(recouple_weights.shape, F32),
            jax.ShapeDtypeStruct(recouple_weights.shape, BF16),
        ),
        in_specs=[SMEM] + [VMEM] * 3,
        out_specs=(VMEM, VMEM),
        compiler_params=params(12),
        cost_estimate=cost(6 * ph_count * states**3, 14 * ph_count * states**2),
        name="prepare",
    )(me, recouple_map, recoupled_occupation, recouple_weights)


def weigh_blocks(states, order, me, turned_ref, recv_refs, bar_ref):
    for recv_ref, (slot, d) in zip(recv_refs, enumerate(order)):
        rows = recv_ref.shape[1]
        span = aligned((me ^ d) * rows, rows)
        for q in range(turned_ref.shape[0]):
            weights = turned_ref[q, span, :]
            for n in range(2):
                values = recv_ref[n, :, q * states : (q + 1) * states].astype(F32) * weights
                bar_ref[n, q, slot * rows : (slot + 1) * rows, :] = values.astype(BF16)


def turn_blocks(select_ref, bar_ref, left_ref):
    for q in range(select_ref.shape[0]):
        for n in range(2):
            for top, height in row_tiles(bar_ref.shape[2]):
                span = slice(top, top + height)
                left_ref[n, q, span, :] = jnp.dot(
                    bar_ref[n, q, span, :], select_ref[q], preferred_element_type=F32
                ).astype(BF16)


def cross_blocks(states, order, me, turned_ref, left_ref, bar_refs, out_refs):
    rows = out_refs[0].shape[0]
    for q in range(turned_ref.shape[0]):
        columns = slice(q * states, (q + 1) * states)
        for top, height in row_tiles(left_ref.shape[2]):
            span = slice(top, top + height)
            crossed = jnp.zeros((height, states), F32)
            start = 0
            for bar_ref in bar_refs:
                inner = slice(start, start + bar_ref.shape[2])
                start = inner.stop
                for n, sign in ((0, 1), (1, -1)):
                    crossed += sign * jnp.dot(
                        left_ref[n, q, span, inner], bar_ref[1 - n, q], preferred_element_type=F32
                    )
            step = min(rows, height)
            for base in range(0, height, step):
                slot, inside = divmod(top + base, rows)
                weights = turned_ref[q, aligned((me ^ order[slot]) * rows + inside, step), :]
                out_refs[slot][inside : inside + step, columns] = (
                    crossed[base : base + step] * weights
                ).astype(BF16)


def first_kernel(states, order, me_ref, turned_ref, select_ref, *rest):
    recv_refs, (bar_ref, left_ref) = rest[:-2], rest[-2:]
    weigh_blocks(states, order, me_ref[0], turned_ref, recv_refs, bar_ref)
    turn_blocks(select_ref, bar_ref, left_ref)


def first_half(me, order, turned, select, received):
    ph_count, states, _ = turned.shape
    rows = received[0].shape[1]
    shape = jax.ShapeDtypeStruct((2, ph_count, rows * len(order), states), BF16)
    return pl.pallas_call(
        functools.partial(first_kernel, states, order),
        out_shape=(shape, shape),
        in_specs=[SMEM] + [VMEM] * (2 + len(order)),
        out_specs=(VMEM, VMEM),
        compiler_params=params(8),
        cost_estimate=cost(4 * ph_count * shape.shape[2] * states**2, 14 * ph_count * states**2),
        name="first_half",
    )(me, turned, select, *received)


def cross_first_kernel(states, order, me_ref, turned_ref, bar_ref, left_ref, *rest):
    first, second = order
    recv_refs, out_refs = rest[: len(second)], rest[len(second) : len(second) + len(first)]
    bar_refs = [bar_ref]
    if second:
        weigh_blocks(states, second, me_ref[0], turned_ref, recv_refs, rest[-1])
        bar_refs.append(rest[-1])
    cross_blocks(states, first, me_ref[0], turned_ref, left_ref, bar_refs, out_refs)


def cross_first(me, order, turned, bar, left, received, flat):
    ph_count, states, _ = turned.shape
    first, second = order
    blocks = len(first) + len(second)
    out_shape = [jax.ShapeDtypeStruct((flat[0] // blocks, flat[1]), BF16)] * len(first)
    if second:
        out_shape.append(
            jax.ShapeDtypeStruct((2, ph_count, states - bar.shape[2], states), BF16)
        )
    out = pl.pallas_call(
        functools.partial(cross_first_kernel, states, order),
        out_shape=out_shape,
        in_specs=[SMEM] + [VMEM] * (3 + len(second)),
        out_specs=[VMEM] * len(out_shape),
        compiler_params=params(8),
        cost_estimate=cost(2 * ph_count * states**3, 14 * ph_count * states**2),
        name="cross_first",
    )(me, turned, bar, left, *received)
    return out[: len(first)], out[-1]


def cross_second_kernel(
    states, order, me_ref, turned_ref, select_ref, bar_ref, second_bar_ref, *rest
):
    out_refs, left_ref = rest[:-1], rest[-1]
    turn_blocks(select_ref, second_bar_ref, left_ref)
    cross_blocks(
        states, order, me_ref[0], turned_ref, left_ref, [bar_ref, second_bar_ref], out_refs
    )


def cross_second(me, order, turned, select, bar, second_bar, flat, blocks):
    ph_count, states, _ = turned.shape
    return pl.pallas_call(
        functools.partial(cross_second_kernel, states, order),
        out_shape=[jax.ShapeDtypeStruct((flat[0] // blocks, flat[1]), BF16)] * len(order),
        in_specs=[SMEM] + [VMEM] * 4,
        out_specs=[VMEM] * len(order),
        scratch_shapes=[pltpu.VMEM(second_bar.shape, BF16)],
        compiler_params=params(12),
        cost_estimate=cost(4 * ph_count * states**3, 14 * ph_count * states**2),
        name="cross_second",
    )(me, turned, select, bar, second_bar)


def pack_rows_kernel(shape, blocks, partners, me_ref, place_ref, sizes_ref, *rest):
    chan_count, tile_rows, states = shape
    source_refs, out_refs = rest[:2], rest[2 : 2 + len(partners)]
    held, sems = rest[2 + len(partners) :]
    rows = chan_count * tile_rows // blocks
    copies = []
    for slot, d in enumerate(partners):
        start = (me_ref[0] ^ d) * rows
        chan = start // tile_rows
        inside = start - chan * tile_rows
        for n, source_ref in enumerate(source_refs):
            copies.append(
                pltpu.make_async_copy(
                    source_ref.at[chan, aligned(inside, rows), :],
                    held.at[slot, n],
                    sems.at[len(copies)],
                )
            )
    for copy in copies:
        copy.start()
    row = lax.broadcasted_iota(jnp.int32, (rows, states), 0) + place_ref[0] * tile_rows
    column = lax.broadcasted_iota(jnp.int32, (rows, states), 1)
    for slot, d in enumerate(partners):
        start = (me_ref[0] ^ d) * rows
        chan = start // tile_rows
        inside = start - chan * tile_rows
        live = jnp.maximum(row + inside, column) < sizes_ref[chan]
        for n in range(2):
            copies[2 * slot + n].wait()
            values = held[slot, n]
            out_refs[slot][n] = jnp.where(live, values, jnp.zeros_like(values))


def pack_rows(me, place, sizes, eta, gamma, blocks, partners):
    chan_count, tile_rows, states = eta.shape
    shape = (2, chan_count * tile_rows // blocks, states)
    return pl.pallas_call(
        functools.partial(pack_rows_kernel, eta.shape, blocks, partners),
        out_shape=[jax.ShapeDtypeStruct(shape, BF16)] * len(partners),
        in_specs=[SMEM] * 3 + [HBM] * 2,
        out_specs=[VMEM] * len(partners),
        scratch_shapes=[
            pltpu.VMEM((len(partners), *shape), BF16),
            pltpu.SemaphoreType.DMA((2 * len(partners),)),
        ],
        compiler_params=params(8),
        cost_estimate=cost(0, 8 * len(partners) * shape[1] * states),
        name="pack_rows",
    )(me, place, sizes, eta, gamma)


def pack_owners_kernel(tiles, rows, place_ref, eta_ref, gamma_ref, *rest):
    out_refs, sems = rest[:-1], rest[-1]
    copies = []
    for step in range(1, tiles):
        owner = place_ref[0] ^ step
        for n, source_ref in enumerate((eta_ref, gamma_ref)):
            for m, other in enumerate(range(step, tiles)):
                copies.append(
                    pltpu.make_async_copy(
                        source_ref.at[owner, :, aligned((owner ^ other) * rows, rows)],
                        out_refs[step - 1].at[n, m],
                        sems.at[len(copies)],
                    )
                )
    for copy in copies:
        copy.start()
    for copy in copies:
        copy.wait()


def pack_owners(place, eta, gamma):
    tiles, rows, _ = eta.shape
    return pl.pallas_call(
        functools.partial(pack_owners_kernel, tiles, rows),
        out_shape=[
            jax.ShapeDtypeStruct((2, tiles - step, rows, rows), BF16) for step in range(1, tiles)
        ],
        in_specs=[SMEM] + [HBM] * 2,
        out_specs=[VMEM] * (tiles - 1),
        scratch_shapes=[pltpu.SemaphoreType.DMA((tiles * (tiles - 1),))],
        compiler_params=params(8),
        cost_estimate=cost(0, 4 * tiles * (tiles - 1) * rows * rows),
        name="pack_owners",
    )(place, eta, gamma)


def free_weight(occ_ref, chan, size):
    occupied = occ_ref[0] + occ_ref[1]
    own = lax.broadcasted_iota(jnp.int32, occupied.shape, 0) == chan
    free = jnp.sum(jnp.where(own, 1 - occupied, 0), axis=0, keepdims=True)
    live = lax.broadcasted_iota(jnp.int32, free.shape, 1) < size
    return jnp.where(live, free, 0).astype(F32)


def diagonal_kernel(sizes_ref, occ_ref, eta_ref, gamma_ref, out_ref):
    for c in range(eta_ref.shape[0]):
        weight = free_weight(occ_ref, c, sizes_ref[c]).astype(BF16)
        out_ref[c] = lax.dot_general(
            eta_ref[c] * weight, gamma_ref[c], NT, preferred_element_type=F32
        ) + lax.dot_general(gamma_ref[c] * weight, eta_ref[c], NT, preferred_element_type=F32)


def ladder_diagonal(sizes, pair_occupation, eta, gamma):
    chan_count, rows, states = eta.shape
    return pl.pallas_call(
        diagonal_kernel,
        out_shape=jax.ShapeDtypeStruct((chan_count, rows, rows), F32),
        in_specs=[SMEM] + [VMEM] * 3,
        out_specs=VMEM,
        compiler_params=params(8),
        cost_estimate=cost(4 * chan_count * rows * rows * states, 8 * chan_count * rows * states),
        name="ladder_diagonal",
    )(sizes, pair_occupation, eta, gamma)


def ladder_kernel(tiles, rows, place_ref, sizes_ref, occ_ref, eta_ref, gamma_ref, *rest):
    packed_refs = rest[: tiles - 1]
    out_refs = rest[tiles - 1 : 2 * tiles - 1]
    eta, gamma, weight, sems = rest[2 * tiles - 1 :]
    place = place_ref[0]
    copies = []
    for source, full in ((eta_ref, eta), (gamma_ref, gamma)):
        for k in range(tiles):
            copies.append(
                pltpu.make_async_copy(
                    source.at[place, :, aligned((place ^ k) * rows, rows)],
                    full.at[0:rows, k * rows : (k + 1) * rows],
                    sems.at[len(copies)],
                )
            )
    for copy in copies:
        copy.start()
    weight[...] = free_weight(occ_ref, place, sizes_ref[place])
    scale = jnp.concatenate(
        [weight[:, aligned((place ^ k) * rows, rows)] for k in range(tiles)], axis=1
    ).astype(BF16)
    for k in range(1, tiles):
        for n, full in enumerate((eta, gamma)):
            for m, other in enumerate(range(k, tiles)):
                block = packed_refs[k - 1][n, m]
                here, there = slice(k * rows, (k + 1) * rows), slice(other * rows, (other + 1) * rows)
                full[here, there] = block
                if other > k:
                    full[there, here] = block.T if n else -block.T
    for copy in copies:
        copy.wait()
    for other in range(1, tiles):
        here, there = slice(0, rows), slice(other * rows, (other + 1) * rows)
        eta[there, here] = -eta[here, there].T
        gamma[there, here] = gamma[here, there].T
    for k in reversed(range(tiles)):
        here = slice(k * rows, (k + 1) * rows)
        total = jnp.dot(eta[here, :] * scale, gamma[...], preferred_element_type=F32)
        total = total - jnp.dot(gamma[here, :] * scale, eta[...], preferred_element_type=F32)
        for m in range(1, tiles):
            out_refs[k][:, (m - 1) * rows : m * rows] = total[
                :, (k ^ m) * rows : ((k ^ m) + 1) * rows
            ].astype(BF16)


def ladder_blocks(place, sizes, pair_occupation, eta, gamma, packed):
    tiles, rows, states = eta.shape
    return pl.pallas_call(
        functools.partial(ladder_kernel, tiles, rows),
        out_shape=[jax.ShapeDtypeStruct((rows, states - rows), BF16)] * tiles,
        in_specs=[SMEM, SMEM, VMEM, HBM, HBM] + [VMEM] * (tiles - 1),
        out_specs=[VMEM] * tiles,
        scratch_shapes=[
            pltpu.VMEM((states, states), BF16),
            pltpu.VMEM((states, states), BF16),
            pltpu.VMEM((1, states), F32),
            pltpu.SemaphoreType.DMA((2 * tiles,)),
        ],
        compiler_params=params(12),
        cost_estimate=cost(4 * states**3, 8 * states**2),
        name="ladder",
    )(place, sizes, pair_occupation, eta, gamma, *packed)


def finish_kernel(blocks, me_ref, place_ref, sizes_ref, diagonal_ref, *rest):
    back_refs, ladder_refs = rest[:blocks], rest[blocks:-2]
    out_ref, back = rest[-2:]
    chan_count, tile_rows, states = out_ref.shape
    place = place_ref[0]
    rows = back_refs[0].shape[0]
    for d, back_ref in enumerate(back_refs):
        back[aligned((me_ref[0] ^ d) * rows, rows), :] = back_ref[...]
    row = lax.broadcasted_iota(jnp.int32, (tile_rows, tile_rows), 0)
    column = lax.broadcasted_iota(jnp.int32, (tile_rows, tile_rows), 1)
    for k, ladder_ref in enumerate(ladder_refs):
        c = place ^ k
        for m in range(len(ladder_refs)):
            ladder = ladder_ref[:, (m - 1) * tile_rows : m * tile_rows] if m else diagonal_ref[c]
            start = (place ^ m) * tile_rows
            span = aligned(start, tile_rows)
            total = ladder.astype(F32) + back[aligned(c * tile_rows, tile_rows), span].astype(F32)
            live = jnp.maximum(row + place * tile_rows, column + start) < sizes_ref[c]
            out_ref[c, :, span] = jnp.where(live, total, 0.0).astype(BF16)


def finish(me, place, sizes, shape, diagonal, back, ladder):
    chan_count, tile_rows, states = shape
    return pl.pallas_call(
        functools.partial(finish_kernel, len(back)),
        out_shape=jax.ShapeDtypeStruct(shape, BF16),
        in_specs=[SMEM] * 3 + [VMEM] * (1 + len(back) + len(ladder)),
        out_specs=VMEM,
        scratch_shapes=[pltpu.VMEM((chan_count * tile_rows, states), BF16)],
        compiler_params=params(12),
        cost_estimate=cost(0, 6 * chan_count * tile_rows * states),
        name="finish",
    )(me, place, sizes, diagonal, *back, *ladder)


def ladder_gathered(sizes, pair_occupation, eta, gamma):
    _, rows, states = eta.shape
    columns = lax.broadcasted_iota(jnp.int32, (eta.shape[0], states), 1)
    weight = (1 - pair_occupation[0] - pair_occupation[1]) * (columns < sizes[:, None])
    first = jnp.einsum(
        "crk,ckj->crj",
        eta * weight.astype(BF16)[:, None, :],
        lax.all_gather(gamma, "tile", axis=1, tiled=True),
        preferred_element_type=F32,
    )
    mirrored = lax.all_to_all(first, "tile", split_axis=2, concat_axis=1, tiled=True)
    return first + jnp.swapaxes(mirrored, 1, 2)


def per_device(
    chans,
    tiles,
    generator,
    hamiltonian,
    chan_sizes,
    pair_occupation,
    recoupled_occupation,
    recouple_map,
    recouple_weights,
):
    chan_count, tile_rows, states = generator.shape
    flat = (chan_count * tile_rows, states)
    me = jnp.reshape(lax.axis_index("chan"), (1,))
    place = jnp.reshape(lax.axis_index("tile"), (1,))
    paired = chans & (chans - 1) == 0 and tiles & (tiles - 1) == 0
    if not (paired and tiles == chan_count and chans in (tiles, 2 * tiles)):
        return per_device_whole(
            place,
            generator,
            hamiltonian,
            chan_sizes,
            pair_occupation,
            recoupled_occupation,
            recouple_map,
            recouple_weights,
        )

    def to_chan(message, d):
        return xor_permute(message, "chan", chans, d)

    def to_tile(message, k):
        return xor_permute(message, "tile", tiles, k)

    first, second = order = block_order(chans)
    near = [d for d in first if d]
    late = [d for d in range(chans) if d not in near]
    packed = dict(
        zip(near, pack_rows(me, place, chan_sizes, generator, hamiltonian, chans, near))
    )
    received = {d: to_chan(packed[d], d) for d in near}
    lacking = list(pack_owners(place, generator, hamiltonian))
    packed.update(
        zip(late, pack_rows(me, place, chan_sizes, generator, hamiltonian, chans, late))
    )
    turned, select = prepare(
        me, first + second, recouple_map, recoupled_occupation, recouple_weights
    )
    for k in range(1, tiles):
        if k > 2:
            lacking[k - 1] = after(lacking[k - 1], lacking[k - 2], select)
        lacking[k - 1] = to_tile(lacking[k - 1], k)
    received[0] = packed[0]
    for d in near:
        received[d + 1] = to_chan(after(packed[d + 1], received[d], select), d + 1)
    received[1] = to_chan(after(packed[1], lacking[0], select), 1)
    diagonal = ladder_diagonal(chan_sizes, pair_occupation, generator, hamiltonian)

    bar, left = first_half(me, first, turned, select, [received[d] for d in first])
    ladder = ladder_blocks(place, chan_sizes, pair_occupation, generator, hamiltonian, lacking)
    ladder = [to_tile(block, k) if k else block for k, block in enumerate(ladder)]

    back = {}
    sent, second_bar = cross_first(
        me, order, turned, bar, left, [received[d] for d in second], flat
    )
    back[0] = sent[0]
    for d, block in zip(first, sent):
        if d:
            back[d] = to_chan(block, d)
    sent = cross_second(me, second, turned, select, bar, second_bar, flat, chans)
    for d, block in zip(second, sent):
        back[d] = to_chan(block if d == 1 else after(block, back[d - 1]), d)
    back = [back[d] for d in range(chans)]
    return finish(me, place, chan_sizes, generator.shape, diagonal, back, ladder)


def per_device_whole(
    place,
    generator,
    hamiltonian,
    chan_sizes,
    pair_occupation,
    recoupled_occupation,
    recouple_map,
    recouple_weights,
):
    chan_count, tile_rows, states = generator.shape
    flat = (chan_count * tile_rows, states)
    alone = jnp.zeros_like(place)
    row = place * tile_rows + jnp.arange(tile_rows, dtype=jnp.int32)
    highest = jnp.maximum(row[:, None], jnp.arange(states, dtype=jnp.int32)[None, :])
    live = highest[None] < chan_sizes[:, None, None]
    pair = jnp.where(live, jnp.stack([generator, hamiltonian]), jnp.zeros((), BF16))
    received = lax.all_to_all(pair.reshape(2, *flat), "chan", 1, 1, tiled=True)
    order = ([0], [])
    turned, select = prepare(
        alone, order[0], recouple_map, recoupled_occupation, recouple_weights
    )
    bar, left = first_half(alone, order[0], turned, select, [received])
    sent, _ = cross_first(alone, order, turned, bar, left, [], flat)
    back = lax.all_to_all(sent[0], "chan", 0, 0, tiled=True).reshape(generator.shape)
    ladder = ladder_gathered(chan_sizes, pair_occupation, generator, hamiltonian)
    return jnp.where(live, ladder + back.astype(F32), 0.0).astype(BF16)


def solution(mesh):
    return jax.shard_map(
        functools.partial(per_device, mesh.shape["chan"], mesh.shape["tile"]),
        mesh=mesh,
        in_specs=(
            P("chan", "tile", None),
            P("chan", "tile", None),
            P("chan"),
            P(None, "chan", None),
            P(None, ("chan", "tile"), None),
            P(("chan", "tile"), None),
            P(("chan", "tile"), None, None),
        ),
        out_specs=P("chan", "tile", None),
        check_vma=False,
    )
```

```python
import functools

import jax
import jax.numpy as jnp
from jax import lax
from jax.experimental import pallas as pl
from jax.experimental.pallas import tpu as pltpu
from jax.sharding import PartitionSpec as P

BF16 = jnp.bfloat16
F32 = jnp.float32
HBM = pl.BlockSpec(memory_space=pltpu.HBM)
VMEM = pl.BlockSpec(memory_space=pltpu.VMEM)
NT = (((1,), (1,)), ((), ()))
SMEM = pl.BlockSpec(memory_space=pltpu.SMEM)


def params(mib):
    return pltpu.CompilerParams(vmem_limit_bytes=mib << 20)


def cost(flops, moved):
    return pl.CostEstimate(flops=int(flops), bytes_accessed=int(moved), transcendentals=0)


def xor_permute(block, axis, size, step):
    return lax.ppermute(block, axis, [(i, i ^ step) for i in range(size)])


def after(message, *arrived):
    return lax.optimization_barrier((message, *arrived))[0]


def aligned(start, size):
    return pl.ds(pl.multiple_of(start, size), size)


def row_tiles(states):
    rows = min(256, states)
    return [(start, rows) for start in range(0, states, rows)]


def block_order(blocks):
    half = list(range(0, blocks, 2))
    return half, [d for d in range(blocks) if d not in half]


def free_weight(occ_ref, chan, size):
    occupied = occ_ref[0] + occ_ref[1]
    own = lax.broadcasted_iota(jnp.int32, occupied.shape, 0) == chan
    free = jnp.sum(jnp.where(own, 1 - occupied, 0), axis=0, keepdims=True)
    live = lax.broadcasted_iota(jnp.int32, free.shape, 1) < size
    return jnp.where(live, free, 0).astype(F32)


def diagonal_blocks(sizes_ref, occ_ref, eta_ref, gamma_ref, out_ref):
    for c in range(eta_ref.shape[0]):
        weight = free_weight(occ_ref, c, sizes_ref[c]).astype(BF16)
        out_ref[c] = lax.dot_general(
            eta_ref[c] * weight, gamma_ref[c], NT, preferred_element_type=F32
        ) + lax.dot_general(gamma_ref[c] * weight, eta_ref[c], NT, preferred_element_type=F32)


def prepare_kernel(
    ph_count, states, order, me_ref, map_ref, occ_ref, weights_ref, turned_ref, select_ref
):
    rows = states // len(order)
    for q in range(ph_count):
        map_row = map_ref[q : q + 1, :]
        spans = [aligned((me_ref[0] ^ d) * rows, rows) for d in order]
        kept_map = jnp.concatenate([map_ref[q : q + 1, s] for s in spans], axis=1)
        signs = jnp.concatenate(
            [occ_ref[0, q : q + 1, s] - occ_ref[1, q : q + 1, s] for s in spans], axis=1
        ).astype(F32)
        for start, height in row_tiles(states):
            index = lax.broadcasted_iota(jnp.int32, (height, states), 0) + start
            select_ref[q, start : start + height, :] = jnp.where(
                index == kept_map, signs, 0.0
            ).astype(BF16)
            hot = jnp.where(index == map_row, 1.0, 0.0).astype(BF16)
            for top, tall in row_tiles(states):
                rest = weights_ref[q, top : top + tall, :]
                total = jnp.zeros((tall, height), F32)
                for _ in range(3):
                    part = rest.astype(BF16)
                    rest = rest - part.astype(F32)
                    total = total + lax.dot_general(
                        part, hot, NT, preferred_element_type=F32
                    )
                turned_ref[q, top : top + tall, start : start + height] = total


def prepare_whole_kernel(ph_count, states, order, *refs):
    prepare_kernel(ph_count, states, order, *refs[:4], *refs[-3:-1])
    diagonal_blocks(*refs[4:-3], refs[-1])


def prepare(me, order, recouple_map, recoupled_occupation, recouple_weights, *pair):
    ph_count, states = recouple_map.shape
    kernel, extra = prepare_kernel, ()
    flops = 6 * ph_count * states**3
    if pair:
        chan_count, rows, columns = pair[-1].shape
        kernel = prepare_whole_kernel
        extra = (jax.ShapeDtypeStruct((chan_count, rows, rows), F32),)
        flops += 4 * chan_count * rows * rows * columns
    return pl.pallas_call(
        functools.partial(kernel, ph_count, states, order),
        out_shape=(
            jax.ShapeDtypeStruct(recouple_weights.shape, F32),
            jax.ShapeDtypeStruct(recouple_weights.shape, BF16),
            *extra,
        ),
        in_specs=[SMEM] + [VMEM] * 3 + [SMEM] * bool(pair) + [VMEM] * len(pair[1:]),
        out_specs=(VMEM,) * (2 + len(extra)),
        compiler_params=params(12),
        cost_estimate=cost(flops, 14 * ph_count * states**2),
        name="prepare",
    )(me, recouple_map, recoupled_occupation, recouple_weights, *pair)


def weigh_blocks(states, order, me, turned_ref, recv_refs, bar_ref):
    for recv_ref, (slot, d) in zip(recv_refs, enumerate(order)):
        rows = recv_ref.shape[1]
        span = aligned((me ^ d) * rows, rows)
        for q in range(turned_ref.shape[0]):
            weights = turned_ref[q, span, :]
            for n in range(2):
                values = recv_ref[n, :, q * states : (q + 1) * states].astype(F32) * weights
                bar_ref[n, q, slot * rows : (slot + 1) * rows, :] = values.astype(BF16)


def turn_blocks(select_ref, bar_ref, left_ref):
    for q in range(select_ref.shape[0]):
        for n in range(2):
            for top, height in row_tiles(bar_ref.shape[2]):
                span = slice(top, top + height)
                left_ref[n, q, span, :] = jnp.dot(
                    bar_ref[n, q, span, :], select_ref[q], preferred_element_type=F32
                ).astype(BF16)


def cross_blocks(states, order, me, turned_ref, left_ref, bar_refs, out_refs):
    rows = out_refs[0].shape[0]
    for q in range(turned_ref.shape[0]):
        columns = slice(q * states, (q + 1) * states)
        for top, height in row_tiles(left_ref.shape[2]):
            span = slice(top, top + height)
            crossed = jnp.zeros((height, states), F32)
            start = 0
            for bar_ref in bar_refs:
                inner = slice(start, start + bar_ref.shape[2])
                start = inner.stop
                for n, sign in ((0, 1), (1, -1)):
                    crossed += sign * jnp.dot(
                        left_ref[n, q, span, inner], bar_ref[1 - n, q], preferred_element_type=F32
                    )
            step = min(rows, height)
            for base in range(0, height, step):
                slot, inside = divmod(top + base, rows)
                weights = turned_ref[q, aligned((me ^ order[slot]) * rows + inside, step), :]
                out_refs[slot][inside : inside + step, columns] = (
                    crossed[base : base + step] * weights
                ).astype(BF16)


def first_kernel(states, order, me_ref, turned_ref, select_ref, *rest):
    recv_refs, (bar_ref, left_ref) = rest[:-2], rest[-2:]
    weigh_blocks(states, order, me_ref[0], turned_ref, recv_refs, bar_ref)
    turn_blocks(select_ref, bar_ref, left_ref)


def first_half(me, order, turned, select, received):
    ph_count, states, _ = turned.shape
    rows = received[0].shape[1]
    shape = jax.ShapeDtypeStruct((2, ph_count, rows * len(order), states), BF16)
    return pl.pallas_call(
        functools.partial(first_kernel, states, order),
        out_shape=(shape, shape),
        in_specs=[SMEM] + [VMEM] * (2 + len(order)),
        out_specs=(VMEM, VMEM),
        compiler_params=params(8),
        cost_estimate=cost(4 * ph_count * shape.shape[2] * states**2, 14 * ph_count * states**2),
        name="first_half",
    )(me, turned, select, *received)


def cross_first_kernel(states, order, me_ref, turned_ref, bar_ref, left_ref, *rest):
    first, second = order
    recv_refs, out_refs = rest[: len(second)], rest[len(second) : len(second) + len(first)]
    bar_refs = [bar_ref]
    if second:
        weigh_blocks(states, second, me_ref[0], turned_ref, recv_refs, rest[-1])
        bar_refs.append(rest[-1])
    cross_blocks(states, first, me_ref[0], turned_ref, left_ref, bar_refs, out_refs)


def cross_first(me, order, turned, bar, left, received, flat):
    ph_count, states, _ = turned.shape
    first, second = order
    blocks = len(first) + len(second)
    out_shape = [jax.ShapeDtypeStruct((flat[0] // blocks, flat[1]), BF16)] * len(first)
    if second:
        out_shape.append(
            jax.ShapeDtypeStruct((2, ph_count, states - bar.shape[2], states), BF16)
        )
    out = pl.pallas_call(
        functools.partial(cross_first_kernel, states, order),
        out_shape=out_shape,
        in_specs=[SMEM] + [VMEM] * (3 + len(second)),
        out_specs=[VMEM] * len(out_shape),
        compiler_params=params(8),
        cost_estimate=cost(2 * ph_count * states**3, 14 * ph_count * states**2),
        name="cross_first",
    )(me, turned, bar, left, *received)
    return out[: len(first)], out[-1]


def cross_second_kernel(
    states, order, me_ref, turned_ref, select_ref, bar_ref, second_bar_ref, *rest
):
    out_refs, left_ref = rest[:-1], rest[-1]
    turn_blocks(select_ref, second_bar_ref, left_ref)
    cross_blocks(
        states, order, me_ref[0], turned_ref, left_ref, [bar_ref, second_bar_ref], out_refs
    )


def cross_second(me, order, turned, select, bar, second_bar, flat, blocks):
    ph_count, states, _ = turned.shape
    return pl.pallas_call(
        functools.partial(cross_second_kernel, states, order),
        out_shape=[jax.ShapeDtypeStruct((flat[0] // blocks, flat[1]), BF16)] * len(order),
        in_specs=[SMEM] + [VMEM] * 4,
        out_specs=[VMEM] * len(order),
        scratch_shapes=[pltpu.VMEM(second_bar.shape, BF16)],
        compiler_params=params(12),
        cost_estimate=cost(4 * ph_count * states**3, 14 * ph_count * states**2),
        name="cross_second",
    )(me, turned, select, bar, second_bar)


def pack_kernel(shape, blocks, tiles, partners, steps, me_ref, place_ref, sizes_ref, *rest):
    chan_count, tile_rows, states = shape
    source_refs, block_refs = rest[:2], rest[2 : 2 + len(partners)]
    owner_refs, (held, sems) = rest[2 + len(partners) : -2], rest[-2:]
    rows = chan_count * tile_rows // blocks
    place = place_ref[0]
    copies, places = [], []

    def fetch(source, target):
        copies.append(pltpu.make_async_copy(source, target, sems.at[len(copies)]))
        copies[-1].start()

    for slot, d in enumerate(partners):
        start = (me_ref[0] ^ d) * rows
        chan = start // tile_rows
        places.append((chan, start - chan * tile_rows))
        for n, source_ref in enumerate(source_refs):
            fetch(source_ref.at[chan, aligned(places[-1][1], rows), :], held.at[slot, n])
    for step, owner_ref in zip(steps, owner_refs):
        owner = place ^ step
        for n, source_ref in enumerate(source_refs):
            for m, other in enumerate(range(step, tiles)):
                column = aligned((owner ^ other) * tile_rows, tile_rows)
                fetch(source_ref.at[owner, :, column], owner_ref.at[n, m])
    row = lax.broadcasted_iota(jnp.int32, (rows, states), 0) + place * tile_rows
    highest = jnp.maximum(row, lax.broadcasted_iota(jnp.int32, (rows, states), 1))
    for slot, (chan, inside) in enumerate(places):
        live = jnp.maximum(highest, row + inside) < sizes_ref[chan]
        for n in range(2):
            copies[2 * slot + n].wait()
            values = held[slot, n]
            block_refs[slot][n] = jnp.where(live, values, jnp.zeros_like(values))
    for copy in copies[2 * len(partners) :]:
        copy.wait()


def pack(me, place, sizes, eta, gamma, blocks, tiles, partners, steps, mib):
    chan_count, rows, states = eta.shape
    shapes = [(2, chan_count * rows // blocks, states)] * len(partners)
    shapes += [(2, tiles - step, rows, rows) for step in steps]
    out = pl.pallas_call(
        functools.partial(pack_kernel, eta.shape, blocks, tiles, partners, steps),
        out_shape=[jax.ShapeDtypeStruct(shape, BF16) for shape in shapes],
        in_specs=[SMEM] * 3 + [HBM] * 2,
        out_specs=[VMEM] * len(shapes),
        scratch_shapes=[
            pltpu.VMEM((len(partners), *shapes[0]), BF16),
            pltpu.SemaphoreType.DMA((2 * len(partners) + 2 * sum(tiles - s for s in steps),)),
        ],
        compiler_params=params(mib),
        cost_estimate=cost(0, 8 * len(partners) * shapes[0][1] * states),
        name="pack",
    )(me, place, sizes, eta, gamma)
    return dict(zip(partners, out)), dict(zip(steps, out[len(partners) :]))


def ladder_kernel(tiles, rows, place_ref, sizes_ref, occ_ref, eta_ref, gamma_ref, *rest):
    packed_refs = rest[: tiles - 1]
    out_refs = rest[tiles - 1 : 2 * tiles - 1]
    eta, gamma, weight, sems = rest[2 * tiles - 1 :]
    place = place_ref[0]
    copies = []
    for source, full in ((eta_ref, eta), (gamma_ref, gamma)):
        for k in range(tiles):
            copies.append(
                pltpu.make_async_copy(
                    source.at[place, :, aligned((place ^ k) * rows, rows)],
                    full.at[0:rows, k * rows : (k + 1) * rows],
                    sems.at[len(copies)],
                )
            )
    for copy in copies:
        copy.start()
    weight[...] = free_weight(occ_ref, place, sizes_ref[place])
    scale = jnp.concatenate(
        [weight[:, aligned((place ^ k) * rows, rows)] for k in range(tiles)], axis=1
    ).astype(BF16)
    for k in range(1, tiles):
        for n, full in enumerate((eta, gamma)):
            for m, other in enumerate(range(k, tiles)):
                block = packed_refs[k - 1][n, m]
                here, there = slice(k * rows, (k + 1) * rows), slice(other * rows, (other + 1) * rows)
                full[here, there] = block
                if other > k:
                    full[there, here] = block.T if n else -block.T
    for copy in copies:
        copy.wait()
    for other in range(1, tiles):
        here, there = slice(0, rows), slice(other * rows, (other + 1) * rows)
        eta[there, here] = -eta[here, there].T
        gamma[there, here] = gamma[here, there].T
    for k in reversed(range(tiles - 1)):
        here, later = slice(k * rows, (k + 1) * rows), slice((k + 1) * rows, tiles * rows)
        total = jnp.dot(eta[here, :] * scale, gamma[:, later], preferred_element_type=F32)
        total -= jnp.dot(gamma[here, :] * scale, eta[:, later], preferred_element_type=F32)
        total = total.astype(BF16)
        for other in range(k + 1, tiles):
            block = total[:, (other - k - 1) * rows : (other - k) * rows]
            column = slice(((k ^ other) - 1) * rows, (k ^ other) * rows)
            out_refs[k][:, column] = block
            out_refs[other][:, column] = block.T


def ladder_blocks(place, sizes, pair_occupation, eta, gamma, packed):
    tiles, rows, states = eta.shape
    return pl.pallas_call(
        functools.partial(ladder_kernel, tiles, rows),
        out_shape=[jax.ShapeDtypeStruct((rows, states - rows), BF16)] * tiles,
        in_specs=[SMEM, SMEM, VMEM, HBM, HBM] + [VMEM] * (tiles - 1),
        out_specs=[VMEM] * tiles,
        scratch_shapes=[
            pltpu.VMEM((states, states), BF16),
            pltpu.VMEM((states, states), BF16),
            pltpu.VMEM((1, states), F32),
            pltpu.SemaphoreType.DMA((2 * tiles,)),
        ],
        compiler_params=params(12),
        cost_estimate=cost(2 * states**3, 8 * states**2),
        name="ladder",
    )(place, sizes, pair_occupation, eta, gamma, *packed)


def finish_kernel(blocks, me_ref, place_ref, sizes_ref, diagonal_ref, *rest):
    back_refs, ladder_refs = rest[:blocks], rest[blocks:-4]
    out_ref, back, held, sems = rest[-4:]
    chan_count, tile_rows, states = out_ref.shape
    place = place_ref[0]
    rows = back_refs[0].shape[0]
    for d, back_ref in enumerate(back_refs):
        back[aligned((me_ref[0] ^ d) * rows, rows), :] = back_ref[...]
    row = lax.broadcasted_iota(jnp.int32, (tile_rows, tile_rows), 0) + place * tile_rows
    column = lax.broadcasted_iota(jnp.int32, (tile_rows, tile_rows), 1)
    copies = []
    for k, ladder_ref in enumerate(ladder_refs):
        c = place ^ k
        for m in range(len(ladder_refs)):
            ladder = ladder_ref[:, (m - 1) * tile_rows : m * tile_rows] if m else diagonal_ref[c]
            start = (place ^ m) * tile_rows
            span = aligned(start, tile_rows)
            total = ladder.astype(F32) + back[aligned(c * tile_rows, tile_rows), span].astype(F32)
            live = jnp.maximum(row, column + start) < sizes_ref[c]
            held[c, :, span] = jnp.where(live, total, 0.0).astype(BF16)
        copies.append(pltpu.make_async_copy(held.at[c], out_ref.at[c], sems.at[k]))
        copies[-1].start()
    for copy in copies:
        copy.wait()


def finish(me, place, sizes, shape, diagonal, back, ladder):
    chan_count, tile_rows, states = shape
    return pl.pallas_call(
        functools.partial(finish_kernel, len(back)),
        out_shape=jax.ShapeDtypeStruct(shape, BF16),
        in_specs=[SMEM] * 3 + [VMEM] * (1 + len(back) + len(ladder)),
        out_specs=HBM,
        scratch_shapes=[
            pltpu.VMEM((chan_count * tile_rows, states), BF16),
            pltpu.VMEM(shape, BF16),
            pltpu.SemaphoreType.DMA((len(ladder),)),
        ],
        compiler_params=params(12),
        cost_estimate=cost(0, 6 * chan_count * tile_rows * states),
        name="finish",
    )(me, place, sizes, diagonal, *back, *ladder)


def ladder_gathered(sizes, pair_occupation, eta, gamma):
    _, rows, states = eta.shape
    columns = lax.broadcasted_iota(jnp.int32, (eta.shape[0], states), 1)
    weight = (1 - pair_occupation[0] - pair_occupation[1]) * (columns < sizes[:, None])
    first = jnp.einsum(
        "crk,ckj->crj",
        eta * weight.astype(BF16)[:, None, :],
        lax.all_gather(gamma, "tile", axis=1, tiled=True),
        preferred_element_type=F32,
    )
    mirrored = lax.all_to_all(first, "tile", split_axis=2, concat_axis=1, tiled=True)
    return first + jnp.swapaxes(mirrored, 1, 2)


def per_device(
    chans,
    tiles,
    generator,
    hamiltonian,
    chan_sizes,
    pair_occupation,
    recoupled_occupation,
    recouple_map,
    recouple_weights,
):
    chan_count, tile_rows, states = generator.shape
    flat = (chan_count * tile_rows, states)
    me = jnp.reshape(lax.axis_index("chan"), (1,))
    place = jnp.reshape(lax.axis_index("tile"), (1,))
    paired = chans & (chans - 1) == 0 and tiles & (tiles - 1) == 0
    if not (paired and tiles == chan_count and chans in (tiles, 2 * tiles)):
        return per_device_whole(
            place,
            generator,
            hamiltonian,
            chan_sizes,
            pair_occupation,
            recoupled_occupation,
            recouple_map,
            recouple_weights,
        )

    def to_chan(message, d):
        return xor_permute(message, "chan", chans, d)

    def to_tile(message, k):
        return xor_permute(message, "tile", tiles, k)

    first, second = order = block_order(chans)
    near = [1] + [d for d in first if d]
    late = [d for d in range(chans) if d not in near]
    pair = (generator, hamiltonian)
    steps = list(range(1, tiles))
    packed, lacking = pack(me, place, chan_sizes, *pair, chans, tiles, near, steps[1:2], 50)
    for kept, rest in zip(
        (packed, lacking),
        pack(me, place, chan_sizes, *pair, chans, tiles, late, steps[:1] + steps[2:], 12),
    ):
        kept.update(rest)
    turned, select, diagonal = prepare(
        me,
        first + second,
        recouple_map,
        recoupled_occupation,
        recouple_weights,
        chan_sizes,
        pair_occupation,
        generator,
        hamiltonian,
    )

    received = {0: packed[0], 1: to_chan(packed[1], 1)}
    for d in first[1:]:
        received[d] = to_chan(packed[d], d)
        received[d + 1] = to_chan(after(packed[d + 1], received[d], select), d + 1)
    lacking[1] = after(lacking[1], received[1])
    for k in steps:
        lacking[k] = to_tile(after(lacking[k], lacking[k - 1], select) if k > 2 else lacking[k], k)

    bar, left = first_half(me, first, turned, select, [received[d] for d in first])
    ladder = ladder_blocks(place, chan_sizes, pair_occupation, generator, hamiltonian, [lacking[k] for k in steps])
    left = after(left, ladder[0])
    ladder = list(ladder)
    ladder[1] = to_tile(ladder[1], 1)
    for k in range(2, tiles):
        ladder[k] = to_tile(after(ladder[k], ladder[1]) if k == 2 else ladder[k], k)

    back = {}
    sent, second_bar = cross_first(
        me, order, turned, bar, left, [received[d] for d in second], flat
    )
    back[0] = sent[0]
    for d, block in zip(first, sent):
        if d:
            back[d] = to_chan(block, d)
    sent = cross_second(me, second, turned, select, bar, second_bar, flat, chans)
    for d, block in zip(second, sent):
        waits = [ladder[-1]] if d == 1 else [back[d - 1]]
        if d == chans - 1:
            waits.append(back[1])
        back[d] = to_chan(after(block, *waits), d)
    back = [back[d] for d in range(chans)]
    return finish(me, place, chan_sizes, generator.shape, diagonal, back, ladder)


def per_device_whole(
    place,
    generator,
    hamiltonian,
    chan_sizes,
    pair_occupation,
    recoupled_occupation,
    recouple_map,
    recouple_weights,
):
    chan_count, tile_rows, states = generator.shape
    flat = (chan_count * tile_rows, states)
    alone = jnp.zeros_like(place)
    row = place * tile_rows + jnp.arange(tile_rows, dtype=jnp.int32)
    highest = jnp.maximum(row[:, None], jnp.arange(states, dtype=jnp.int32)[None, :])
    live = highest[None] < chan_sizes[:, None, None]
    pair = jnp.where(live, jnp.stack([generator, hamiltonian]), jnp.zeros((), BF16))
    received = lax.all_to_all(pair.reshape(2, *flat), "chan", 1, 1, tiled=True)
    order = ([0], [])
    turned, select = prepare(
        alone, order[0], recouple_map, recoupled_occupation, recouple_weights
    )
    bar, left = first_half(alone, order[0], turned, select, [received])
    sent, _ = cross_first(alone, order, turned, bar, left, [], flat)
    back = lax.all_to_all(sent[0], "chan", 0, 0, tiled=True).reshape(generator.shape)
    ladder = ladder_gathered(chan_sizes, pair_occupation, generator, hamiltonian)
    return jnp.where(live, ladder + back.astype(F32), 0.0).astype(BF16)


def solution(mesh):
    return jax.shard_map(
        functools.partial(per_device, mesh.shape["chan"], mesh.shape["tile"]),
        mesh=mesh,
        in_specs=(
            P("chan", "tile", None),
            P("chan", "tile", None),
            P("chan"),
            P(None, "chan", None),
            P(None, ("chan", "tile"), None),
            P(("chan", "tile"), None),
            P(("chan", "tile"), None, None),
        ),
        out_specs=P("chan", "tile", None),
        check_vma=False,
    )
```

```python
import functools

import jax
import jax.numpy as jnp
from jax import lax
from jax.experimental import pallas as pl
from jax.experimental.pallas import tpu as pltpu
from jax.sharding import PartitionSpec as P

BF16 = jnp.bfloat16
F32 = jnp.float32
HBM = pl.BlockSpec(memory_space=pltpu.HBM)
VMEM = pl.BlockSpec(memory_space=pltpu.VMEM)
NT = (((1,), (1,)), ((), ()))
SMEM = pl.BlockSpec(memory_space=pltpu.SMEM)


def params(mib):
    return pltpu.CompilerParams(vmem_limit_bytes=mib << 20)


def cost(flops, moved):
    return pl.CostEstimate(flops=int(flops), bytes_accessed=int(moved), transcendentals=0)


def xor_permute(block, axis, size, step):
    return lax.ppermute(block, axis, [(i, i ^ step) for i in range(size)])


def aligned(start, size):
    return pl.ds(pl.multiple_of(start, size), size)


def row_tiles(states):
    return [(start, min(256, states - start)) for start in range(0, states, 256)]


def block_order(blocks):
    first = [0, 1, *range(2, blocks, 2)]
    return first, [d for d in range(blocks) if d not in first]


def free_weight(occ_ref, chan, size):
    occupied = occ_ref[0] + occ_ref[1]
    own = lax.broadcasted_iota(jnp.int32, occupied.shape, 0) == chan
    free = jnp.sum(jnp.where(own, 1 - occupied, 0), axis=0, keepdims=True)
    live = lax.broadcasted_iota(jnp.int32, free.shape, 1) < size
    return jnp.where(live, free, 0).astype(F32)


def diagonal_blocks(sizes_ref, occ_ref, eta_ref, gamma_ref, out_ref):
    for c in range(eta_ref.shape[0]):
        weight = free_weight(occ_ref, c, sizes_ref[c]).astype(BF16)
        out_ref[c] = lax.dot_general(
            eta_ref[c] * weight, gamma_ref[c], NT, preferred_element_type=F32
        ) + lax.dot_general(gamma_ref[c] * weight, eta_ref[c], NT, preferred_element_type=F32)


def prepare_kernel(
    ph_count, states, order, me_ref, map_ref, occ_ref, weights_ref, turned_ref, select_ref
):
    rows = states // len(order)
    for q in range(ph_count):
        map_row = map_ref[q : q + 1, :]
        spans = [aligned((me_ref[0] ^ d) * rows, rows) for d in order]
        kept_map = jnp.concatenate([map_ref[q : q + 1, s] for s in spans], axis=1)
        signs = jnp.concatenate(
            [occ_ref[0, q : q + 1, s] - occ_ref[1, q : q + 1, s] for s in spans], axis=1
        ).astype(F32)
        for start, height in row_tiles(states):
            index = lax.broadcasted_iota(jnp.int32, (height, states), 0) + start
            select_ref[q, start : start + height, :] = jnp.where(
                index == kept_map, signs, 0.0
            ).astype(BF16)
            hot = jnp.where(index == map_row, 1.0, 0.0).astype(BF16)
            for top, tall in row_tiles(states):
                rest = weights_ref[q, top : top + tall, :]
                total = jnp.zeros((tall, height), F32)
                for _ in range(3):
                    part = rest.astype(BF16)
                    rest = rest - part.astype(F32)
                    total = total + lax.dot_general(
                        part, hot, NT, preferred_element_type=F32
                    )
                turned_ref[q, top : top + tall, start : start + height] = total


def prepare_whole_kernel(ph_count, states, order, *refs):
    prepare_kernel(ph_count, states, order, *refs[:4], *refs[-3:-1])
    diagonal_blocks(*refs[4:-3], refs[-1])


def prepare(me, order, recouple_map, recoupled_occupation, recouple_weights, *pair):
    ph_count, states = recouple_map.shape
    kernel, extra = prepare_kernel, ()
    flops = 6 * ph_count * states**3
    if pair:
        chan_count, rows, columns = pair[-1].shape
        kernel = prepare_whole_kernel
        extra = (jax.ShapeDtypeStruct((chan_count, rows, rows), F32),)
        flops += 4 * chan_count * rows * rows * columns
    return pl.pallas_call(
        functools.partial(kernel, ph_count, states, order),
        out_shape=(
            jax.ShapeDtypeStruct(recouple_weights.shape, F32),
            jax.ShapeDtypeStruct(recouple_weights.shape, BF16),
            *extra,
        ),
        in_specs=[SMEM] + [VMEM] * 3 + [SMEM] * bool(pair) + [VMEM] * len(pair[1:]),
        out_specs=(VMEM,) * (2 + len(extra)),
        compiler_params=params(12),
        cost_estimate=cost(flops, 14 * ph_count * states**2),
        name="prepare",
    )(me, recouple_map, recoupled_occupation, recouple_weights, *pair)


def weigh_blocks(states, order, me, turned_ref, recv_refs, bar_ref):
    for recv_ref, (slot, d) in zip(recv_refs, enumerate(order)):
        rows = recv_ref.shape[1]
        span = aligned((me ^ d) * rows, rows)
        for q in range(turned_ref.shape[0]):
            weights = turned_ref[q, span, :]
            for n in range(2):
                values = recv_ref[n, :, q * states : (q + 1) * states].astype(F32) * weights
                bar_ref[n, q, slot * rows : (slot + 1) * rows, :] = values.astype(BF16)


def turn_blocks(select_ref, bar_ref, left_ref):
    for q in range(select_ref.shape[0]):
        for n in range(2):
            for top, height in row_tiles(bar_ref.shape[2]):
                span = slice(top, top + height)
                left_ref[n, q, span, :] = jnp.dot(
                    bar_ref[n, q, span, :], select_ref[q], preferred_element_type=F32
                ).astype(BF16)


def cross_rows(q, span, inner, left_ref, bar_ref):
    return jnp.dot(
        left_ref[0, q, span, inner], bar_ref[1, q], preferred_element_type=F32
    ) - jnp.dot(left_ref[1, q, span, inner], bar_ref[0, q], preferred_element_type=F32)


def store_blocks(states, order, me, q, top, crossed, turned_ref, out_refs):
    rows = out_refs[0].shape[0]
    step = min(rows, crossed.shape[0])
    for base in range(0, crossed.shape[0], step):
        slot, inside = divmod(top + base, rows)
        weights = turned_ref[q, aligned((me ^ order[slot]) * rows + inside, step), :]
        out_refs[slot][inside : inside + step, q * states : (q + 1) * states] = (
            crossed[base : base + step] * weights
        ).astype(BF16)


def first_kernel(states, order, me_ref, turned_ref, select_ref, *rest):
    recv_refs, (bar_ref, left_ref, part_ref) = rest[:-3], rest[-3:]
    weigh_blocks(states, order, me_ref[0], turned_ref, recv_refs, bar_ref)
    turn_blocks(select_ref, bar_ref, left_ref)
    for q in range(turned_ref.shape[0]):
        for top, height in row_tiles(bar_ref.shape[2]):
            span = slice(top, top + height)
            part_ref[q, span, :] = cross_rows(
                q, span, slice(0, bar_ref.shape[2]), left_ref, bar_ref
            )


def first_part(me, order, turned, select, received):
    ph_count, states, _ = turned.shape
    rows = received[0].shape[1] * len(order)
    shape = jax.ShapeDtypeStruct((2, ph_count, rows, states), BF16)
    return pl.pallas_call(
        functools.partial(first_kernel, states, order),
        out_shape=(shape, shape, jax.ShapeDtypeStruct((ph_count, rows, states), F32)),
        in_specs=[SMEM] + [VMEM] * (2 + len(order)),
        out_specs=(VMEM,) * 3,
        compiler_params=params(8),
        cost_estimate=cost(8 * ph_count * rows * states**2, 14 * ph_count * states**2),
        name="first_part",
    )(me, turned, select, *received)


def cross_first_kernel(states, order, me_ref, turned_ref, left_ref, part_ref, *rest):
    first, second = order
    recv_refs, out_refs = rest[: len(second)], rest[len(second) : len(second) + len(first)]
    if second:
        weigh_blocks(states, second, me_ref[0], turned_ref, recv_refs, rest[-1])
    for q in range(turned_ref.shape[0]):
        for top, height in row_tiles(left_ref.shape[2]):
            span = slice(top, top + height)
            crossed = part_ref[q, span, :]
            if second:
                inner = slice(left_ref.shape[2], states)
                crossed += cross_rows(q, span, inner, left_ref, rest[-1])
            store_blocks(states, first, me_ref[0], q, top, crossed, turned_ref, out_refs)


def cross_first(me, order, turned, left, part, received, flat):
    ph_count, states, _ = turned.shape
    first, second = order
    blocks = len(first) + len(second)
    out_shape = [jax.ShapeDtypeStruct((flat[0] // blocks, flat[1]), BF16)] * len(first)
    if second:
        out_shape.append(
            jax.ShapeDtypeStruct((2, ph_count, states - left.shape[2], states), BF16)
        )
    out = pl.pallas_call(
        functools.partial(cross_first_kernel, states, order),
        out_shape=out_shape,
        in_specs=[SMEM] + [VMEM] * (3 + len(second)),
        out_specs=[VMEM] * len(out_shape),
        compiler_params=params(8),
        cost_estimate=cost(2 * ph_count * states**3, 14 * ph_count * states**2),
        name="cross_first",
    )(me, turned, left, part, *received)
    return out[: len(first)], out[-1]


def cross_second_kernel(
    states, order, me_ref, turned_ref, select_ref, bar_ref, second_bar_ref, *rest
):
    out_refs, left_ref = rest[:-1], rest[-1]
    turn_blocks(select_ref, second_bar_ref, left_ref)
    middle = bar_ref.shape[2]
    for q in range(turned_ref.shape[0]):
        for top, height in row_tiles(left_ref.shape[2]):
            span = slice(top, top + height)
            crossed = cross_rows(q, span, slice(0, middle), left_ref, bar_ref)
            crossed += cross_rows(q, span, slice(middle, states), left_ref, second_bar_ref)
            store_blocks(states, order, me_ref[0], q, top, crossed, turned_ref, out_refs)


def cross_second(me, order, turned, select, bar, second_bar, flat, blocks):
    ph_count, states, _ = turned.shape
    return pl.pallas_call(
        functools.partial(cross_second_kernel, states, order),
        out_shape=[jax.ShapeDtypeStruct((flat[0] // blocks, flat[1]), BF16)] * len(order),
        in_specs=[SMEM] + [VMEM] * 4,
        out_specs=[VMEM] * len(order),
        scratch_shapes=[pltpu.VMEM(second_bar.shape, BF16)],
        compiler_params=params(12),
        cost_estimate=cost(4 * ph_count * states**3, 14 * ph_count * states**2),
        name="cross_second",
    )(me, turned, select, bar, second_bar)


def pack_kernel(shape, blocks, tiles, partners, steps, me_ref, place_ref, sizes_ref, *rest):
    chan_count, tile_rows, states = shape
    source_refs, block_refs = rest[:2], rest[2 : 2 + len(partners)]
    owner_refs, (held, sems) = rest[2 + len(partners) : -2], rest[-2:]
    rows = chan_count * tile_rows // blocks
    place = place_ref[0]
    copies, places = [], []

    def fetch(source, target):
        copies.append(pltpu.make_async_copy(source, target, sems.at[len(copies)]))
        copies[-1].start()

    for slot, d in enumerate(partners):
        start = (me_ref[0] ^ d) * rows
        chan = start // tile_rows
        places.append((chan, start - chan * tile_rows))
        for n, source_ref in enumerate(source_refs):
            fetch(source_ref.at[chan, aligned(places[-1][1], rows), :], held.at[slot, n])
    for step, owner_ref in zip(steps, owner_refs):
        owner = place ^ step
        for n, source_ref in enumerate(source_refs):
            for m, other in enumerate(range(step, tiles)):
                column = aligned((owner ^ other) * tile_rows, tile_rows)
                fetch(source_ref.at[owner, :, column], owner_ref.at[n, m])
    row = lax.broadcasted_iota(jnp.int32, (rows, states), 0) + place * tile_rows
    highest = jnp.maximum(row, lax.broadcasted_iota(jnp.int32, (rows, states), 1))
    for slot, (chan, inside) in enumerate(places):
        live = jnp.maximum(highest, row + inside) < sizes_ref[chan]
        for n in range(2):
            copies[2 * slot + n].wait()
            values = held[slot, n]
            block_refs[slot][n] = jnp.where(live, values, jnp.zeros_like(values))
    for copy in copies[2 * len(partners) :]:
        copy.wait()


def pack(me, place, sizes, eta, gamma, blocks, tiles, partners, steps, mib):
    chan_count, rows, states = eta.shape
    shapes = [(2, chan_count * rows // blocks, states)] * len(partners)
    shapes += [(2, tiles - step, rows, rows) for step in steps]
    out = pl.pallas_call(
        functools.partial(pack_kernel, eta.shape, blocks, tiles, partners, steps),
        out_shape=[jax.ShapeDtypeStruct(shape, BF16) for shape in shapes],
        in_specs=[SMEM] * 3 + [HBM] * 2,
        out_specs=[VMEM] * len(shapes),
        scratch_shapes=[
            pltpu.VMEM((len(partners), *shapes[0]), BF16),
            pltpu.SemaphoreType.DMA((2 * len(partners) + 2 * sum(tiles - s for s in steps),)),
        ],
        compiler_params=params(mib),
        cost_estimate=cost(0, 8 * len(partners) * shapes[0][1] * states),
        name="pack",
    )(me, place, sizes, eta, gamma)
    return dict(zip(partners, out)), dict(zip(steps, out[len(partners) :]))


def ladder_kernel(tiles, rows, place_ref, sizes_ref, occ_ref, eta_ref, gamma_ref, *rest):
    packed_refs = rest[: tiles - 1]
    out_refs = rest[tiles - 1 : 2 * tiles - 1]
    eta, gamma, weight, sems = rest[2 * tiles - 1 :]
    place = place_ref[0]
    copies = []
    for source, full in ((eta_ref, eta), (gamma_ref, gamma)):
        for k in range(tiles):
            copies.append(
                pltpu.make_async_copy(
                    source.at[place, :, aligned((place ^ k) * rows, rows)],
                    full.at[0:rows, k * rows : (k + 1) * rows],
                    sems.at[len(copies)],
                )
            )
    for copy in copies:
        copy.start()
    weight[...] = free_weight(occ_ref, place, sizes_ref[place])
    scale = jnp.concatenate(
        [weight[:, aligned((place ^ k) * rows, rows)] for k in range(tiles)], axis=1
    ).astype(BF16)
    for k in range(1, tiles):
        for n, full in enumerate((eta, gamma)):
            for m, other in enumerate(range(k, tiles)):
                block = packed_refs[k - 1][n, m]
                here, there = slice(k * rows, (k + 1) * rows), slice(other * rows, (other + 1) * rows)
                full[here, there] = block
                if other > k:
                    full[there, here] = block.T if n else -block.T
    for copy in copies:
        copy.wait()
    for other in range(1, tiles):
        here, there = slice(0, rows), slice(other * rows, (other + 1) * rows)
        eta[there, here] = -eta[here, there].T
        gamma[there, here] = gamma[here, there].T
    for k in reversed(range(tiles - 1)):
        here, later = slice(k * rows, (k + 1) * rows), slice((k + 1) * rows, tiles * rows)
        total = jnp.dot(eta[here, :] * scale, gamma[:, later], preferred_element_type=F32)
        total -= jnp.dot(gamma[here, :] * scale, eta[:, later], preferred_element_type=F32)
        total = total.astype(BF16)
        for other in range(k + 1, tiles):
            block = total[:, (other - k - 1) * rows : (other - k) * rows]
            column = slice(((k ^ other) - 1) * rows, (k ^ other) * rows)
            out_refs[k][:, column] = block
            out_refs[other][:, column] = block.T


def ladder_blocks(place, sizes, pair_occupation, eta, gamma, packed):
    tiles, rows, states = eta.shape
    return pl.pallas_call(
        functools.partial(ladder_kernel, tiles, rows),
        out_shape=[jax.ShapeDtypeStruct((rows, states - rows), BF16)] * tiles,
        in_specs=[SMEM, SMEM, VMEM, HBM, HBM] + [VMEM] * (tiles - 1),
        out_specs=[VMEM] * tiles,
        scratch_shapes=[
            pltpu.VMEM((states, states), BF16),
            pltpu.VMEM((states, states), BF16),
            pltpu.VMEM((1, states), F32),
            pltpu.SemaphoreType.DMA((2 * tiles,)),
        ],
        compiler_params=params(12),
        cost_estimate=cost(2 * states**3, 8 * states**2),
        name="ladder",
    )(place, sizes, pair_occupation, eta, gamma, *packed)


def finish_kernel(blocks, me_ref, place_ref, sizes_ref, diagonal_ref, *rest):
    back_refs, ladder_refs = rest[:blocks], rest[blocks:-4]
    out_ref, back, held, sems = rest[-4:]
    chan_count, tile_rows, states = out_ref.shape
    place = place_ref[0]
    rows = back_refs[0].shape[0]
    for d, back_ref in enumerate(back_refs):
        back[aligned((me_ref[0] ^ d) * rows, rows), :] = back_ref[...]
    row = lax.broadcasted_iota(jnp.int32, (tile_rows, tile_rows), 0) + place * tile_rows
    column = lax.broadcasted_iota(jnp.int32, (tile_rows, tile_rows), 1)
    copies = []
    for k, ladder_ref in enumerate(ladder_refs):
        c = place ^ k
        for m in range(len(ladder_refs)):
            ladder = ladder_ref[:, (m - 1) * tile_rows : m * tile_rows] if m else diagonal_ref[c]
            start = (place ^ m) * tile_rows
            span = aligned(start, tile_rows)
            total = ladder.astype(F32) + back[aligned(c * tile_rows, tile_rows), span].astype(F32)
            live = jnp.maximum(row, column + start) < sizes_ref[c]
            held[c, :, span] = jnp.where(live, total, 0.0).astype(BF16)
        copies.append(pltpu.make_async_copy(held.at[c], out_ref.at[c], sems.at[k]))
        copies[-1].start()
    for copy in copies:
        copy.wait()


def finish(me, place, sizes, shape, diagonal, back, ladder):
    chan_count, tile_rows, states = shape
    return pl.pallas_call(
        functools.partial(finish_kernel, len(back)),
        out_shape=jax.ShapeDtypeStruct(shape, BF16),
        in_specs=[SMEM] * 3 + [VMEM] * (1 + len(back) + len(ladder)),
        out_specs=HBM,
        scratch_shapes=[
            pltpu.VMEM((chan_count * tile_rows, states), BF16),
            pltpu.VMEM(shape, BF16),
            pltpu.SemaphoreType.DMA((len(ladder),)),
        ],
        compiler_params=params(12),
        cost_estimate=cost(0, 6 * chan_count * tile_rows * states),
        name="finish",
    )(me, place, sizes, diagonal, *back, *ladder)


def ladder_gathered(sizes, pair_occupation, eta, gamma):
    _, rows, states = eta.shape
    columns = lax.broadcasted_iota(jnp.int32, (eta.shape[0], states), 1)
    weight = (1 - pair_occupation[0] - pair_occupation[1]) * (columns < sizes[:, None])
    first = jnp.einsum(
        "crk,ckj->crj",
        eta * weight.astype(BF16)[:, None, :],
        lax.all_gather(gamma, "tile", axis=1, tiled=True),
        preferred_element_type=F32,
    )
    mirrored = lax.all_to_all(first, "tile", split_axis=2, concat_axis=1, tiled=True)
    return first + jnp.swapaxes(mirrored, 1, 2)


WAITS = {
    "lack1": ("in1",),
    "lack3": ("in2", "prepare"),
    "in3": ("in2", "prepare"),
    "in5": ("in4", "prepare"),
    "in7": ("in6", "prepare"),
    "cross_first": ("ladder",),
    "own2": ("own1",),
    "back1": ("own3",),
    "back3": ("back2",),
    "back5": ("back4",),
    "back7": ("back6", "back1"),
}


ORDER = (
    "pack_near",
    "pack_late",
    "prepare",
    "in1",
    "in2",
    "in4",
    "in6",
    "lack1",
    "lack2",
    "lack3",
    "in3",
    "in5",
    "in7",
    "first",
    "ladder",
    "own1",
    "own2",
    "own3",
    "cross_first",
    "back1",
    "back2",
    "back4",
    "back6",
    "cross_second",
    "back3",
    "back5",
    "back7",
)


def per_device(
    chans,
    tiles,
    generator,
    hamiltonian,
    chan_sizes,
    pair_occupation,
    recoupled_occupation,
    recouple_map,
    recouple_weights,
):
    chan_count, tile_rows, states = generator.shape
    flat = (chan_count * tile_rows, states)
    me = jnp.reshape(lax.axis_index("chan"), (1,))
    place = jnp.reshape(lax.axis_index("tile"), (1,))
    paired = chans & (chans - 1) == 0 and tiles & (tiles - 1) == 0
    if not (paired and tiles == chan_count and chans in (tiles, 2 * tiles)):
        return per_device_whole(
            place,
            generator,
            hamiltonian,
            chan_sizes,
            pair_occupation,
            recoupled_occupation,
            recouple_map,
            recouple_weights,
        )

    def to_chan(message, d):
        return xor_permute(message, "chan", chans, d)

    def to_tile(message, k):
        return xor_permute(message, "tile", tiles, k)

    first, second = order = block_order(chans)
    near = first[1:]
    late = [d for d in range(chans) if d not in near]
    pair = (generator, hamiltonian)
    steps = list(range(1, tiles))
    done = {}

    def value(name):
        if name not in done:
            done[name] = make[name]()
        return done[name]

    def held(name, operand):
        waits = [value(wait) for wait in WAITS.get(name, ()) if wait in make]
        waits = [w[1] if isinstance(w, tuple) else w[0] if isinstance(w, list) else w for w in waits]
        return lax.optimization_barrier((operand, waits))[0] if waits else operand

    def pack_part(partners, chosen, mib):
        return pack(me, place, chan_sizes, *pair, chans, tiles, partners, chosen, mib)

    def to_chan(name, block, d):
        return xor_permute(held(name, block), "chan", chans, d) if d else block

    def to_tile(name, block, k):
        return xor_permute(held(name, block), "tile", tiles, k) if k else block

    def make_first():
        turned, select, _ = value("prepare")
        received = held("first", [value(f"in{d}") for d in first])
        return first_part(me, first, turned, select, received)

    def make_ladder():
        lacking = held("ladder", [value(f"lack{k}") for k in steps])
        return ladder_blocks(place, chan_sizes, pair_occupation, *pair, lacking)

    def make_cross_first():
        _, left, part = value("first")
        part = held("cross_first", part)
        received = [value(f"in{d}") for d in second]
        return cross_first(me, order, value("prepare")[0], left, part, received, flat)

    def make_cross_second():
        turned, select, _ = value("prepare")
        bar, second_bar = held("cross_second", (value("first")[0], value("cross_first")[1]))
        return cross_second(me, second, turned, select, bar, second_bar, flat, chans)

    make = {
        "pack_near": lambda: pack_part(near, steps[1:2], 50),
        "pack_late": lambda: pack_part(late, steps[:1] + steps[2:], 12),
        "prepare": lambda: prepare(
            me,
            first + second,
            recouple_map,
            recoupled_occupation,
            recouple_weights,
            chan_sizes,
            pair_occupation,
            *pair,
        ),
        "first": make_first,
        "ladder": make_ladder,
        "cross_first": make_cross_first,
        "cross_second": make_cross_second,
    }
    for d in range(chans):
        source = "pack_near" if d in near else "pack_late"
        make[f"in{d}"] = lambda d=d, s=source: to_chan(f"in{d}", value(s)[0][d], d)
        group, place_in, blocks = (
            ("cross_first", first.index(d), 0) if d in first else ("cross_second", second.index(d), 1)
        )
        make[f"back{d}"] = lambda d=d, g=group, i=place_in, b=blocks: to_chan(
            f"back{d}", (value(g) if b else value(g)[0])[i], d
        )
    for k in range(tiles):
        source = "pack_near" if k in steps[1:2] else "pack_late"
        make[f"lack{k}"] = lambda k=k, s=source: to_tile(f"lack{k}", value(s)[1][k], k)
        make[f"own{k}"] = lambda k=k: to_tile(f"own{k}", value("ladder")[k], k)

    for name in ORDER:
        if name in make:
            value(name)
    back = [value(f"back{d}") for d in range(chans)]
    ladder = [value(f"own{k}") for k in range(tiles)]
    return finish(me, place, chan_sizes, generator.shape, value("prepare")[2], back, ladder)


def per_device_whole(
    place,
    generator,
    hamiltonian,
    chan_sizes,
    pair_occupation,
    recoupled_occupation,
    recouple_map,
    recouple_weights,
):
    chan_count, tile_rows, states = generator.shape
    flat = (chan_count * tile_rows, states)
    alone = jnp.zeros_like(place)
    row = place * tile_rows + jnp.arange(tile_rows, dtype=jnp.int32)
    highest = jnp.maximum(row[:, None], jnp.arange(states, dtype=jnp.int32)[None, :])
    live = highest[None] < chan_sizes[:, None, None]
    pair = jnp.where(live, jnp.stack([generator, hamiltonian]), jnp.zeros((), BF16))
    received = lax.all_to_all(pair.reshape(2, *flat), "chan", 1, 1, tiled=True)
    order = ([0], [])
    turned, select = prepare(
        alone, order[0], recouple_map, recoupled_occupation, recouple_weights
    )
    _, left, part = first_part(alone, order[0], turned, select, [received])
    sent, _ = cross_first(alone, order, turned, left, part, [], flat)
    back = lax.all_to_all(sent[0], "chan", 0, 0, tiled=True).reshape(generator.shape)
    ladder = ladder_gathered(chan_sizes, pair_occupation, generator, hamiltonian)
    return jnp.where(live, ladder + back.astype(F32), 0.0).astype(BF16)


def solution(mesh):
    return jax.shard_map(
        functools.partial(per_device, mesh.shape["chan"], mesh.shape["tile"]),
        mesh=mesh,
        in_specs=(
            P("chan", "tile", None),
            P("chan", "tile", None),
            P("chan"),
            P(None, "chan", None),
            P(None, ("chan", "tile"), None),
            P(("chan", "tile"), None),
            P(("chan", "tile"), None, None),
        ),
        out_specs=P("chan", "tile", None),
        check_vma=False,
    )
```

```python
import functools

import jax
import jax.numpy as jnp
from jax import lax
from jax.experimental import pallas as pl
from jax.experimental.pallas import tpu as pltpu
from jax.sharding import PartitionSpec as P

BF16 = jnp.bfloat16
F32 = jnp.float32
HBM = pl.BlockSpec(memory_space=pltpu.HBM)
VMEM = pl.BlockSpec(memory_space=pltpu.VMEM)
NT = (((1,), (1,)), ((), ()))
SMEM = pl.BlockSpec(memory_space=pltpu.SMEM)


def params(mib):
    return pltpu.CompilerParams(vmem_limit_bytes=mib << 20)


def cost(flops, moved):
    return pl.CostEstimate(flops=int(flops), bytes_accessed=int(moved), transcendentals=0)


def xor_permute(block, axis, size, step):
    return lax.ppermute(block, axis, [(i, i ^ step) for i in range(size)])


def aligned(start, size):
    return pl.ds(pl.multiple_of(start, size), size)


def row_tiles(states):
    return [(start, min(256, states - start)) for start in range(0, states, 256)]


def block_order(blocks):
    first = [0, 1, *range(2, blocks, 2)]
    return first, [d for d in range(blocks) if d not in first]


def free_weight(occ_ref, chan, size):
    occupied = occ_ref[0] + occ_ref[1]
    own = lax.broadcasted_iota(jnp.int32, occupied.shape, 0) == chan
    free = jnp.sum(jnp.where(own, 1 - occupied, 0), axis=0, keepdims=True)
    live = lax.broadcasted_iota(jnp.int32, free.shape, 1) < size
    return jnp.where(live, free, 0).astype(F32)


def diagonal_blocks(sizes_ref, occ_ref, eta_ref, gamma_ref, out_ref):
    for c in range(eta_ref.shape[0]):
        weight = free_weight(occ_ref, c, sizes_ref[c]).astype(BF16)
        out_ref[c] = lax.dot_general(
            eta_ref[c] * weight, gamma_ref[c], NT, preferred_element_type=F32
        ) + lax.dot_general(gamma_ref[c] * weight, eta_ref[c], NT, preferred_element_type=F32)


def prepare_kernel(
    ph_count, states, order, me_ref, map_ref, occ_ref, weights_ref, turned_ref, select_ref
):
    rows = states // len(order)
    for q in range(ph_count):
        map_row = map_ref[q : q + 1, :]
        spans = [aligned((me_ref[0] ^ d) * rows, rows) for d in order]
        kept_map = jnp.concatenate([map_ref[q : q + 1, s] for s in spans], axis=1)
        signs = jnp.concatenate(
            [occ_ref[0, q : q + 1, s] - occ_ref[1, q : q + 1, s] for s in spans], axis=1
        ).astype(F32)
        for start, height in row_tiles(states):
            index = lax.broadcasted_iota(jnp.int32, (height, states), 0) + start
            select_ref[q, start : start + height, :] = jnp.where(
                index == kept_map, signs, 0.0
            ).astype(BF16)
            hot = jnp.where(index == map_row, 1.0, 0.0).astype(BF16)
            for top, tall in row_tiles(states):
                rest = weights_ref[q, top : top + tall, :]
                total = jnp.zeros((tall, height), F32)
                for _ in range(3):
                    part = rest.astype(BF16)
                    rest = rest - part.astype(F32)
                    total = total + lax.dot_general(
                        part, hot, NT, preferred_element_type=F32
                    )
                turned_ref[q, top : top + tall, start : start + height] = total


def own_rows(place, sizes_ref, occ_ref, eta_ref, gamma_ref, full_refs, scale_ref):
    tiles, rows, _ = eta_ref.shape
    weight = free_weight(occ_ref, place, sizes_ref[place])
    scale_ref[1:2, :] = weight
    for k in range(tiles):
        column, later = aligned((place ^ k) * rows, rows), slice(k * rows, (k + 1) * rows)
        scale_ref[0:1, later] = scale_ref[1:2, column]
        for n, source_ref in enumerate((eta_ref, gamma_ref)):
            block = source_ref[place, :, column]
            full_refs[n][0:rows, later] = block
            if k:
                full_refs[n][later, 0:rows] = block.T if n else -block.T


def prepare_whole_kernel(ph_count, states, order, *refs):
    place_ref, refs = refs[0], refs[1:]
    prepare_kernel(ph_count, states, order, *refs[:4], *refs[8:10])
    diagonal_blocks(*refs[4:8], refs[10])
    own_rows(place_ref[0], *refs[4:8], refs[11:13], refs[13])


def prepare(me, order, recouple_map, recoupled_occupation, recouple_weights, place=None, *pair):
    ph_count, states = recouple_map.shape
    kernel, extra, lead = prepare_kernel, [], []
    flops = 6 * ph_count * states**3
    if pair:
        chan_count, rows, columns = pair[-1].shape
        kernel, lead = prepare_whole_kernel, [place]
        extra = [jax.ShapeDtypeStruct((chan_count, rows, rows), F32)]
        extra += [jax.ShapeDtypeStruct((columns, columns), BF16)] * 2
        extra += [jax.ShapeDtypeStruct((8, columns), F32)]
        flops += 4 * chan_count * rows * rows * columns
    return pl.pallas_call(
        functools.partial(kernel, ph_count, states, order),
        out_shape=(
            jax.ShapeDtypeStruct(recouple_weights.shape, F32),
            jax.ShapeDtypeStruct(recouple_weights.shape, BF16),
            *extra,
        ),
        in_specs=[SMEM] * (len(lead) + 1)
        + [VMEM] * 3
        + [SMEM] * bool(pair)
        + [VMEM] * len(pair[1:]),
        out_specs=(VMEM,) * (2 + len(extra)),
        compiler_params=params(12),
        cost_estimate=cost(flops, 14 * ph_count * states**2),
        name="prepare",
    )(*lead, me, recouple_map, recoupled_occupation, recouple_weights, *pair)


def weigh_blocks(states, order, me, turned_ref, recv_refs, bar_ref):
    for recv_ref, (slot, d) in zip(recv_refs, enumerate(order)):
        rows = recv_ref.shape[1]
        span = aligned((me ^ d) * rows, rows)
        for q in range(turned_ref.shape[0]):
            weights = turned_ref[q, span, :]
            for n in range(2):
                values = recv_ref[n, :, q * states : (q + 1) * states].astype(F32) * weights
                bar_ref[n, q, slot * rows : (slot + 1) * rows, :] = values.astype(BF16)


def turn_blocks(select_ref, bar_ref, left_ref):
    for q in range(select_ref.shape[0]):
        for n in range(2):
            for top, height in row_tiles(bar_ref.shape[2]):
                span = slice(top, top + height)
                left_ref[n, q, span, :] = jnp.dot(
                    bar_ref[n, q, span, :], select_ref[q], preferred_element_type=F32
                ).astype(BF16)


def cross_rows(q, span, inner, left_ref, bar_ref):
    return jnp.dot(
        left_ref[0, q, span, inner], bar_ref[1, q], preferred_element_type=F32
    ) - jnp.dot(left_ref[1, q, span, inner], bar_ref[0, q], preferred_element_type=F32)


def store_blocks(states, order, me, q, top, crossed, turned_ref, out_refs):
    rows = next(iter(out_refs.values())).shape[0]
    step = min(rows, crossed.shape[0])
    for base in range(0, crossed.shape[0], step):
        slot, inside = divmod(top + base, rows)
        weights = turned_ref[q, aligned((me ^ order[slot]) * rows + inside, step), :]
        out_refs[slot][inside : inside + step, q * states : (q + 1) * states] = (
            crossed[base : base + step] * weights
        ).astype(BF16)


def first_kernel(states, order, me_ref, turned_ref, select_ref, *rest):
    recv_refs, (bar_ref, left_ref, part_ref) = rest[:-3], rest[-3:]
    weigh_blocks(states, order, me_ref[0], turned_ref, recv_refs, bar_ref)
    turn_blocks(select_ref, bar_ref, left_ref)
    for q in range(turned_ref.shape[0]):
        for top, height in row_tiles(bar_ref.shape[2]):
            span = slice(top, top + height)
            part_ref[q, span, :] = cross_rows(
                q, span, slice(0, bar_ref.shape[2]), left_ref, bar_ref
            )


def first_part(me, order, turned, select, received):
    ph_count, states, _ = turned.shape
    rows = received[0].shape[1] * len(order)
    shape = jax.ShapeDtypeStruct((2, ph_count, rows, states), BF16)
    return pl.pallas_call(
        functools.partial(first_kernel, states, order),
        out_shape=(shape, shape, jax.ShapeDtypeStruct((ph_count, rows, states), F32)),
        in_specs=[SMEM] + [VMEM] * (2 + len(order)),
        out_specs=(VMEM,) * 3,
        compiler_params=params(8),
        cost_estimate=cost(8 * ph_count * rows * states**2, 14 * ph_count * states**2),
        name="first_part",
    )(me, turned, select, *received)


def cross_first_kernel(states, order, slots, fresh, me_ref, turned_ref, left_ref, part_ref, *rest):
    first, second = order
    recv_refs, rest = (rest[: len(second)], rest[len(second) :]) if fresh else ((), rest)
    bar_ref, outs = (rest[-1], rest[: len(slots)]) if fresh else (rest[0], rest[1:])
    if not second:
        outs = rest
    out_refs = dict(zip(slots, outs))
    if second and fresh:
        weigh_blocks(states, second, me_ref[0], turned_ref, recv_refs, bar_ref)
    rows = outs[0].shape[0]
    runs = []
    for slot in slots:
        if runs and runs[-1][1] == slot * rows and runs[-1][1] - runs[-1][0] < 256:
            runs[-1][1] += rows
        else:
            runs.append([slot * rows, (slot + 1) * rows])
    for q in range(turned_ref.shape[0]):
        for start, stop in runs:
            for top, height in row_tiles(stop - start):
                span = slice(start + top, start + top + height)
                crossed = part_ref[q, span, :]
                if second:
                    inner = slice(left_ref.shape[2], states)
                    crossed += cross_rows(q, span, inner, left_ref, bar_ref)
                store_blocks(
                    states, first, me_ref[0], q, start + top, crossed, turned_ref, out_refs
                )


def cross_first(me, order, slots, turned, left, part, received, second_bar, flat):
    ph_count, states, _ = turned.shape
    first, second = order
    fresh = second_bar is None
    blocks = len(first) + len(second)
    out_shape = [jax.ShapeDtypeStruct((flat[0] // blocks, flat[1]), BF16)] * len(slots)
    if second and fresh:
        out_shape.append(
            jax.ShapeDtypeStruct((2, ph_count, states - left.shape[2], states), BF16)
        )
    operands = received if fresh else [second_bar]
    out = pl.pallas_call(
        functools.partial(cross_first_kernel, states, order, slots, fresh),
        out_shape=out_shape,
        in_specs=[SMEM] + [VMEM] * (3 + len(operands)),
        out_specs=[VMEM] * len(out_shape),
        compiler_params=params(8),
        cost_estimate=cost(ph_count * states**3, 7 * ph_count * states**2),
        name="cross_first",
    )(me, turned, left, part, *operands)
    return out[: len(slots)], out[-1]


def cross_second_kernel(
    states, order, me_ref, turned_ref, select_ref, bar_ref, second_bar_ref, *rest
):
    out_refs, left_ref = dict(enumerate(rest[:-1])), rest[-1]
    turn_blocks(select_ref, second_bar_ref, left_ref)
    middle = bar_ref.shape[2]
    for q in range(turned_ref.shape[0]):
        for top, height in row_tiles(left_ref.shape[2]):
            span = slice(top, top + height)
            crossed = cross_rows(q, span, slice(0, middle), left_ref, bar_ref)
            crossed += cross_rows(q, span, slice(middle, states), left_ref, second_bar_ref)
            store_blocks(states, order, me_ref[0], q, top, crossed, turned_ref, out_refs)


def cross_second(me, order, turned, select, bar, second_bar, flat, blocks):
    ph_count, states, _ = turned.shape
    return pl.pallas_call(
        functools.partial(cross_second_kernel, states, order),
        out_shape=[jax.ShapeDtypeStruct((flat[0] // blocks, flat[1]), BF16)] * len(order),
        in_specs=[SMEM] + [VMEM] * 4,
        out_specs=[VMEM] * len(order),
        scratch_shapes=[pltpu.VMEM(second_bar.shape, BF16)],
        compiler_params=params(12),
        cost_estimate=cost(4 * ph_count * states**3, 14 * ph_count * states**2),
        name="cross_second",
    )(me, turned, select, bar, second_bar)


def pack_kernel(shape, blocks, tiles, partners, steps, me_ref, place_ref, sizes_ref, *rest):
    chan_count, tile_rows, states = shape
    source_refs, block_refs = rest[:2], rest[2 : 2 + len(partners)]
    owner_refs, (held, sems) = rest[2 + len(partners) : -2], rest[-2:]
    rows = chan_count * tile_rows // blocks
    place = place_ref[0]
    copies, places = [], []

    def fetch(source, target):
        copies.append(pltpu.make_async_copy(source, target, sems.at[len(copies)]))
        copies[-1].start()

    for slot, d in enumerate(partners):
        start = (me_ref[0] ^ d) * rows
        chan = start // tile_rows
        places.append((chan, start - chan * tile_rows))
        for n, source_ref in enumerate(source_refs):
            fetch(source_ref.at[chan, aligned(places[-1][1], rows), :], held.at[slot, n])
    for step, owner_ref in zip(steps, owner_refs):
        owner = place ^ step
        for n, source_ref in enumerate(source_refs):
            for m, other in enumerate(range(step, tiles)):
                column = aligned((owner ^ other) * tile_rows, tile_rows)
                fetch(source_ref.at[owner, :, column], owner_ref.at[n, m])
    row = lax.broadcasted_iota(jnp.int32, (rows, states), 0) + place * tile_rows
    highest = jnp.maximum(row, lax.broadcasted_iota(jnp.int32, (rows, states), 1))
    for slot, (chan, inside) in enumerate(places):
        live = jnp.maximum(highest, row + inside) < sizes_ref[chan]
        for n in range(2):
            copies[2 * slot + n].wait()
            values = held[slot, n]
            block_refs[slot][n] = jnp.where(live, values, jnp.zeros_like(values))
    for copy in copies[2 * len(partners) :]:
        copy.wait()


def pack(me, place, sizes, eta, gamma, blocks, tiles, partners, steps, mib):
    chan_count, rows, states = eta.shape
    shapes = [(2, chan_count * rows // blocks, states)] * len(partners)
    shapes += [(2, tiles - step, rows, rows) for step in steps]
    out = pl.pallas_call(
        functools.partial(pack_kernel, eta.shape, blocks, tiles, partners, steps),
        out_shape=[jax.ShapeDtypeStruct(shape, BF16) for shape in shapes],
        in_specs=[SMEM] * 3 + [HBM] * 2,
        out_specs=[VMEM] * len(shapes),
        scratch_shapes=[
            pltpu.VMEM((len(partners), *shapes[0]), BF16),
            pltpu.SemaphoreType.DMA((2 * len(partners) + 2 * sum(tiles - s for s in steps),)),
        ],
        compiler_params=params(mib),
        cost_estimate=cost(0, 8 * len(partners) * shapes[0][1] * states),
        name="pack",
    )(me, place, sizes, eta, gamma)
    return dict(zip(partners, out)), dict(zip(steps, out[len(partners) :]))


def ladder_kernel(tiles, rows, eta_ref, gamma_ref, scale_ref, *rest):
    packed_refs = rest[: tiles - 1]
    out_refs, (eta, gamma) = rest[tiles - 1 : -2], rest[-2:]
    del eta_ref, gamma_ref
    scale = scale_ref[0:1, :].astype(BF16)
    for k in range(1, tiles):
        for n, full in enumerate((eta, gamma)):
            for m, other in enumerate(range(k, tiles)):
                block = packed_refs[k - 1][n, m]
                here, there = slice(k * rows, (k + 1) * rows), slice(other * rows, (other + 1) * rows)
                full[here, there] = block
                if other > k:
                    full[there, here] = block.T if n else -block.T
    for k in reversed(range(tiles - 1)):
        here, later = slice(k * rows, (k + 1) * rows), slice((k + 1) * rows, tiles * rows)
        total = jnp.dot(eta[here, :] * scale, gamma[:, later], preferred_element_type=F32)
        total -= jnp.dot(gamma[here, :] * scale, eta[:, later], preferred_element_type=F32)
        total = total.astype(BF16)
        for other in range(k + 1, tiles):
            block = total[:, (other - k - 1) * rows : (other - k) * rows]
            column = slice(((k ^ other) - 1) * rows, (k ^ other) * rows)
            out_refs[k][:, column] = block
            out_refs[other][:, column] = block.T


def ladder_blocks(eta, gamma, scale, packed):
    states = eta.shape[0]
    tiles = len(packed) + 1
    rows = states // tiles
    full = jax.ShapeDtypeStruct(eta.shape, BF16)
    out = pl.pallas_call(
        functools.partial(ladder_kernel, tiles, rows),
        out_shape=[jax.ShapeDtypeStruct((rows, states - rows), BF16)] * tiles + [full] * 2,
        in_specs=[VMEM] * (2 + tiles),
        out_specs=[VMEM] * (tiles + 2),
        input_output_aliases={0: tiles, 1: tiles + 1},
        compiler_params=params(8),
        cost_estimate=cost(2 * states**3, 8 * states**2),
        name="ladder",
    )(eta, gamma, scale, *packed)
    return out[:tiles]


def finish_kernel(blocks, me_ref, place_ref, sizes_ref, diagonal_ref, *rest):
    back_refs, ladder_refs = rest[:blocks], rest[blocks:-4]
    out_ref, back, held, sems = rest[-4:]
    chan_count, tile_rows, states = out_ref.shape
    place = place_ref[0]
    rows = back_refs[0].shape[0]
    for d, back_ref in enumerate(back_refs):
        back[aligned((me_ref[0] ^ d) * rows, rows), :] = back_ref[...]
    row = lax.broadcasted_iota(jnp.int32, (tile_rows, tile_rows), 0) + place * tile_rows
    column = lax.broadcasted_iota(jnp.int32, (tile_rows, tile_rows), 1)
    starts = [(place ^ m) * tile_rows for m in range(len(ladder_refs))]
    highest = [jnp.maximum(row, column + start) for start in starts]
    copies = []
    for k, ladder_ref in enumerate(ladder_refs):
        c = place ^ k
        size = sizes_ref[c]
        for m, start in enumerate(starts):
            span = aligned(start, tile_rows)
            part = back[aligned(c * tile_rows, tile_rows), span]
            if m:
                total = ladder_ref[:, (m - 1) * tile_rows : m * tile_rows] + part
            else:
                total = (diagonal_ref[c] + part.astype(F32)).astype(BF16)
            held[c, :, span] = jnp.where(highest[m] < size, total, jnp.zeros_like(total))
        copies.append(pltpu.make_async_copy(held.at[c], out_ref.at[c], sems.at[k]))
        copies[-1].start()
    for copy in copies:
        copy.wait()


def finish(me, place, sizes, shape, diagonal, back, ladder):
    chan_count, tile_rows, states = shape
    return pl.pallas_call(
        functools.partial(finish_kernel, len(back)),
        out_shape=jax.ShapeDtypeStruct(shape, BF16),
        in_specs=[SMEM] * 3 + [VMEM] * (1 + len(back) + len(ladder)),
        out_specs=HBM,
        scratch_shapes=[
            pltpu.VMEM((chan_count * tile_rows, states), BF16),
            pltpu.VMEM(shape, BF16),
            pltpu.SemaphoreType.DMA((len(ladder),)),
        ],
        compiler_params=params(12),
        cost_estimate=cost(0, 6 * chan_count * tile_rows * states),
        name="finish",
    )(me, place, sizes, diagonal, *back, *ladder)


def ladder_gathered(sizes, pair_occupation, eta, gamma):
    _, rows, states = eta.shape
    columns = lax.broadcasted_iota(jnp.int32, (eta.shape[0], states), 1)
    weight = (1 - pair_occupation[0] - pair_occupation[1]) * (columns < sizes[:, None])
    first = jnp.einsum(
        "crk,ckj->crj",
        eta * weight.astype(BF16)[:, None, :],
        lax.all_gather(gamma, "tile", axis=1, tiled=True),
        preferred_element_type=F32,
    )
    mirrored = lax.all_to_all(first, "tile", split_axis=2, concat_axis=1, tiled=True)
    return first + jnp.swapaxes(mirrored, 1, 2)


WAITS = {
    "lack1": ("in1",),
    "lack3": ("in2", "prepare",),
    "in3": ("in2", "prepare",),
    "in5": ("in4", "prepare",),
    "in7": ("in6", "prepare",),
    "cross_first": ("ladder",),
    "own2": ("own1", "cross_second",),
    "back1": ("own3",),
    "back3": ("back2",),
    "back5": ("back4",),
    "back7": ("back6", "back1",),
}


ORDER = (
    "pack_near",
    "pack_late",
    "prepare",
    "in1",
    "in2",
    "in4",
    "in6",
    "lack1",
    "lack2",
    "lack3",
    "in3",
    "in5",
    "in7",
    "first",
    "ladder",
    "own1",
    "own2",
    "own3",
    "cross_first",
    "back2",
    "back4",
    "cross_next",
    "back1",
    "back6",
    "cross_second",
    "back3",
    "back5",
    "back7",
)


def per_device(
    chans,
    tiles,
    generator,
    hamiltonian,
    chan_sizes,
    pair_occupation,
    recoupled_occupation,
    recouple_map,
    recouple_weights,
):
    chan_count, tile_rows, states = generator.shape
    flat = (chan_count * tile_rows, states)
    me = jnp.reshape(lax.axis_index("chan"), (1,))
    place = jnp.reshape(lax.axis_index("tile"), (1,))
    paired = chans & (chans - 1) == 0 and tiles & (tiles - 1) == 0
    if not (paired and tiles == chan_count and chans in (tiles, 2 * tiles)):
        return per_device_whole(
            place,
            generator,
            hamiltonian,
            chan_sizes,
            pair_occupation,
            recoupled_occupation,
            recouple_map,
            recouple_weights,
        )

    def to_chan(message, d):
        return xor_permute(message, "chan", chans, d)

    def to_tile(message, k):
        return xor_permute(message, "tile", tiles, k)

    first, second = order = block_order(chans)
    sooner = [slot for slot, d in enumerate(first) if d in (2, 4)]
    later = [slot for slot in range(len(first)) if slot not in sooner]
    near = first[1:]
    late = [d for d in range(chans) if d not in near]
    pair = (generator, hamiltonian)
    steps = list(range(1, tiles))
    done = {}

    def value(name):
        if name not in done:
            done[name] = make[name]()
        return done[name]

    def held(name, operand):
        waits = [value(wait) for wait in WAITS.get(name, ()) if wait in make]
        waits = [w[1] if isinstance(w, tuple) else w[0] if isinstance(w, list) else w for w in waits]
        return lax.optimization_barrier((operand, waits))[0] if waits else operand

    def pack_part(partners, chosen, mib):
        return pack(me, place, chan_sizes, *pair, chans, tiles, partners, chosen, mib)

    def to_chan(name, block, d):
        return xor_permute(held(name, block), "chan", chans, d) if d else block

    def to_tile(name, block, k):
        return xor_permute(held(name, block), "tile", tiles, k) if k else block

    def make_first():
        turned, select, *_ = value("prepare")
        received = held("first", [value(f"in{d}") for d in first])
        return first_part(me, first, turned, select, received)

    def make_ladder():
        lacking = held("ladder", [value(f"lack{k}") for k in steps])
        return ladder_blocks(*value("prepare")[3:], lacking)

    def make_cross_next():
        _, left, part = value("first")
        second_bar = held("cross_next", value("cross_first")[1])
        return cross_first(
            me, order, later, value("prepare")[0], left, part, [], second_bar, flat
        )

    def make_cross_first():
        _, left, part = value("first")
        part = held("cross_first", part)
        received = [value(f"in{d}") for d in second]
        return cross_first(
            me, order, sooner, value("prepare")[0], left, part, received, None, flat
        )

    def make_cross_second():
        turned, select, *_ = value("prepare")
        bar, second_bar = held("cross_second", (value("first")[0], value("cross_first")[1]))
        return cross_second(me, second, turned, select, bar, second_bar, flat, chans)

    make = {
        "pack_near": lambda: pack_part(near, steps[1:2], 50),
        "pack_late": lambda: pack_part(late, steps[:1] + steps[2:], 12),
        "prepare": lambda: prepare(
            me,
            first + second,
            recouple_map,
            recoupled_occupation,
            recouple_weights,
            place,
            chan_sizes,
            pair_occupation,
            *pair,
        ),
        "first": make_first,
        "ladder": make_ladder,
        "cross_first": make_cross_first,
        "cross_next": make_cross_next,
        "cross_second": make_cross_second,
    }
    for d in range(chans):
        source = "pack_near" if d in near else "pack_late"
        make[f"in{d}"] = lambda d=d, s=source: to_chan(f"in{d}", value(s)[0][d], d)
        if d in second:
            make[f"back{d}"] = lambda d=d: to_chan(
                f"back{d}", value("cross_second")[second.index(d)], d
            )
            continue
        slot = first.index(d)
        group, slots = ("cross_first", sooner) if slot in sooner else ("cross_next", later)
        make[f"back{d}"] = lambda d=d, g=group, i=slots.index(slot): to_chan(
            f"back{d}", value(g)[0][i], d
        )
    for k in range(tiles):
        source = "pack_near" if k in steps[1:2] else "pack_late"
        make[f"lack{k}"] = lambda k=k, s=source: to_tile(f"lack{k}", value(s)[1][k], k)
        make[f"own{k}"] = lambda k=k: to_tile(f"own{k}", value("ladder")[k], k)

    for name in ORDER:
        if name in make:
            value(name)
    back = [value(f"back{d}") for d in range(chans)]
    ladder = [value(f"own{k}") for k in range(tiles)]
    return finish(me, place, chan_sizes, generator.shape, value("prepare")[2], back, ladder)


def per_device_whole(
    place,
    generator,
    hamiltonian,
    chan_sizes,
    pair_occupation,
    recoupled_occupation,
    recouple_map,
    recouple_weights,
):
    chan_count, tile_rows, states = generator.shape
    flat = (chan_count * tile_rows, states)
    alone = jnp.zeros_like(place)
    row = place * tile_rows + jnp.arange(tile_rows, dtype=jnp.int32)
    highest = jnp.maximum(row[:, None], jnp.arange(states, dtype=jnp.int32)[None, :])
    live = highest[None] < chan_sizes[:, None, None]
    pair = jnp.where(live, jnp.stack([generator, hamiltonian]), jnp.zeros((), BF16))
    received = lax.all_to_all(pair.reshape(2, *flat), "chan", 1, 1, tiled=True)
    order = ([0], [])
    turned, select = prepare(
        alone, order[0], recouple_map, recoupled_occupation, recouple_weights
    )
    _, left, part = first_part(alone, order[0], turned, select, [received])
    sent, _ = cross_first(alone, order, [0], turned, left, part, [], None, flat)
    back = lax.all_to_all(sent[0], "chan", 0, 0, tiled=True).reshape(generator.shape)
    ladder = ladder_gathered(chan_sizes, pair_occupation, generator, hamiltonian)
    return jnp.where(live, ladder + back.astype(F32), 0.0).astype(BF16)


def solution(mesh):
    return jax.shard_map(
        functools.partial(per_device, mesh.shape["chan"], mesh.shape["tile"]),
        mesh=mesh,
        in_specs=(
            P("chan", "tile", None),
            P("chan", "tile", None),
            P("chan"),
            P(None, "chan", None),
            P(None, ("chan", "tile"), None),
            P(("chan", "tile"), None),
            P(("chan", "tile"), None, None),
        ),
        out_specs=P("chan", "tile", None),
        check_vma=False,
    )
```

```python
import functools

import jax
import jax.numpy as jnp
from jax import lax
from jax.experimental import pallas as pl
from jax.experimental.pallas import tpu as pltpu
from jax.sharding import PartitionSpec as P

BF16 = jnp.bfloat16
F32 = jnp.float32
HBM = pl.BlockSpec(memory_space=pltpu.HBM)
VMEM = pl.BlockSpec(memory_space=pltpu.VMEM)
NT = (((1,), (1,)), ((), ()))
SMEM = pl.BlockSpec(memory_space=pltpu.SMEM)


def params(mib):
    return pltpu.CompilerParams(vmem_limit_bytes=mib << 20)


def cost(flops, moved):
    return pl.CostEstimate(flops=int(flops), bytes_accessed=int(moved), transcendentals=0)


def xor_permute(block, axis, size, step):
    return lax.ppermute(block, axis, [(i, i ^ step) for i in range(size)])


def aligned(start, size):
    return pl.ds(pl.multiple_of(start, size), size)


def row_tiles(states):
    return [(start, min(256, states - start)) for start in range(0, states, 256)]


def block_order(blocks):
    first = [0, 1, *range(2, blocks, 2)]
    return first, [d for d in range(blocks) if d not in first]


def free_weight(occ_ref, chan, size):
    occupied = occ_ref[0] + occ_ref[1]
    own = lax.broadcasted_iota(jnp.int32, occupied.shape, 0) == chan
    free = jnp.sum(jnp.where(own, 1 - occupied, 0), axis=0, keepdims=True)
    live = lax.broadcasted_iota(jnp.int32, free.shape, 1) < size
    return jnp.where(live, free, 0).astype(F32)


def diagonal_blocks(sizes_ref, occ_ref, eta_ref, gamma_ref, out_ref):
    for c in range(eta_ref.shape[0]):
        weight = free_weight(occ_ref, c, sizes_ref[c]).astype(BF16)
        out_ref[c] = lax.dot_general(
            eta_ref[c] * weight, gamma_ref[c], NT, preferred_element_type=F32
        ) + lax.dot_general(gamma_ref[c] * weight, eta_ref[c], NT, preferred_element_type=F32)


def prepare_kernel(
    ph_count, states, order, me_ref, map_ref, occ_ref, weights_ref, turned_ref, select_ref
):
    rows = states // len(order)
    for q in range(ph_count):
        map_row = map_ref[q : q + 1, :]
        spans = [aligned((me_ref[0] ^ d) * rows, rows) for d in order]
        kept_map = jnp.concatenate([map_ref[q : q + 1, s] for s in spans], axis=1)
        signs = jnp.concatenate(
            [occ_ref[0, q : q + 1, s] - occ_ref[1, q : q + 1, s] for s in spans], axis=1
        ).astype(F32)
        for start, height in row_tiles(states):
            index = lax.broadcasted_iota(jnp.int32, (height, states), 0) + start
            select_ref[q, start : start + height, :] = jnp.where(
                index == kept_map, signs, 0.0
            ).astype(BF16)
            hot = jnp.where(index == map_row, 1.0, 0.0).astype(BF16)
            for top, tall in row_tiles(states):
                rest = weights_ref[q, top : top + tall, :]
                total = jnp.zeros((tall, height), F32)
                for _ in range(3):
                    part = rest.astype(BF16)
                    rest = rest - part.astype(F32)
                    total = total + lax.dot_general(
                        part, hot, NT, preferred_element_type=F32
                    )
                turned_ref[q, top : top + tall, start : start + height] = total


def own_rows(place, sizes_ref, occ_ref, eta_ref, gamma_ref, full_refs, scale_ref):
    tiles, rows, _ = eta_ref.shape
    weight = free_weight(occ_ref, place, sizes_ref[place])
    scale_ref[1:2, :] = weight
    for k in range(tiles):
        column, later = aligned((place ^ k) * rows, rows), slice(k * rows, (k + 1) * rows)
        scale_ref[0:1, later] = scale_ref[1:2, column]
        for n, source_ref in enumerate((eta_ref, gamma_ref)):
            block = source_ref[place, :, column]
            full_refs[n][0:rows, later] = block
            if k:
                full_refs[n][later, 0:rows] = block.T if n else -block.T


def prepare_whole_kernel(ph_count, states, order, *refs):
    place_ref, refs = refs[0], refs[1:]
    prepare_kernel(ph_count, states, order, *refs[:4], *refs[8:10])
    diagonal_blocks(*refs[4:8], refs[10])
    own_rows(place_ref[0], *refs[4:8], refs[11:13], refs[13])


def prepare(me, order, recouple_map, recoupled_occupation, recouple_weights, place=None, *pair):
    ph_count, states = recouple_map.shape
    kernel, extra, lead = prepare_kernel, [], []
    flops = 6 * ph_count * states**3
    if pair:
        chan_count, rows, columns = pair[-1].shape
        kernel, lead = prepare_whole_kernel, [place]
        extra = [jax.ShapeDtypeStruct((chan_count, rows, rows), F32)]
        extra += [jax.ShapeDtypeStruct((columns, columns), BF16)] * 2
        extra += [jax.ShapeDtypeStruct((8, columns), F32)]
        flops += 4 * chan_count * rows * rows * columns
    return pl.pallas_call(
        functools.partial(kernel, ph_count, states, order),
        out_shape=(
            jax.ShapeDtypeStruct(recouple_weights.shape, F32),
            jax.ShapeDtypeStruct(recouple_weights.shape, BF16),
            *extra,
        ),
        in_specs=[SMEM] * (len(lead) + 1)
        + [VMEM] * 3
        + [SMEM] * bool(pair)
        + [VMEM] * len(pair[1:]),
        out_specs=(VMEM,) * (2 + len(extra)),
        compiler_params=params(12),
        cost_estimate=cost(flops, 14 * ph_count * states**2),
        name="prepare",
    )(*lead, me, recouple_map, recoupled_occupation, recouple_weights, *pair)


def weigh_blocks(states, order, me, turned_ref, recv_refs, bar_ref):
    for recv_ref, (slot, d) in zip(recv_refs, enumerate(order)):
        rows = recv_ref.shape[1]
        span = aligned((me ^ d) * rows, rows)
        for q in range(turned_ref.shape[0]):
            weights = turned_ref[q, span, :]
            for n in range(2):
                values = recv_ref[n, :, q * states : (q + 1) * states].astype(F32) * weights
                bar_ref[n, q, slot * rows : (slot + 1) * rows, :] = values.astype(BF16)


def turn_blocks(select_ref, bar_ref, left_ref):
    for q in range(select_ref.shape[0]):
        for n in range(2):
            for top, height in row_tiles(bar_ref.shape[2]):
                span = slice(top, top + height)
                left_ref[n, q, span, :] = jnp.dot(
                    bar_ref[n, q, span, :], select_ref[q], preferred_element_type=F32
                ).astype(BF16)


def cross_rows(q, span, inner, left_ref, bar_ref):
    return jnp.dot(
        left_ref[0, q, span, inner], bar_ref[1, q], preferred_element_type=F32
    ) - jnp.dot(left_ref[1, q, span, inner], bar_ref[0, q], preferred_element_type=F32)


def store_blocks(states, order, me, q, top, crossed, turned_ref, out_refs):
    rows = next(iter(out_refs.values())).shape[0]
    step = min(rows, crossed.shape[0])
    for base in range(0, crossed.shape[0], step):
        slot, inside = divmod(top + base, rows)
        weights = turned_ref[q, aligned((me ^ order[slot]) * rows + inside, step), :]
        out_refs[slot][inside : inside + step, q * states : (q + 1) * states] = (
            crossed[base : base + step] * weights
        ).astype(BF16)


def first_kernel(states, order, me_ref, turned_ref, select_ref, *rest):
    recv_refs, (bar_ref, left_ref, part_ref) = rest[:-3], rest[-3:]
    weigh_blocks(states, order, me_ref[0], turned_ref, recv_refs, bar_ref)
    turn_blocks(select_ref, bar_ref, left_ref)
    for q in range(turned_ref.shape[0]):
        for top, height in row_tiles(bar_ref.shape[2]):
            span = slice(top, top + height)
            part_ref[q, span, :] = cross_rows(
                q, span, slice(0, bar_ref.shape[2]), left_ref, bar_ref
            )


def first_part(me, order, turned, select, received):
    ph_count, states, _ = turned.shape
    rows = received[0].shape[1] * len(order)
    shape = jax.ShapeDtypeStruct((2, ph_count, rows, states), BF16)
    return pl.pallas_call(
        functools.partial(first_kernel, states, order),
        out_shape=(shape, shape, jax.ShapeDtypeStruct((ph_count, rows, states), F32)),
        in_specs=[SMEM] + [VMEM] * (2 + len(order)),
        out_specs=(VMEM,) * 3,
        compiler_params=params(8),
        cost_estimate=cost(8 * ph_count * rows * states**2, 14 * ph_count * states**2),
        name="first_part",
    )(me, turned, select, *received)


def cross_first_kernel(states, order, slots, fresh, me_ref, turned_ref, left_ref, part_ref, *rest):
    first, second = order
    recv_refs, rest = (rest[: len(second)], rest[len(second) :]) if fresh else ((), rest)
    bar_ref, outs = (rest[-1], rest[: len(slots)]) if fresh else (rest[0], rest[1:])
    if not second:
        outs = rest
    out_refs = dict(zip(slots, outs))
    if second and fresh:
        weigh_blocks(states, second, me_ref[0], turned_ref, recv_refs, bar_ref)
    rows = outs[0].shape[0]
    runs = []
    for slot in slots:
        if runs and runs[-1][1] == slot * rows and runs[-1][1] - runs[-1][0] < 256:
            runs[-1][1] += rows
        else:
            runs.append([slot * rows, (slot + 1) * rows])
    for q in range(turned_ref.shape[0]):
        for start, stop in runs:
            for top, height in row_tiles(stop - start):
                span = slice(start + top, start + top + height)
                crossed = part_ref[q, span, :]
                if second:
                    inner = slice(left_ref.shape[2], states)
                    crossed += cross_rows(q, span, inner, left_ref, bar_ref)
                store_blocks(
                    states, first, me_ref[0], q, start + top, crossed, turned_ref, out_refs
                )


def cross_first(me, order, slots, turned, left, part, received, second_bar, flat):
    ph_count, states, _ = turned.shape
    first, second = order
    fresh = second_bar is None
    blocks = len(first) + len(second)
    out_shape = [jax.ShapeDtypeStruct((flat[0] // blocks, flat[1]), BF16)] * len(slots)
    if second and fresh:
        out_shape.append(
            jax.ShapeDtypeStruct((2, ph_count, states - left.shape[2], states), BF16)
        )
    operands = received if fresh else [second_bar]
    out = pl.pallas_call(
        functools.partial(cross_first_kernel, states, order, slots, fresh),
        out_shape=out_shape,
        in_specs=[SMEM] + [VMEM] * (3 + len(operands)),
        out_specs=[VMEM] * len(out_shape),
        compiler_params=params(8),
        cost_estimate=cost(ph_count * states**3, 7 * ph_count * states**2),
        name="cross_first",
    )(me, turned, left, part, *operands)
    return out[: len(slots)], out[-1]


def cross_second_kernel(
    states, order, me_ref, turned_ref, select_ref, bar_ref, second_bar_ref, *rest
):
    out_refs, left_ref = dict(enumerate(rest[:-1])), rest[-1]
    turn_blocks(select_ref, second_bar_ref, left_ref)
    middle = bar_ref.shape[2]
    for q in range(turned_ref.shape[0]):
        for top, height in row_tiles(left_ref.shape[2]):
            span = slice(top, top + height)
            crossed = cross_rows(q, span, slice(0, middle), left_ref, bar_ref)
            crossed += cross_rows(q, span, slice(middle, states), left_ref, second_bar_ref)
            store_blocks(states, order, me_ref[0], q, top, crossed, turned_ref, out_refs)


def cross_second(me, order, turned, select, bar, second_bar, flat, blocks):
    ph_count, states, _ = turned.shape
    return pl.pallas_call(
        functools.partial(cross_second_kernel, states, order),
        out_shape=[jax.ShapeDtypeStruct((flat[0] // blocks, flat[1]), BF16)] * len(order),
        in_specs=[SMEM] + [VMEM] * 4,
        out_specs=[VMEM] * len(order),
        scratch_shapes=[pltpu.VMEM(second_bar.shape, BF16)],
        compiler_params=params(12),
        cost_estimate=cost(4 * ph_count * states**3, 14 * ph_count * states**2),
        name="cross_second",
    )(me, turned, select, bar, second_bar)


def pack_kernel(shape, blocks, tiles, partners, steps, me_ref, place_ref, sizes_ref, *rest):
    chan_count, tile_rows, states = shape
    source_refs, block_refs = rest[:2], rest[2 : 2 + len(partners)]
    owner_refs, (held, sems) = rest[2 + len(partners) : -2], rest[-2:]
    rows = chan_count * tile_rows // blocks
    place = place_ref[0]
    copies, places = [], []

    def fetch(source, target):
        copies.append(pltpu.make_async_copy(source, target, sems.at[len(copies)]))
        copies[-1].start()

    for slot, d in enumerate(partners):
        start = (me_ref[0] ^ d) * rows
        chan = start // tile_rows
        places.append((chan, start - chan * tile_rows))
        for n, source_ref in enumerate(source_refs):
            fetch(source_ref.at[chan, aligned(places[-1][1], rows), :], held.at[slot, n])
    for step, owner_ref in zip(steps, owner_refs):
        owner = place ^ step
        for n, source_ref in enumerate(source_refs):
            for m, other in enumerate(range(step, tiles)):
                column = aligned((owner ^ other) * tile_rows, tile_rows)
                fetch(source_ref.at[owner, :, column], owner_ref.at[n, m])
    row = lax.broadcasted_iota(jnp.int32, (rows, states), 0) + place * tile_rows
    highest = jnp.maximum(row, lax.broadcasted_iota(jnp.int32, (rows, states), 1))
    for slot, (chan, inside) in enumerate(places):
        live = jnp.maximum(highest, row + inside) < sizes_ref[chan]
        for n in range(2):
            copies[2 * slot + n].wait()
            values = held[slot, n]
            block_refs[slot][n] = jnp.where(live, values, jnp.zeros_like(values))
    for copy in copies[2 * len(partners) :]:
        copy.wait()


def pack(me, place, sizes, eta, gamma, blocks, tiles, partners, steps, mib):
    chan_count, rows, states = eta.shape
    shapes = [(2, chan_count * rows // blocks, states)] * len(partners)
    shapes += [(2, tiles - step, rows, rows) for step in steps]
    out = pl.pallas_call(
        functools.partial(pack_kernel, eta.shape, blocks, tiles, partners, steps),
        out_shape=[jax.ShapeDtypeStruct(shape, BF16) for shape in shapes],
        in_specs=[SMEM] * 3 + [HBM] * 2,
        out_specs=[VMEM] * len(shapes),
        scratch_shapes=[
            pltpu.VMEM((len(partners), *shapes[0]), BF16),
            pltpu.SemaphoreType.DMA((2 * len(partners) + 2 * sum(tiles - s for s in steps),)),
        ],
        compiler_params=params(mib),
        cost_estimate=cost(0, 8 * len(partners) * shapes[0][1] * states),
        name="pack",
    )(me, place, sizes, eta, gamma)
    return dict(zip(partners, out)), dict(zip(steps, out[len(partners) :]))


def ladder_kernel(tiles, rows, eta_ref, gamma_ref, scale_ref, *rest):
    packed_refs = rest[: tiles - 1]
    out_refs, (eta, gamma) = rest[tiles - 1 : -2], rest[-2:]
    del eta_ref, gamma_ref
    scale = scale_ref[0:1, :].astype(BF16)
    for k in range(1, tiles):
        for n, full in enumerate((eta, gamma)):
            for m, other in enumerate(range(k, tiles)):
                block = packed_refs[k - 1][n, m]
                here, there = slice(k * rows, (k + 1) * rows), slice(other * rows, (other + 1) * rows)
                full[here, there] = block
                if other > k:
                    full[there, here] = block.T if n else -block.T
    for k in reversed(range(tiles - 1)):
        here, later = slice(k * rows, (k + 1) * rows), slice((k + 1) * rows, tiles * rows)
        total = jnp.dot(eta[here, :] * scale, gamma[:, later], preferred_element_type=F32)
        total -= jnp.dot(gamma[here, :] * scale, eta[:, later], preferred_element_type=F32)
        total = total.astype(BF16)
        for other in range(k + 1, tiles):
            block = total[:, (other - k - 1) * rows : (other - k) * rows]
            column = slice(((k ^ other) - 1) * rows, (k ^ other) * rows)
            out_refs[k][:, column] = block
            out_refs[other][:, column] = block.T


def ladder_blocks(eta, gamma, scale, packed):
    states = eta.shape[0]
    tiles = len(packed) + 1
    rows = states // tiles
    full = jax.ShapeDtypeStruct(eta.shape, BF16)
    out = pl.pallas_call(
        functools.partial(ladder_kernel, tiles, rows),
        out_shape=[jax.ShapeDtypeStruct((rows, states - rows), BF16)] * tiles + [full] * 2,
        in_specs=[VMEM] * (2 + tiles),
        out_specs=[VMEM] * (tiles + 2),
        input_output_aliases={0: tiles, 1: tiles + 1},
        compiler_params=params(8),
        cost_estimate=cost(2 * states**3, 8 * states**2),
        name="ladder",
    )(eta, gamma, scale, *packed)
    return out[:tiles]


def finish_kernel(blocks, me_ref, place_ref, sizes_ref, diagonal_ref, *rest):
    back_refs, ladder_refs = rest[: blocks - 1], rest[blocks - 1 : -4]
    out_ref, back, held, sems = rest[-4:]
    chan_count, tile_rows, states = out_ref.shape
    place = place_ref[0]
    rows = back_refs[0].shape[0]
    for d, back_ref in enumerate(back_refs):
        back[aligned((me_ref[0] ^ d) * rows, rows), :] = back_ref[...]
    back[aligned((me_ref[0] ^ (blocks - 1)) * rows, rows), :] = jnp.zeros((rows, states), BF16)
    row = lax.broadcasted_iota(jnp.int32, (tile_rows, tile_rows), 0) + place * tile_rows
    column = lax.broadcasted_iota(jnp.int32, (tile_rows, tile_rows), 1)
    starts = [(place ^ m) * tile_rows for m in range(len(ladder_refs))]
    highest = [jnp.maximum(row, column + start) for start in starts]
    copies = []
    for k, ladder_ref in enumerate(ladder_refs):
        c = place ^ k
        for m, start in enumerate(starts):
            span = aligned(start, tile_rows)
            part = back[aligned(c * tile_rows, tile_rows), span]
            if m:
                total = ladder_ref[:, (m - 1) * tile_rows : m * tile_rows] + part
            else:
                total = (diagonal_ref[c] + part.astype(F32)).astype(BF16)
            held[c, :, span] = jnp.where(highest[m] < sizes_ref[c], total, jnp.zeros_like(total))
        copies.append(pltpu.make_async_copy(held.at[c], out_ref.at[c], sems.at[k]))
        copies[-1].start()
    for copy in copies:
        copy.wait()


def finish(me, place, sizes, shape, diagonal, back, ladder):
    chan_count, tile_rows, states = shape
    return pl.pallas_call(
        functools.partial(finish_kernel, len(back) + 1),
        out_shape=jax.ShapeDtypeStruct(shape, BF16),
        in_specs=[SMEM] * 3 + [VMEM] * (1 + len(back) + len(ladder)),
        out_specs=HBM,
        scratch_shapes=[
            pltpu.VMEM((chan_count * tile_rows, states), BF16),
            pltpu.VMEM(shape, BF16),
            pltpu.SemaphoreType.DMA((len(ladder),)),
        ],
        compiler_params=params(12),
        cost_estimate=cost(0, 6 * chan_count * tile_rows * states),
        name="finish",
    )(me, place, sizes, diagonal, *back, *ladder)


def finish_last_kernel(
    blocks, me_ref, place_ref, sizes_ref, started_ref, diagonal_ref, back_ref, *rest
):
    del started_ref
    ladder_refs, (out_ref, ladder, held, sem) = rest[:-4], rest[-4:]
    tile_rows = out_ref.shape[1]
    place = place_ref[0]
    rows = back_ref.shape[0]
    first_row = (me_ref[0] ^ (blocks - 1)) * rows
    c = first_row // tile_rows
    inside = pl.multiple_of(first_row - c * tile_rows, rows)
    span = pl.ds(inside, rows)
    for k, ladder_ref in enumerate(ladder_refs):

        @pl.when((c ^ place) == k)
        def _(ladder_ref=ladder_ref):
            ladder[...] = ladder_ref[span, :]

    row = lax.broadcasted_iota(jnp.int32, (rows, tile_rows), 0) + (place * tile_rows + inside)
    column = lax.broadcasted_iota(jnp.int32, (rows, tile_rows), 1)
    for m in range(len(ladder_refs)):
        start = (place ^ m) * tile_rows
        columns = aligned(start, tile_rows)
        part = back_ref[:, columns]
        if m:
            total = ladder[:, (m - 1) * tile_rows : m * tile_rows] + part
        else:
            total = (diagonal_ref[c, span, :] + part.astype(F32)).astype(BF16)
        live = jnp.maximum(row, column + start) < sizes_ref[c]
        held[:, columns] = jnp.where(live, total, jnp.zeros_like(total))
    copy = pltpu.make_async_copy(held, out_ref.at[c, span, :], sem)
    copy.start()
    copy.wait()


def finish_last(me, place, sizes, started, diagonal, back, blocks, ladder):
    rows, states = back.shape
    return pl.pallas_call(
        functools.partial(finish_last_kernel, blocks),
        out_shape=jax.ShapeDtypeStruct(started.shape, BF16),
        in_specs=[SMEM] * 3 + [HBM] + [VMEM] * (2 + len(ladder)),
        out_specs=HBM,
        scratch_shapes=[
            pltpu.VMEM((rows, ladder[0].shape[1]), BF16),
            pltpu.VMEM((rows, states), BF16),
            pltpu.SemaphoreType.DMA,
        ],
        input_output_aliases={3: 0},
        compiler_params=params(4),
        cost_estimate=cost(0, 6 * rows * states),
        name="finish_last",
    )(me, place, sizes, started, diagonal, back, *ladder)


def ladder_gathered(sizes, pair_occupation, eta, gamma):
    _, rows, states = eta.shape
    columns = lax.broadcasted_iota(jnp.int32, (eta.shape[0], states), 1)
    weight = (1 - pair_occupation[0] - pair_occupation[1]) * (columns < sizes[:, None])
    first = jnp.einsum(
        "crk,ckj->crj",
        eta * weight.astype(BF16)[:, None, :],
        lax.all_gather(gamma, "tile", axis=1, tiled=True),
        preferred_element_type=F32,
    )
    mirrored = lax.all_to_all(first, "tile", split_axis=2, concat_axis=1, tiled=True)
    return first + jnp.swapaxes(mirrored, 1, 2)


WAITS = {
    "lack1": ("in1",),
    "lack3": ("in2", "prepare",),
    "in3": ("in2", "prepare",),
    "in5": ("in4", "prepare",),
    "in7": ("in6", "prepare",),
    "cross_first": ("ladder",),
    "own2": ("own3",),
    "back1": ("own3", "back2",),
    "back3": ("back2", "back1",),
    "back5": ("back4",),
    "back7": ("back6", "back1",),
    "own1": ("own3",),
}


ORDER = (
    "pack_near",
    "pack_late",
    "prepare",
    "in1",
    "in2",
    "in4",
    "in6",
    "lack1",
    "lack2",
    "lack3",
    "in3",
    "in5",
    "in7",
    "first",
    "ladder",
    "own1",
    "own2",
    "own3",
    "cross_first",
    "back2",
    "back4",
    "cross_next",
    "back1",
    "back6",
    "cross_second",
    "back3",
    "back5",
    "back7",
)


def per_device(
    chans,
    tiles,
    generator,
    hamiltonian,
    chan_sizes,
    pair_occupation,
    recoupled_occupation,
    recouple_map,
    recouple_weights,
):
    chan_count, tile_rows, states = generator.shape
    flat = (chan_count * tile_rows, states)
    me = jnp.reshape(lax.axis_index("chan"), (1,))
    place = jnp.reshape(lax.axis_index("tile"), (1,))
    paired = chans & (chans - 1) == 0 and tiles & (tiles - 1) == 0
    if not (paired and tiles == chan_count and chans in (tiles, 2 * tiles)):
        return per_device_whole(
            place,
            generator,
            hamiltonian,
            chan_sizes,
            pair_occupation,
            recoupled_occupation,
            recouple_map,
            recouple_weights,
        )

    def to_chan(message, d):
        return xor_permute(message, "chan", chans, d)

    def to_tile(message, k):
        return xor_permute(message, "tile", tiles, k)

    first, second = order = block_order(chans)
    sooner = [slot for slot, d in enumerate(first) if d in (2, 4)]
    later = [slot for slot in range(len(first)) if slot not in sooner]
    near = first[1:]
    late = [d for d in range(chans) if d not in near]
    pair = (generator, hamiltonian)
    steps = list(range(1, tiles))
    done = {}

    def value(name):
        if name not in done:
            done[name] = make[name]()
        return done[name]

    def held(name, operand):
        waits = [value(wait) for wait in WAITS.get(name, ()) if wait in make]
        waits = [w[1] if isinstance(w, tuple) else w[0] if isinstance(w, list) else w for w in waits]
        return lax.optimization_barrier((operand, waits))[0] if waits else operand

    def pack_part(partners, chosen, mib):
        return pack(me, place, chan_sizes, *pair, chans, tiles, partners, chosen, mib)

    def to_chan(name, block, d):
        return xor_permute(held(name, block), "chan", chans, d) if d else block

    def to_tile(name, block, k):
        return xor_permute(held(name, block), "tile", tiles, k) if k else block

    def make_first():
        turned, select, *_ = value("prepare")
        received = held("first", [value(f"in{d}") for d in first])
        return first_part(me, first, turned, select, received)

    def make_ladder():
        lacking = held("ladder", [value(f"lack{k}") for k in steps])
        return ladder_blocks(*value("prepare")[3:], lacking)

    def make_cross_next():
        _, left, part = value("first")
        second_bar = held("cross_next", value("cross_first")[1])
        return cross_first(
            me, order, later, value("prepare")[0], left, part, [], second_bar, flat
        )

    def make_cross_first():
        _, left, part = value("first")
        part = held("cross_first", part)
        received = [value(f"in{d}") for d in second]
        return cross_first(
            me, order, sooner, value("prepare")[0], left, part, received, None, flat
        )

    def make_cross_second():
        turned, select, *_ = value("prepare")
        bar, second_bar = held("cross_second", (value("first")[0], value("cross_first")[1]))
        return cross_second(me, second, turned, select, bar, second_bar, flat, chans)

    make = {
        "pack_near": lambda: pack_part(near, steps[1:2], 50),
        "pack_late": lambda: pack_part(late, steps[:1] + steps[2:], 12),
        "prepare": lambda: prepare(
            me,
            first + second,
            recouple_map,
            recoupled_occupation,
            recouple_weights,
            place,
            chan_sizes,
            pair_occupation,
            *pair,
        ),
        "first": make_first,
        "ladder": make_ladder,
        "cross_first": make_cross_first,
        "cross_next": make_cross_next,
        "cross_second": make_cross_second,
    }
    for d in range(chans):
        source = "pack_near" if d in near else "pack_late"
        make[f"in{d}"] = lambda d=d, s=source: to_chan(f"in{d}", value(s)[0][d], d)
        if d in second:
            make[f"back{d}"] = lambda d=d: to_chan(
                f"back{d}", value("cross_second")[second.index(d)], d
            )
            continue
        slot = first.index(d)
        group, slots = ("cross_first", sooner) if slot in sooner else ("cross_next", later)
        make[f"back{d}"] = lambda d=d, g=group, i=slots.index(slot): to_chan(
            f"back{d}", value(g)[0][i], d
        )
    for k in range(tiles):
        source = "pack_near" if k in steps[1:2] else "pack_late"
        make[f"lack{k}"] = lambda k=k, s=source: to_tile(f"lack{k}", value(s)[1][k], k)
        make[f"own{k}"] = lambda k=k: to_tile(f"own{k}", value("ladder")[k], k)

    for name in ORDER:
        if name in make:
            value(name)
    back = [value(f"back{d}") for d in range(chans)]
    ladder = [value(f"own{k}") for k in range(tiles)]
    diagonal = value("prepare")[2]
    started = finish(me, place, chan_sizes, generator.shape, diagonal, back[:-1], ladder)
    return finish_last(me, place, chan_sizes, started, diagonal, back[-1], chans, ladder)


def per_device_whole(
    place,
    generator,
    hamiltonian,
    chan_sizes,
    pair_occupation,
    recoupled_occupation,
    recouple_map,
    recouple_weights,
):
    chan_count, tile_rows, states = generator.shape
    flat = (chan_count * tile_rows, states)
    alone = jnp.zeros_like(place)
    row = place * tile_rows + jnp.arange(tile_rows, dtype=jnp.int32)
    highest = jnp.maximum(row[:, None], jnp.arange(states, dtype=jnp.int32)[None, :])
    live = highest[None] < chan_sizes[:, None, None]
    pair = jnp.where(live, jnp.stack([generator, hamiltonian]), jnp.zeros((), BF16))
    received = lax.all_to_all(pair.reshape(2, *flat), "chan", 1, 1, tiled=True)
    order = ([0], [])
    turned, select = prepare(
        alone, order[0], recouple_map, recoupled_occupation, recouple_weights
    )
    _, left, part = first_part(alone, order[0], turned, select, [received])
    sent, _ = cross_first(alone, order, [0], turned, left, part, [], None, flat)
    back = lax.all_to_all(sent[0], "chan", 0, 0, tiled=True).reshape(generator.shape)
    ladder = ladder_gathered(chan_sizes, pair_occupation, generator, hamiltonian)
    return jnp.where(live, ladder + back.astype(F32), 0.0).astype(BF16)


def solution(mesh):
    return jax.shard_map(
        functools.partial(per_device, mesh.shape["chan"], mesh.shape["tile"]),
        mesh=mesh,
        in_specs=(
            P("chan", "tile", None),
            P("chan", "tile", None),
            P("chan"),
            P(None, "chan", None),
            P(None, ("chan", "tile"), None),
            P(("chan", "tile"), None),
            P(("chan", "tile"), None, None),
        ),
        out_specs=P("chan", "tile", None),
        check_vma=False,
    )
```

```python
import functools

import jax
import jax.numpy as jnp
from jax import lax
from jax.experimental import pallas as pl
from jax.experimental.pallas import tpu as pltpu
from jax.sharding import PartitionSpec as P

BF16 = jnp.bfloat16
F32 = jnp.float32
HBM = pl.BlockSpec(memory_space=pltpu.HBM)
VMEM = pl.BlockSpec(memory_space=pltpu.VMEM)
NT = (((1,), (1,)), ((), ()))
SMEM = pl.BlockSpec(memory_space=pltpu.SMEM)


def params(mib):
    return pltpu.CompilerParams(vmem_limit_bytes=mib << 20)


def cost(flops, moved):
    return pl.CostEstimate(flops=int(flops), bytes_accessed=int(moved), transcendentals=0)


def xor_permute(block, axis, size, step):
    return lax.ppermute(block, axis, [(i, i ^ step) for i in range(size)])


def aligned(start, size):
    return pl.ds(pl.multiple_of(start, size), size)


def row_tiles(states):
    return [(start, min(256, states - start)) for start in range(0, states, 256)]


def block_order(blocks):
    first = [0, 1, *range(2, blocks, 2)]
    return first, [d for d in range(blocks) if d not in first]


def free_weight(occ_ref, chan, size):
    occupied = occ_ref[0] + occ_ref[1]
    own = lax.broadcasted_iota(jnp.int32, occupied.shape, 0) == chan
    free = jnp.sum(jnp.where(own, 1 - occupied, 0), axis=0, keepdims=True)
    live = lax.broadcasted_iota(jnp.int32, free.shape, 1) < size
    return jnp.where(live, free, 0).astype(F32)


def diagonal_blocks(sizes_ref, occ_ref, eta_ref, gamma_ref, out_ref):
    for c in range(eta_ref.shape[0]):
        weight = free_weight(occ_ref, c, sizes_ref[c]).astype(BF16)
        out_ref[c] = lax.dot_general(
            eta_ref[c] * weight, gamma_ref[c], NT, preferred_element_type=F32
        ) + lax.dot_general(gamma_ref[c] * weight, eta_ref[c], NT, preferred_element_type=F32)


def prepare_kernel(
    ph_count, states, order, me_ref, map_ref, occ_ref, weights_ref, turned_ref, select_ref
):
    rows = states // len(order)
    for q in range(ph_count):
        map_row = map_ref[q : q + 1, :]
        spans = [aligned((me_ref[0] ^ d) * rows, rows) for d in order]
        kept_map = jnp.concatenate([map_ref[q : q + 1, s] for s in spans], axis=1)
        signs = jnp.concatenate(
            [occ_ref[0, q : q + 1, s] - occ_ref[1, q : q + 1, s] for s in spans], axis=1
        ).astype(F32)
        for start, height in row_tiles(states):
            index = lax.broadcasted_iota(jnp.int32, (height, states), 0) + start
            select_ref[q, start : start + height, :] = jnp.where(
                index == kept_map, signs, 0.0
            ).astype(BF16)
            hot = jnp.where(index == map_row, 1.0, 0.0).astype(BF16)
            for top, tall in row_tiles(states):
                rest = weights_ref[q, top : top + tall, :]
                total = jnp.zeros((tall, height), F32)
                for _ in range(3):
                    part = rest.astype(BF16)
                    rest = rest - part.astype(F32)
                    total = total + lax.dot_general(
                        part, hot, NT, preferred_element_type=F32
                    )
                turned_ref[q, top : top + tall, start : start + height] = total


def own_rows(place, sizes_ref, occ_ref, eta_ref, gamma_ref, full_refs, scale_ref):
    tiles, rows, _ = eta_ref.shape
    weight = free_weight(occ_ref, place, sizes_ref[place])
    scale_ref[1:2, :] = weight
    for k in range(tiles):
        column, later = aligned((place ^ k) * rows, rows), slice(k * rows, (k + 1) * rows)
        scale_ref[0:1, later] = scale_ref[1:2, column]
        for n, source_ref in enumerate((eta_ref, gamma_ref)):
            block = source_ref[place, :, column]
            full_refs[n][0:rows, later] = block
            if k:
                full_refs[n][later, 0:rows] = block.T if n else -block.T


def prepare_whole_kernel(ph_count, states, order, *refs):
    place_ref, refs = refs[0], refs[1:]
    prepare_kernel(ph_count, states, order, *refs[:4], *refs[8:10])
    diagonal_blocks(*refs[4:8], refs[10])
    own_rows(place_ref[0], *refs[4:8], refs[11:13], refs[13])


def prepare(me, order, recouple_map, recoupled_occupation, recouple_weights, place=None, *pair):
    ph_count, states = recouple_map.shape
    kernel, extra, lead = prepare_kernel, [], []
    flops = 6 * ph_count * states**3
    if pair:
        chan_count, rows, columns = pair[-1].shape
        kernel, lead = prepare_whole_kernel, [place]
        extra = [jax.ShapeDtypeStruct((chan_count, rows, rows), F32)]
        extra += [jax.ShapeDtypeStruct((columns, columns), BF16)] * 2
        extra += [jax.ShapeDtypeStruct((8, columns), F32)]
        flops += 4 * chan_count * rows * rows * columns
    return pl.pallas_call(
        functools.partial(kernel, ph_count, states, order),
        out_shape=(
            jax.ShapeDtypeStruct(recouple_weights.shape, F32),
            jax.ShapeDtypeStruct(recouple_weights.shape, BF16),
            *extra,
        ),
        in_specs=[SMEM] * (len(lead) + 1)
        + [VMEM] * 3
        + [SMEM] * bool(pair)
        + [VMEM] * len(pair[1:]),
        out_specs=(VMEM,) * (2 + len(extra)),
        compiler_params=params(12),
        cost_estimate=cost(flops, 14 * ph_count * states**2),
        name="prepare",
    )(*lead, me, recouple_map, recoupled_occupation, recouple_weights, *pair)


def weigh_blocks(states, order, me, turned_ref, recv_refs, bar_ref):
    for recv_ref, (slot, d) in zip(recv_refs, enumerate(order)):
        rows = recv_ref.shape[1]
        span = aligned((me ^ d) * rows, rows)
        for q in range(turned_ref.shape[0]):
            weights = turned_ref[q, span, :]
            for n in range(2):
                values = recv_ref[n, :, q * states : (q + 1) * states].astype(F32) * weights
                bar_ref[n, q, slot * rows : (slot + 1) * rows, :] = values.astype(BF16)


def turn_blocks(select_ref, bar_ref, left_ref):
    for q in range(select_ref.shape[0]):
        for n in range(2):
            for top, height in row_tiles(bar_ref.shape[2]):
                span = slice(top, top + height)
                left_ref[n, q, span, :] = jnp.dot(
                    bar_ref[n, q, span, :], select_ref[q], preferred_element_type=F32
                ).astype(BF16)


def cross_rows(q, span, inner, left_ref, bar_ref):
    return jnp.dot(
        left_ref[0, q, span, inner], bar_ref[1, q], preferred_element_type=F32
    ) - jnp.dot(left_ref[1, q, span, inner], bar_ref[0, q], preferred_element_type=F32)


def store_blocks(states, order, me, q, top, crossed, turned_ref, out_refs):
    rows = next(iter(out_refs.values())).shape[0]
    step = min(rows, crossed.shape[0])
    for base in range(0, crossed.shape[0], step):
        slot, inside = divmod(top + base, rows)
        weights = turned_ref[q, aligned((me ^ order[slot]) * rows + inside, step), :]
        out_refs[slot][inside : inside + step, q * states : (q + 1) * states] = (
            crossed[base : base + step] * weights
        ).astype(BF16)


def first_kernel(states, order, me_ref, turned_ref, select_ref, *rest):
    recv_refs, (bar_ref, left_ref, part_ref) = rest[:-3], rest[-3:]
    weigh_blocks(states, order, me_ref[0], turned_ref, recv_refs, bar_ref)
    turn_blocks(select_ref, bar_ref, left_ref)
    for q in range(turned_ref.shape[0]):
        for top, height in row_tiles(bar_ref.shape[2]):
            span = slice(top, top + height)
            part_ref[q, span, :] = cross_rows(
                q, span, slice(0, bar_ref.shape[2]), left_ref, bar_ref
            )


def first_part(me, order, turned, select, received):
    ph_count, states, _ = turned.shape
    rows = received[0].shape[1] * len(order)
    shape = jax.ShapeDtypeStruct((2, ph_count, rows, states), BF16)
    return pl.pallas_call(
        functools.partial(first_kernel, states, order),
        out_shape=(shape, shape, jax.ShapeDtypeStruct((ph_count, rows, states), F32)),
        in_specs=[SMEM] + [VMEM] * (2 + len(order)),
        out_specs=(VMEM,) * 3,
        compiler_params=params(8),
        cost_estimate=cost(8 * ph_count * rows * states**2, 14 * ph_count * states**2),
        name="first_part",
    )(me, turned, select, *received)


def cross_first_kernel(states, order, slots, fresh, me_ref, turned_ref, left_ref, part_ref, *rest):
    first, second = order
    recv_refs, rest = (rest[: len(second)], rest[len(second) :]) if fresh else ((), rest)
    bar_ref, outs = (rest[-1], rest[: len(slots)]) if fresh else (rest[0], rest[1:])
    if not second:
        outs = rest
    out_refs = dict(zip(slots, outs))
    if second and fresh:
        weigh_blocks(states, second, me_ref[0], turned_ref, recv_refs, bar_ref)
    rows = outs[0].shape[0]
    runs = []
    for slot in slots:
        if runs and runs[-1][1] == slot * rows and runs[-1][1] - runs[-1][0] < 256:
            runs[-1][1] += rows
        else:
            runs.append([slot * rows, (slot + 1) * rows])
    for q in range(turned_ref.shape[0]):
        for start, stop in runs:
            for top, height in row_tiles(stop - start):
                span = slice(start + top, start + top + height)
                crossed = part_ref[q, span, :]
                if second:
                    inner = slice(left_ref.shape[2], states)
                    crossed += cross_rows(q, span, inner, left_ref, bar_ref)
                store_blocks(
                    states, first, me_ref[0], q, start + top, crossed, turned_ref, out_refs
                )


def cross_first(me, order, slots, turned, left, part, received, second_bar, flat):
    ph_count, states, _ = turned.shape
    first, second = order
    fresh = second_bar is None
    blocks = len(first) + len(second)
    out_shape = [jax.ShapeDtypeStruct((flat[0] // blocks, flat[1]), BF16)] * len(slots)
    if second and fresh:
        out_shape.append(
            jax.ShapeDtypeStruct((2, ph_count, states - left.shape[2], states), BF16)
        )
    operands = received if fresh else [second_bar]
    out = pl.pallas_call(
        functools.partial(cross_first_kernel, states, order, slots, fresh),
        out_shape=out_shape,
        in_specs=[SMEM] + [VMEM] * (3 + len(operands)),
        out_specs=[VMEM] * len(out_shape),
        compiler_params=params(8),
        cost_estimate=cost(ph_count * states**3, 7 * ph_count * states**2),
        name="cross_first",
    )(me, turned, left, part, *operands)
    return out[: len(slots)], out[-1]


def cross_second_kernel(
    states, order, me_ref, turned_ref, select_ref, bar_ref, second_bar_ref, *rest
):
    out_refs, left_ref = dict(enumerate(rest[:-1])), rest[-1]
    turn_blocks(select_ref, second_bar_ref, left_ref)
    middle = bar_ref.shape[2]
    for q in range(turned_ref.shape[0]):
        for top, height in row_tiles(left_ref.shape[2]):
            span = slice(top, top + height)
            crossed = cross_rows(q, span, slice(0, middle), left_ref, bar_ref)
            crossed += cross_rows(q, span, slice(middle, states), left_ref, second_bar_ref)
            store_blocks(states, order, me_ref[0], q, top, crossed, turned_ref, out_refs)


def cross_second(me, order, turned, select, bar, second_bar, flat, blocks):
    ph_count, states, _ = turned.shape
    return pl.pallas_call(
        functools.partial(cross_second_kernel, states, order),
        out_shape=[jax.ShapeDtypeStruct((flat[0] // blocks, flat[1]), BF16)] * len(order),
        in_specs=[SMEM] + [VMEM] * 4,
        out_specs=[VMEM] * len(order),
        scratch_shapes=[pltpu.VMEM(second_bar.shape, BF16)],
        compiler_params=params(12),
        cost_estimate=cost(4 * ph_count * states**3, 14 * ph_count * states**2),
        name="cross_second",
    )(me, turned, select, bar, second_bar)


def pack_kernel(shape, blocks, tiles, partners, steps, me_ref, place_ref, sizes_ref, *rest):
    chan_count, tile_rows, states = shape
    source_refs, block_refs = rest[:2], rest[2 : 2 + len(partners)]
    owner_refs, (held, sems) = rest[2 + len(partners) : -2], rest[-2:]
    rows = chan_count * tile_rows // blocks
    place = place_ref[0]
    copies, places = [], []

    def fetch(source, target):
        copies.append(pltpu.make_async_copy(source, target, sems.at[len(copies)]))
        copies[-1].start()

    for slot, d in enumerate(partners):
        start = (me_ref[0] ^ d) * rows
        chan = start // tile_rows
        places.append((chan, start - chan * tile_rows))
        for n, source_ref in enumerate(source_refs):
            fetch(source_ref.at[chan, aligned(places[-1][1], rows), :], held.at[slot, n])
    for step, owner_ref in zip(steps, owner_refs):
        owner = place ^ step
        for n, source_ref in enumerate(source_refs):
            for m, other in enumerate(range(step, tiles)):
                column = aligned((owner ^ other) * tile_rows, tile_rows)
                fetch(source_ref.at[owner, :, column], owner_ref.at[n, m])
    row = lax.broadcasted_iota(jnp.int32, (rows, states), 0) + place * tile_rows
    highest = jnp.maximum(row, lax.broadcasted_iota(jnp.int32, (rows, states), 1))
    for slot, (chan, inside) in enumerate(places):
        live = jnp.maximum(highest, row + inside) < sizes_ref[chan]
        for n in range(2):
            copies[2 * slot + n].wait()
            values = held[slot, n]
            block_refs[slot][n] = jnp.where(live, values, jnp.zeros_like(values))
    for copy in copies[2 * len(partners) :]:
        copy.wait()


def pack(me, place, sizes, eta, gamma, blocks, tiles, partners, steps, mib):
    chan_count, rows, states = eta.shape
    shapes = [(2, chan_count * rows // blocks, states)] * len(partners)
    shapes += [(2, tiles - step, rows, rows) for step in steps]
    out = pl.pallas_call(
        functools.partial(pack_kernel, eta.shape, blocks, tiles, partners, steps),
        out_shape=[jax.ShapeDtypeStruct(shape, BF16) for shape in shapes],
        in_specs=[SMEM] * 3 + [HBM] * 2,
        out_specs=[VMEM] * len(shapes),
        scratch_shapes=[
            pltpu.VMEM((len(partners), *shapes[0]), BF16),
            pltpu.SemaphoreType.DMA((2 * len(partners) + 2 * sum(tiles - s for s in steps),)),
        ],
        compiler_params=params(mib),
        cost_estimate=cost(0, 8 * len(partners) * shapes[0][1] * states),
        name="pack",
    )(me, place, sizes, eta, gamma)
    return dict(zip(partners, out)), dict(zip(steps, out[len(partners) :]))


def ladder_kernel(tiles, rows, eta_ref, gamma_ref, scale_ref, *rest):
    packed_refs = rest[: tiles - 1]
    out_refs, (eta, gamma) = rest[tiles - 1 : -2], rest[-2:]
    del eta_ref, gamma_ref
    scale = scale_ref[0:1, :].astype(BF16)
    for k in range(1, tiles):
        for n, full in enumerate((eta, gamma)):
            for m, other in enumerate(range(k, tiles)):
                block = packed_refs[k - 1][n, m]
                here, there = slice(k * rows, (k + 1) * rows), slice(other * rows, (other + 1) * rows)
                full[here, there] = block
                if other > k:
                    full[there, here] = block.T if n else -block.T
    for k in reversed(range(tiles - 1)):
        here, later = slice(k * rows, (k + 1) * rows), slice((k + 1) * rows, tiles * rows)
        total = jnp.dot(eta[here, :] * scale, gamma[:, later], preferred_element_type=F32)
        total -= jnp.dot(gamma[here, :] * scale, eta[:, later], preferred_element_type=F32)
        total = total.astype(BF16)
        for other in range(k + 1, tiles):
            block = total[:, (other - k - 1) * rows : (other - k) * rows]
            column = slice(((k ^ other) - 1) * rows, (k ^ other) * rows)
            out_refs[k][:, column] = block
            out_refs[other][:, column] = block.T


def ladder_blocks(eta, gamma, scale, packed):
    states = eta.shape[0]
    tiles = len(packed) + 1
    rows = states // tiles
    full = jax.ShapeDtypeStruct(eta.shape, BF16)
    out = pl.pallas_call(
        functools.partial(ladder_kernel, tiles, rows),
        out_shape=[jax.ShapeDtypeStruct((rows, states - rows), BF16)] * tiles + [full] * 2,
        in_specs=[VMEM] * (2 + tiles),
        out_specs=[VMEM] * (tiles + 2),
        input_output_aliases={0: tiles, 1: tiles + 1},
        compiler_params=params(8),
        cost_estimate=cost(2 * states**3, 8 * states**2),
        name="ladder",
    )(eta, gamma, scale, *packed)
    return out[:tiles]


def finish_kernel(blocks, me_ref, place_ref, sizes_ref, diagonal_ref, *rest):
    back_refs, ladder_refs = rest[: blocks - 1], rest[blocks - 1 : -4]
    out_ref, back, held, sems = rest[-4:]
    chan_count, tile_rows, states = out_ref.shape
    place = place_ref[0]
    rows = back_refs[0].shape[0]
    for d, back_ref in enumerate(back_refs):
        back[aligned((me_ref[0] ^ d) * rows, rows), :] = back_ref[...]
    back[aligned((me_ref[0] ^ (blocks - 1)) * rows, rows), :] = jnp.zeros((rows, states), BF16)
    row = lax.broadcasted_iota(jnp.int32, (tile_rows, tile_rows), 0) + place * tile_rows
    column = lax.broadcasted_iota(jnp.int32, (tile_rows, tile_rows), 1)
    starts = [(place ^ m) * tile_rows for m in range(len(ladder_refs))]
    highest = [jnp.maximum(row, column + start) for start in starts]
    copies = []
    for k, ladder_ref in enumerate(ladder_refs):
        c = place ^ k
        for m, start in enumerate(starts):
            span = aligned(start, tile_rows)
            part = back[aligned(c * tile_rows, tile_rows), span]
            if m:
                total = ladder_ref[:, (m - 1) * tile_rows : m * tile_rows] + part
            else:
                total = (diagonal_ref[c] + part.astype(F32)).astype(BF16)
            held[c, :, span] = jnp.where(highest[m] < sizes_ref[c], total, jnp.zeros_like(total))
        copies.append(pltpu.make_async_copy(held.at[c], out_ref.at[c], sems.at[k]))
        copies[-1].start()
    for copy in copies:
        copy.wait()


def finish(me, place, sizes, shape, diagonal, back, ladder):
    chan_count, tile_rows, states = shape
    return pl.pallas_call(
        functools.partial(finish_kernel, len(back) + 1),
        out_shape=jax.ShapeDtypeStruct(shape, BF16),
        in_specs=[SMEM] * 3 + [VMEM] * (1 + len(back) + len(ladder)),
        out_specs=HBM,
        scratch_shapes=[
            pltpu.VMEM((chan_count * tile_rows, states), BF16),
            pltpu.VMEM(shape, BF16),
            pltpu.SemaphoreType.DMA((len(ladder),)),
        ],
        compiler_params=params(12),
        cost_estimate=cost(0, 6 * chan_count * tile_rows * states),
        name="finish",
    )(me, place, sizes, diagonal, *back, *ladder)


def finish_last_kernel(
    blocks, me_ref, place_ref, sizes_ref, started_ref, diagonal_ref, back_ref, *rest
):
    del started_ref
    ladder_refs, (out_ref, ladder, held, sem) = rest[:-4], rest[-4:]
    tile_rows = out_ref.shape[1]
    place = place_ref[0]
    rows = back_ref.shape[0]
    first_row = (me_ref[0] ^ (blocks - 1)) * rows
    c = first_row // tile_rows
    inside = pl.multiple_of(first_row - c * tile_rows, rows)
    span = pl.ds(inside, rows)
    for k, ladder_ref in enumerate(ladder_refs):

        @pl.when((c ^ place) == k)
        def _(ladder_ref=ladder_ref):
            ladder[...] = ladder_ref[span, :]

    row = lax.broadcasted_iota(jnp.int32, (rows, tile_rows), 0) + (place * tile_rows + inside)
    column = lax.broadcasted_iota(jnp.int32, (rows, tile_rows), 1)
    for m in range(len(ladder_refs)):
        start = (place ^ m) * tile_rows
        columns = aligned(start, tile_rows)
        part = back_ref[:, columns]
        if m:
            total = ladder[:, (m - 1) * tile_rows : m * tile_rows] + part
        else:
            total = (diagonal_ref[c, span, :] + part.astype(F32)).astype(BF16)
        live = jnp.maximum(row, column + start) < sizes_ref[c]
        held[:, columns] = jnp.where(live, total, jnp.zeros_like(total))
    copy = pltpu.make_async_copy(held, out_ref.at[c, span, :], sem)
    copy.start()
    copy.wait()


def finish_last(me, place, sizes, started, diagonal, back, blocks, ladder):
    rows, states = back.shape
    return pl.pallas_call(
        functools.partial(finish_last_kernel, blocks),
        out_shape=jax.ShapeDtypeStruct(started.shape, BF16),
        in_specs=[SMEM] * 3 + [HBM] + [VMEM] * (2 + len(ladder)),
        out_specs=HBM,
        scratch_shapes=[
            pltpu.VMEM((rows, ladder[0].shape[1]), BF16),
            pltpu.VMEM((rows, states), BF16),
            pltpu.SemaphoreType.DMA,
        ],
        input_output_aliases={3: 0},
        compiler_params=params(4),
        cost_estimate=cost(0, 6 * rows * states),
        name="finish_last",
    )(me, place, sizes, started, diagonal, back, *ladder)


def ladder_gathered(sizes, pair_occupation, eta, gamma):
    _, rows, states = eta.shape
    columns = lax.broadcasted_iota(jnp.int32, (eta.shape[0], states), 1)
    weight = (1 - pair_occupation[0] - pair_occupation[1]) * (columns < sizes[:, None])
    first = jnp.einsum(
        "crk,ckj->crj",
        eta * weight.astype(BF16)[:, None, :],
        lax.all_gather(gamma, "tile", axis=1, tiled=True),
        preferred_element_type=F32,
    )
    mirrored = lax.all_to_all(first, "tile", split_axis=2, concat_axis=1, tiled=True)
    return first + jnp.swapaxes(mirrored, 1, 2)


WAITS = {
    "lack1": ("in1",),
    "lack3": ("in2", "prepare",),
    "in3": ("in2", "prepare",),
    "in5": ("in4", "prepare",),
    "in7": ("in6", "prepare",),
    "cross_first": ("ladder",),
    "own2": ("own3",),
    "back1": ("own3", "back2",),
    "back3": ("back2", "back1",),
    "back5": ("back4",),
    "back7": ("back6",),
    "own1": ("own3",),
}


ORDER = (
    "pack_near",
    "pack_late",
    "prepare",
    "in1",
    "in2",
    "in4",
    "in6",
    "lack1",
    "lack2",
    "lack3",
    "in5",
    "in3",
    "in7",
    "first",
    "ladder",
    "own1",
    "own2",
    "own3",
    "cross_first",
    "back2",
    "back4",
    "cross_next",
    "back1",
    "back6",
    "cross_second",
    "back3",
    "back5",
    "back7",
)


def per_device(
    chans,
    tiles,
    generator,
    hamiltonian,
    chan_sizes,
    pair_occupation,
    recoupled_occupation,
    recouple_map,
    recouple_weights,
):
    chan_count, tile_rows, states = generator.shape
    flat = (chan_count * tile_rows, states)
    me = jnp.reshape(lax.axis_index("chan"), (1,))
    place = jnp.reshape(lax.axis_index("tile"), (1,))
    paired = chans & (chans - 1) == 0 and tiles & (tiles - 1) == 0
    if not (paired and tiles == chan_count and chans in (tiles, 2 * tiles)):
        return per_device_whole(
            place,
            generator,
            hamiltonian,
            chan_sizes,
            pair_occupation,
            recoupled_occupation,
            recouple_map,
            recouple_weights,
        )

    def to_chan(message, d):
        return xor_permute(message, "chan", chans, d)

    def to_tile(message, k):
        return xor_permute(message, "tile", tiles, k)

    first, second = order = block_order(chans)
    sooner = [slot for slot, d in enumerate(first) if d in (2, 4)]
    later = [slot for slot in range(len(first)) if slot not in sooner]
    near = first[1:]
    late = [d for d in range(chans) if d not in near]
    pair = (generator, hamiltonian)
    steps = list(range(1, tiles))
    done = {}

    def value(name):
        if name not in done:
            done[name] = make[name]()
        return done[name]

    def held(name, operand):
        waits = [value(wait) for wait in WAITS.get(name, ()) if wait in make]
        waits = [w[1] if isinstance(w, tuple) else w[0] if isinstance(w, list) else w for w in waits]
        return lax.optimization_barrier((operand, waits))[0] if waits else operand

    def pack_part(partners, chosen, mib):
        return pack(me, place, chan_sizes, *pair, chans, tiles, partners, chosen, mib)

    def to_chan(name, block, d):
        return xor_permute(held(name, block), "chan", chans, d) if d else block

    def to_tile(name, block, k):
        return xor_permute(held(name, block), "tile", tiles, k) if k else block

    def make_first():
        turned, select, *_ = value("prepare")
        received = held("first", [value(f"in{d}") for d in first])
        return first_part(me, first, turned, select, received)

    def make_ladder():
        lacking = held("ladder", [value(f"lack{k}") for k in steps])
        return ladder_blocks(*value("prepare")[3:], lacking)

    def make_cross_next():
        _, left, part = value("first")
        second_bar = held("cross_next", value("cross_first")[1])
        return cross_first(
            me, order, later, value("prepare")[0], left, part, [], second_bar, flat
        )

    def make_cross_first():
        _, left, part = value("first")
        part = held("cross_first", part)
        received = [value(f"in{d}") for d in second]
        return cross_first(
            me, order, sooner, value("prepare")[0], left, part, received, None, flat
        )

    def make_cross_second():
        turned, select, *_ = value("prepare")
        bar, second_bar = held("cross_second", (value("first")[0], value("cross_first")[1]))
        return cross_second(me, second, turned, select, bar, second_bar, flat, chans)

    make = {
        "pack_near": lambda: pack_part(near, steps[1:2], 50),
        "pack_late": lambda: pack_part(late, steps[:1] + steps[2:], 12),
        "prepare": lambda: prepare(
            me,
            first + second,
            recouple_map,
            recoupled_occupation,
            recouple_weights,
            place,
            chan_sizes,
            pair_occupation,
            *pair,
        ),
        "first": make_first,
        "ladder": make_ladder,
        "cross_first": make_cross_first,
        "cross_next": make_cross_next,
        "cross_second": make_cross_second,
    }
    for d in range(chans):
        source = "pack_near" if d in near else "pack_late"
        make[f"in{d}"] = lambda d=d, s=source: to_chan(f"in{d}", value(s)[0][d], d)
        if d in second:
            make[f"back{d}"] = lambda d=d: to_chan(
                f"back{d}", value("cross_second")[second.index(d)], d
            )
            continue
        slot = first.index(d)
        group, slots = ("cross_first", sooner) if slot in sooner else ("cross_next", later)
        make[f"back{d}"] = lambda d=d, g=group, i=slots.index(slot): to_chan(
            f"back{d}", value(g)[0][i], d
        )
    for k in range(tiles):
        source = "pack_near" if k in steps[1:2] else "pack_late"
        make[f"lack{k}"] = lambda k=k, s=source: to_tile(f"lack{k}", value(s)[1][k], k)
        make[f"own{k}"] = lambda k=k: to_tile(f"own{k}", value("ladder")[k], k)

    for name in ORDER:
        if name in make:
            value(name)
    back = [value(f"back{d}") for d in range(chans)]
    ladder = [value(f"own{k}") for k in range(tiles)]
    diagonal = value("prepare")[2]
    started = finish(me, place, chan_sizes, generator.shape, diagonal, back[:-1], ladder)
    return finish_last(me, place, chan_sizes, started, diagonal, back[-1], chans, ladder)


def per_device_whole(
    place,
    generator,
    hamiltonian,
    chan_sizes,
    pair_occupation,
    recoupled_occupation,
    recouple_map,
    recouple_weights,
):
    chan_count, tile_rows, states = generator.shape
    flat = (chan_count * tile_rows, states)
    alone = jnp.zeros_like(place)
    row = place * tile_rows + jnp.arange(tile_rows, dtype=jnp.int32)
    highest = jnp.maximum(row[:, None], jnp.arange(states, dtype=jnp.int32)[None, :])
    live = highest[None] < chan_sizes[:, None, None]
    pair = jnp.where(live, jnp.stack([generator, hamiltonian]), jnp.zeros((), BF16))
    received = lax.all_to_all(pair.reshape(2, *flat), "chan", 1, 1, tiled=True)
    order = ([0], [])
    turned, select = prepare(
        alone, order[0], recouple_map, recoupled_occupation, recouple_weights
    )
    _, left, part = first_part(alone, order[0], turned, select, [received])
    sent, _ = cross_first(alone, order, [0], turned, left, part, [], None, flat)
    back = lax.all_to_all(sent[0], "chan", 0, 0, tiled=True).reshape(generator.shape)
    ladder = ladder_gathered(chan_sizes, pair_occupation, generator, hamiltonian)
    return jnp.where(live, ladder + back.astype(F32), 0.0).astype(BF16)


def solution(mesh):
    return jax.shard_map(
        functools.partial(per_device, mesh.shape["chan"], mesh.shape["tile"]),
        mesh=mesh,
        in_specs=(
            P("chan", "tile", None),
            P("chan", "tile", None),
            P("chan"),
            P(None, "chan", None),
            P(None, ("chan", "tile"), None),
            P(("chan", "tile"), None),
            P(("chan", "tile"), None, None),
        ),
        out_specs=P("chan", "tile", None),
        check_vma=False,
    )
```
